32 devices in a mesh: rep: 4 (over x, core), blk: 8 (over z, y).
Axes of the slice: x: 2, y: 2, z: 4, core: 2. Of those that a mesh axis runs over, the one named last changes fastest.
Arguments:
- features: bfloat16 [65536, 256], P(('blk', 'rep')), may hold values from -6 to 6
- restriction: float32 [64, 16, 16], replicated, may hold values from -1.5 to 1.5
- mixing: float32 [16, 16], replicated, may hold values from -1.5 to 1.5
- source_index: int32 [8, 4, 2, 2048], P('blk', 'rep'), may hold values from 0 to 8191
- target_index: int32 [8, 4, 2, 2048], P('blk', 'rep'), may hold values from 0 to 8191
- map_index: int32 [8, 4, 2, 2048], P('blk', 'rep'), may hold values from 0 to 63
- edge_counts: int32 [8, 4, 2], P('blk', 'rep'), may hold values from 32 to 2048, as said below
Outputs:
- updated: bfloat16 [65536, 256], P(('blk', 'rep'))
The draws below stay inside these ranges and needn't reach their ends.
Inputs may be any that keep to these rules, and one draw needn't show every extreme that they name: `edge_counts`: each count is max(1, 2048 * l * l // 64) for a whole l from 1 to 8; some tile has exactly 2048 live slots in every draw.
All inputs are finite; a program needn't handle non-finite values.
Results may differ from the reference program's by a relative error of at most 0.0034.
Values may be sent and summed in bfloat16 or wider, within the bound.
No kernel may reach another device: no remote copies, remote signals or barrier semaphores. Data moves between devices by JAX's collectives and lax.ppermute only.
A program may use at most 128 MiB of HBM per device.

```python
import jax
import jax.numpy as jnp
from jax import lax

STALK = 16
CHAN = 16
MAPS = 64
CAP = 2048
STEPS = 2
BLOCKS = 8
REPLICAS = 4
BLOCK_NODES = 8192
NODES = 65536


def draw_edge_counts(key, part):
    tile_total = BLOCKS * REPLICAS * STEPS
    levels = jax.random.randint(key, (tile_total,), 1, 9)
    counted = jnp.maximum(1, CAP * levels * levels // 64)
    chosen_tile = jax.random.randint(jax.random.fold_in(key, 7), (), 0, tile_total)
    tile_ids = jnp.arange(tile_total, dtype=jnp.int32)
    counted = jnp.where(tile_ids == chosen_tile, CAP, counted)
    return counted.astype(jnp.int32).reshape(BLOCKS, REPLICAS, STEPS)


def touch_ends(drawn, own_key, low, largest):
    longest = drawn.shape.index(max(drawn.shape))
    spots = []
    for shift in (0, 1):
        where = [jax.random.randint(jax.random.fold_in(own_key, axis), (), 0, length) for axis, length in enumerate(drawn.shape)]
        where[longest] = (where[longest] + shift) % drawn.shape[longest]
        spots.append(tuple(where))
    return drawn.at[spots[0]].set(low).at[spots[1]].set(largest)


def level_of(key, dims, shards, smallest, top_value):
    gain, own = 1.0, jax.random.fold_in(key, 6)
    for axis_at, blocks in shards:
        steps = jnp.exp(jax.random.uniform(jax.random.fold_in(own, axis_at), (blocks,), jnp.float32, smallest / len(shards), top_value / len(shards)))
        gain = gain * jnp.repeat(steps, dims[axis_at] // blocks).reshape([-1 if axis == axis_at else 1 for axis in range(len(dims))])
    return gain


def centred(stream_key, shape, width, limit, split=(), kind=jnp.bfloat16):
    array = jax.random.normal(stream_key, shape, jnp.float32) * width
    if len(split) > 0:
        array = level_of(stream_key, shape, split, -0.22, 0.18) * array
    return jnp.clip(array, min=-limit, max=limit).astype(kind)


def setup_inputs(seed: int = 0) -> dict:
    splits = jax.random.split(jax.random.key(seed), 8)
    return {
        "features": centred(splits[0], (NODES, STALK * CHAN), 1.0, 6.0, ((0, 32),)),
        "restriction": centred(splits[1], (MAPS, STALK, STALK), STALK ** -0.5, 1.5, (), jnp.float32),
        "mixing": centred(splits[2], (CHAN, CHAN), CHAN ** -0.5, 1.5, (), jnp.float32),
        "source_index": touch_ends(jax.random.randint(splits[3], (BLOCKS, REPLICAS, STEPS, CAP), 0, BLOCK_NODES), jax.random.fold_in(splits[3], 1), 0, BLOCK_NODES - 1).astype(jnp.int32),
        "target_index": touch_ends(jax.random.randint(splits[4], (BLOCKS, REPLICAS, STEPS, CAP), 0, BLOCK_NODES), jax.random.fold_in(splits[4], 1), 0, BLOCK_NODES - 1).astype(jnp.int32),
        "map_index": touch_ends(jax.random.randint(splits[5], (BLOCKS, REPLICAS, STEPS, CAP), 0, MAPS), jax.random.fold_in(splits[5], 1), 0, MAPS - 1).astype(jnp.int32),
        "edge_counts": draw_edge_counts(jax.random.fold_in(splits[7], 71), 0),
    }


def reference(features, restriction, mixing, source_index, target_index, map_index, edge_counts):
    feature_width = STALK * CHAN
    tile_total = BLOCKS * REPLICAS * STEPS
    flat_sources = source_index.reshape(tile_total, CAP)
    flat_targets = target_index.reshape(tile_total, CAP)
    flat_maps = map_index.reshape(tile_total, CAP)
    flat_counts = edge_counts.reshape(tile_total)
    tile_ids = jnp.arange(tile_total, dtype=jnp.int32)
    target_blocks = tile_ids // (REPLICAS * STEPS)
    cycle_turns = tile_ids % STEPS
    source_blocks = (target_blocks - cycle_turns) % BLOCKS
    slot_ids = jnp.arange(CAP, dtype=jnp.int32)

    def tile_terms(totals, tile):
        sources, targets, maps, live_count, target_block, source_block = tile
        source_rows = (source_block * BLOCK_NODES + sources).astype(jnp.int32)
        gathered = jnp.take(features, source_rows, axis=0).astype(jnp.float32).reshape(CAP, STALK, CHAN)
        chosen = jnp.take(restriction, maps, axis=0)
        message = jnp.einsum("eij,ejc->eic", chosen, gathered, precision=lax.Precision.HIGHEST)
        message = message.reshape(CAP, feature_width).astype(jnp.bfloat16)
        message = lax.optimization_barrier(message).astype(jnp.float32)
        live = (slot_ids < live_count).astype(jnp.float32)
        target_rows = (target_block * BLOCK_NODES + targets).astype(jnp.int32)
        totals = totals.at[target_rows].add(message * live[:, None])
        return totals, None

    totals = jnp.zeros((NODES, feature_width), jnp.float32)
    totals, _ = lax.scan(tile_terms, totals, (flat_sources, flat_targets, flat_maps, flat_counts, target_blocks, source_blocks))
    mixed = jnp.einsum("nsc,ck->nsk", totals.reshape(NODES, STALK, CHAN), mixing, precision=lax.Precision.HIGHEST)
    updated = features.astype(jnp.float32) + mixed.reshape(NODES, feature_width)
    return updated.astype(jnp.bfloat16)
```

```python
import functools

import jax
import jax.numpy as jnp
from jax import lax
from jax.experimental import pallas as pl
from jax.experimental.pallas import tpu as pltpu
from jax.sharding import PartitionSpec as P

EDGES = 256
LANES = 128
UNROLL = 16
VMEM_LIMIT = 48 * 1024 * 1024


def bits_for(count):
    return max(1, (count - 1).bit_length())


def passed_along(block, axis, distance):
    devices = range(lax.axis_size(axis))
    route = [((i - distance) % len(devices), i) for i in devices]
    return lax.ppermute(block, axis, route)


def swapped(block, bit):
    route = [(i, i ^ bit) for i in range(lax.axis_size("rep"))]
    return lax.ppermute(block, "rep", route)


def spread_near(piece, near):
    pieces = [piece]
    bit = 1
    while bit < near:
        pieces = pieces + [swapped(p, bit) for p in pieces]
        bit *= 2
    return pieces


def pick_kernel(capacity, groups, counts_ref, soon_ref, late_ref, soon_out, late_out, ends_out):
    tiles = counts_ref.shape[0]

    def first_turn(tile, at):
        base = tile * capacity

        def some(i, at):
            for u in range(UNROLL):
                word = soon_ref[base + i * UNROLL + u]
                soon_out[at] = word
                at = at + 1 + (word >> 31)
            return at

        return lax.fori_loop(0, pl.cdiv(counts_ref[tile], UNROLL), some, at)

    def other_turn(tile, ats):
        base = tile * capacity
        late_base = (tile - groups) * capacity

        def some(i, ats):
            at, late_at = ats
            for u in range(UNROLL):
                word = soon_ref[base + i * UNROLL + u]
                soon_out[at] = word
                at = at + 1 + (word >> 31)
                word = late_ref[late_base + i * UNROLL + u]
                late_out[late_at] = word
                late_at = late_at + 1 + (word >> 31)
            return at, late_at

        return lax.fori_loop(0, pl.cdiv(counts_ref[tile], UNROLL), some, ats)

    at = lax.fori_loop(0, groups, first_turn, jnp.int32(0))
    at, late_at = lax.fori_loop(groups, tiles, other_turn, (at, jnp.int32(0)))

    def fill(i, _):
        for u in range(UNROLL):
            soon_out[at + i * UNROLL + u] = 0
            late_out[late_at + i * UNROLL + u] = 0
        return 0

    lax.fori_loop(0, EDGES // UNROLL, fill, 0)
    ends_out[0] = at
    ends_out[1] = late_at


def add_edges(sizes, count, words_ref, vector_words_ref, rows_ref, bank_ref, total_ref, gathered_ref, chosen_ref, sent_ref):
    stalk, channels, maps, source_bits, target_bits, nodes = sizes
    source_mask = (1 << source_bits) - 1
    target_mask = (1 << target_bits) - 1

    def add_block(block, _):
        first = block * EDGES

        def gather(i, _):
            for u in range(UNROLL):
                row = words_ref[first + i * UNROLL + u] & source_mask
                gathered_ref[pl.ds(i * UNROLL + u, 1), :] = rows_ref[pl.ds(row, 1), :]
            return 0

        lax.fori_loop(0, EDGES // UNROLL, gather, 0)
        words = vector_words_ref[pl.ds(block, 1), :]
        slots = first + lax.broadcasted_iota(jnp.int32, (1, EDGES), 1)
        targets = jnp.where(slots < count, (words >> source_bits) & target_mask, -1)
        map_ids = words >> (source_bits + target_bits)
        wanted = (lax.broadcasted_iota(jnp.int32, (maps, EDGES), 0) == map_ids).astype(jnp.bfloat16)
        wanted = jnp.concatenate([wanted, wanted], axis=0)
        chosen_ref[...] = jnp.dot(bank_ref[...], wanted, preferred_element_type=jnp.float32)
        for part in range(EDGES // LANES):
            lanes = slice(part * LANES, (part + 1) * LANES)
            features = gathered_ref[lanes, :].T
            for i in range(stalk):
                message = None
                for j in range(stalk):
                    factor = chosen_ref[i * stalk + j : i * stalk + j + 1, lanes]
                    term = factor * features[j * channels : (j + 1) * channels, :]
                    message = term if message is None else message + term
                sent_ref[i * channels : (i + 1) * channels, lanes] = message.astype(jnp.bfloat16)

        def scatter(chunk, _):
            start = pl.multiple_of(chunk * EDGES, EDGES)
            ids = start + lax.broadcasted_iota(jnp.int32, (EDGES, EDGES), 0)
            selector = (ids == targets).astype(jnp.bfloat16)
            total_ref[pl.ds(start, EDGES), :] += lax.dot_general(
                selector, sent_ref[...], (((1,), (1,)), ((), ())), preferred_element_type=jnp.float32
            )
            return 0

        lax.fori_loop(0, nodes // EDGES, scatter, 0)
        return 0

    lax.fori_loop(0, pl.cdiv(count, EDGES), add_block, 0)


def two_parts(value):
    high = value.astype(jnp.bfloat16)
    return high, (value - high.astype(jnp.float32)).astype(jnp.bfloat16)


def load_bank(bank_ref, bank_parts_ref):
    maps = bank_ref.shape[1]
    high, low = two_parts(bank_ref[...])
    bank_parts_ref[:, :maps] = high
    bank_parts_ref[:, maps:] = low


def load_rows(piece_refs, rows_ref):
    start = 0
    for ref in piece_refs:
        rows = ref.shape[0]

        def widen(i, _, ref=ref, start=start):
            at = pl.multiple_of(i * 64, 64)
            rows_ref[pl.ds(start + at, 64), :] = ref[pl.ds(at, 64), :].astype(jnp.float32)
            return 0

        lax.fori_loop(0, rows // 64, widen, 0)
        start += rows


def soon_kernel(sizes, piece_count, *refs):
    ends_ref, words_ref, vector_words_ref, bank_ref = refs[:4]
    pieces = refs[4 : 4 + piece_count]
    total_ref, rows_ref, bank_parts_ref, gathered_ref, chosen_ref, sent_ref = refs[4 + piece_count :]
    load_bank(bank_ref, bank_parts_ref)
    load_rows(pieces, rows_ref)
    total_ref[...] = jnp.zeros_like(total_ref)
    add_edges(sizes, ends_ref[0], words_ref, vector_words_ref, rows_ref, bank_parts_ref, total_ref, gathered_ref, chosen_ref, sent_ref)


def late_kernel(sizes, piece_count, *refs):
    ends_ref, words_ref, vector_words_ref, bank_ref, spread_ref, own_ref, before_ref = refs[:7]
    pieces = refs[7 : 7 + piece_count]
    out_ref, total_ref, rows_ref, bank_parts_ref, gathered_ref, chosen_ref, sent_ref = refs[7 + piece_count :]
    load_bank(bank_ref, bank_parts_ref)
    load_rows(pieces, rows_ref)
    total_ref[...] = before_ref[...]
    add_edges(sizes, ends_ref[1], words_ref, vector_words_ref, rows_ref, bank_parts_ref, total_ref, gathered_ref, chosen_ref, sent_ref)
    spread_high, spread_low = two_parts(spread_ref[...])

    def mix(chunk, _):
        start = pl.multiple_of(chunk * EDGES, EDGES)
        high, low = two_parts(total_ref[pl.ds(start, EDGES), :])
        mixed = jnp.dot(high, spread_high, preferred_element_type=jnp.float32)
        mixed += jnp.dot(high, spread_low, preferred_element_type=jnp.float32)
        mixed += jnp.dot(low, spread_high, preferred_element_type=jnp.float32)
        updated = own_ref[pl.ds(start, EDGES), :].astype(jnp.float32) + mixed
        out_ref[pl.ds(start, EDGES), :] = updated.astype(jnp.bfloat16)
        return 0

    lax.fori_loop(0, own_ref.shape[0] // EDGES, mix, 0)


def body(features, restriction, mixing, source_index, target_index, map_index, edge_counts):
    nodes, width = features.shape
    replicas = lax.axis_size("rep")
    near = replicas // 2
    half = nodes // 2
    maps, stalk, _ = restriction.shape
    channels = mixing.shape[0]
    capacity = source_index.shape[3]
    turns = source_index.shape[2]
    assert replicas == 2 * near and near & (near - 1) == 0 and turns == 2
    me = lax.axis_index("rep")

    live = lax.broadcasted_iota(jnp.int32, (turns, capacity), 1) < edge_counts[0, 0][:, None]
    own_edges = jnp.stack(
        [source_index[0, 0], jnp.where(live, target_index[0, 0], -1), map_index[0, 0]]
    )
    edges = jnp.stack([own_edges] + [swapped(own_edges, bit) for bit in range(1, replicas)], axis=2)
    sources, targets, map_ids = edges[0], edges[1], edges[2]

    across = swapped(features, near)
    before = passed_along(features, "blk", 1)
    block_pieces = spread_near(features, near) + spread_near(across, near)
    before_pieces = spread_near(before, near)
    late_low = swapped(before[:half], near)
    late_high = passed_along(across[half:], "blk", 1)
    late_pieces = [
        piece for pair in zip(spread_near(late_low, near), spread_near(late_high, near)) for piece in pair
    ]

    slot = (sources // nodes) ^ me
    local = sources % nodes
    turn = lax.broadcasted_iota(jnp.int32, sources.shape, 0)
    source_bits = bits_for((replicas + near) * nodes)
    target_bits = bits_for(nodes)
    assert source_bits + target_bits + bits_for(maps) <= 31
    mine = (targets >= 0) & (targets // nodes == me)
    rest = ((targets % nodes) << source_bits) | (map_ids << (source_bits + target_bits))
    soon = mine & ((turn == 0) | (slot < near))
    late = mine & (turn == 1) & (slot >= near)
    soon_words = jnp.where(soon, rest | ((turn * replicas + slot) * nodes + local), -1).reshape(-1)
    late_words = jnp.where(late, rest | ((slot - near) * nodes + local), -1)[1:].reshape(-1)
    counts = jnp.sum((targets >= 0).astype(jnp.int32), axis=2).reshape(-1)

    smem = pl.BlockSpec(memory_space=pltpu.SMEM)
    vmem = pl.BlockSpec(memory_space=pltpu.VMEM)
    soon_room = turns * replicas * capacity + EDGES
    late_room = replicas * capacity + EDGES
    soon_list, late_list, ends = pl.pallas_call(
        functools.partial(pick_kernel, capacity, replicas),
        out_shape=[
            jax.ShapeDtypeStruct((soon_room,), jnp.int32),
            jax.ShapeDtypeStruct((late_room,), jnp.int32),
            jax.ShapeDtypeStruct((2,), jnp.int32),
        ],
        in_specs=[smem] * 3,
        out_specs=[smem] * 3,
        cost_estimate=pl.CostEstimate(flops=0, bytes_accessed=60_000_000, transcendentals=0),
        name="pick_edges",
    )(counts, soon_words, late_words)

    sizes = (stalk, channels, maps, source_bits, target_bits, nodes)
    bank = restriction.reshape(maps, stalk * stalk).T
    spread = jnp.kron(jnp.eye(stalk, dtype=jnp.float32), mixing)

    def scratch(rows):
        return [
            pltpu.VMEM((rows, width), jnp.float32),
            pltpu.VMEM((stalk * stalk, 2 * maps), jnp.bfloat16),
            pltpu.VMEM((EDGES, width), jnp.float32),
            pltpu.VMEM((stalk * stalk, EDGES), jnp.float32),
            pltpu.VMEM((width, EDGES), jnp.bfloat16),
        ]

    pieces = block_pieces + before_pieces
    total = pl.pallas_call(
        functools.partial(soon_kernel, sizes, len(pieces)),
        out_shape=jax.ShapeDtypeStruct((nodes, width), jnp.float32),
        in_specs=[smem, smem] + [vmem] * (2 + len(pieces)),
        out_specs=vmem,
        scratch_shapes=scratch((replicas + near) * nodes),
        compiler_params=pltpu.CompilerParams(vmem_limit_bytes=VMEM_LIMIT),
        cost_estimate=pl.CostEstimate(flops=0, bytes_accessed=40_000_000, transcendentals=0),
        name="soon_edges",
    )(ends, soon_list, soon_list.reshape(-1, EDGES), bank, *pieces)

    return pl.pallas_call(
        functools.partial(late_kernel, sizes, len(late_pieces)),
        out_shape=jax.ShapeDtypeStruct((nodes, width), jnp.bfloat16),
        in_specs=[smem, smem] + [vmem] * (5 + len(late_pieces)),
        out_specs=vmem,
        scratch_shapes=[pltpu.VMEM((nodes, width), jnp.float32)] + scratch(near * nodes),
        compiler_params=pltpu.CompilerParams(vmem_limit_bytes=VMEM_LIMIT),
        cost_estimate=pl.CostEstimate(flops=0, bytes_accessed=20_000_000, transcendentals=0),
        name="late_edges",
    )(ends, late_list, late_list.reshape(-1, EDGES), bank, spread, features, total, *late_pieces)


def solution(mesh):
    in_specs = (
        P(("blk", "rep"), None),
        P(),
        P(),
        P("blk", "rep", None, None),
        P("blk", "rep", None, None),
        P("blk", "rep", None, None),
        P("blk", "rep", None),
    )
    out_specs = P(("blk", "rep"), None)
    return jax.shard_map(body, mesh=mesh, in_specs=in_specs, out_specs=out_specs, check_vma=False)
```

```python
import functools

import jax
import jax.numpy as jnp
from jax import lax
from jax.experimental import pallas as pl
from jax.experimental.pallas import tpu as pltpu
from jax.sharding import PartitionSpec as P

EDGES = 256
LANES = 128
UNROLL = 16
VMEM_LIMIT = 48 * 1024 * 1024


def bits_for(count):
    return max(1, (count - 1).bit_length())


def passed_along(block, axis, distance):
    devices = range(lax.axis_size(axis))
    route = [((i - distance) % len(devices), i) for i in devices]
    return lax.ppermute(block, axis, route)


def swapped(block, bit):
    route = [(i, i ^ bit) for i in range(lax.axis_size("rep"))]
    return lax.ppermute(block, "rep", route)


def spread_near(piece, near):
    pieces = [piece]
    bit = 1
    while bit < near:
        pieces = pieces + [swapped(p, bit) for p in pieces]
        bit *= 2
    return pieces


def pick_kernel(sizes, near, *refs):
    source_bits, target_bits, node_bits, capacity = sizes
    replicas = 2 * near
    edge_refs = refs[:replicas]
    lists, ends_ref = refs[replicas : replicas + 3], refs[replicas + 3]
    words_ref, scalar_words_ref, counts_ref, sems = refs[replicas + 4 :]
    rows = capacity // LANES
    me = lax.axis_index("rep")
    count_copies = []
    for k, edge_ref in enumerate(edge_refs):
        copy = pltpu.make_async_copy(edge_ref.at[pl.ds(6 * rows, 8)], counts_ref.at[pl.ds(8 * k, 8)], sems.at[k])
        copy.start()
        count_copies.append(copy)
    positions = lax.broadcasted_iota(jnp.int32, (rows, LANES), 0) * LANES + lax.broadcasted_iota(
        jnp.int32, (rows, LANES), 1
    )
    word_copies = []
    for turn in range(2):
        for k, edge_ref in enumerate(edge_refs):
            start = turn * 3 * rows
            source = edge_ref[start : start + rows, :]
            target = edge_ref[start + rows : start + 2 * rows, :]
            map_id = edge_ref[start + 2 * rows : start + 3 * rows, :]
            live = positions < edge_ref[6 * rows + turn : 6 * rows + turn + 1, :]
            mine = live & ((target >> node_bits) == me)
            slot = (source >> node_bits) ^ me
            far = slot >= near
            row = source & ((1 << node_bits) - 1)
            row += jnp.where(far, slot - near, slot + near * turn) << node_bits
            word = row | ((target & ((1 << node_bits) - 1)) << source_bits) | (map_id << (source_bits + target_bits))
            word |= jnp.where(far, jnp.int32(1 << 30), jnp.int32(-(1 << 31)))
            at = (turn * replicas + k) * rows
            words_ref[at : at + rows, :] = jnp.where(mine, word, 0)
        half = replicas * rows
        copy = pltpu.make_async_copy(
            words_ref.at[pl.ds(turn * half, half)], scalar_words_ref.at[pl.ds(turn * half, half)], sems.at[replicas + turn]
        )
        copy.start()
        word_copies.append(copy)
    for copy in count_copies:
        copy.wait()

    def scan(turn, near_list, far_list, ends):
        def over_tile(k, ends):
            first_row = (turn * replicas + k) * rows

            def some(i, ends):
                near_end, far_end = ends
                row = first_row + i // (LANES // UNROLL)
                lane = (i % (LANES // UNROLL)) * UNROLL
                words = [scalar_words_ref[row, lane + u] for u in range(UNROLL)]
                for word in words:
                    near_list[near_end] = word
                    far_list[far_end] = word
                    near_end += lax.shift_right_logical(word, 31)
                    far_end += lax.shift_right_logical(word, 30) & 1
                return near_end, far_end

            return lax.fori_loop(0, pl.cdiv(counts_ref[8 * k + turn, 0], UNROLL), some, ends)

        return lax.fori_loop(0, replicas, over_tile, ends)

    word_copies[0].wait()
    end0, end1 = scan(0, lists[0], lists[1], (jnp.int32(0), jnp.int32(0)))
    word_copies[1].wait()
    end1, end2 = scan(1, lists[1], lists[2], (end1, jnp.int32(0)))

    def fill(i, _):
        for u in range(UNROLL):
            for listed, end in zip(lists, (end0, end1, end2)):
                listed[end + i * UNROLL + u] = 0
        return 0

    lax.fori_loop(0, EDGES // UNROLL, fill, 0)
    for number, end in enumerate((end0, end1, end2)):
        ends_ref[number] = end


def cut_kernel(earlier_ref, before_ref, across_ref, low_ref, high_ref):
    half = low_ref.shape[0]
    low_ref[...] = before_ref[:half, :]
    high_ref[...] = across_ref[half:, :]


def join_kernel(earlier_ref, low_ref, high_ref, joined_ref):
    half = low_ref.shape[0]
    joined_ref[:half, :] = low_ref[...]
    joined_ref[half:, :] = high_ref[...]


def two_parts(value):
    high = value.astype(jnp.bfloat16)
    return high, (value - high.astype(jnp.float32)).astype(jnp.bfloat16)


def load_bank(bank_ref, bank_parts_ref):
    maps = bank_ref.shape[1]
    high, low = two_parts(bank_ref[...])
    bank_parts_ref[:, :maps] = high
    bank_parts_ref[:, maps:] = low


def load_rows(piece_refs, rows_ref):
    start = 0
    for ref in piece_refs:
        rows = ref.shape[0]

        def widen(i, _, ref=ref, start=start):
            at = pl.multiple_of(i * 256, 256)
            rows_ref[pl.ds(start + at, 256), :] = ref[pl.ds(at, 256), :].astype(jnp.float32)
            return 0

        lax.fori_loop(0, rows // 256, widen, 0)
        start += rows


def add_edges(sizes, count, words_ref, vector_words_ref, rows_ref, total_ref, bank_parts_ref, gathered_ref, chosen_ref, turned_ref, sent_ref):
    stalk, channels, maps, source_bits, target_bits, nodes = sizes
    source_mask = (1 << source_bits) - 1
    target_mask = (1 << target_bits) - 1
    map_mask = (1 << bits_for(maps)) - 1

    def add_block(block, _):
        first = block * EDGES

        def gather(i, _):
            at = pl.multiple_of(i * UNROLL, UNROLL)
            places = [words_ref[first + at + u] & source_mask for u in range(UNROLL)]
            values = [rows_ref[pl.ds(place, 1), :] for place in places]
            for u, value in enumerate(values):
                gathered_ref[pl.ds(at + u, 1), :] = value
            return 0

        lax.fori_loop(0, EDGES // UNROLL, gather, 0)
        words = vector_words_ref[pl.ds(block, 1), :]
        slots = first + lax.broadcasted_iota(jnp.int32, (1, EDGES), 1)
        targets = jnp.where(slots < count, (words >> source_bits) & target_mask, -1)
        map_ids = (words >> (source_bits + target_bits)) & map_mask
        wanted = (lax.broadcasted_iota(jnp.int32, (maps, EDGES), 0) == map_ids).astype(jnp.bfloat16)
        wanted = jnp.concatenate([wanted, wanted], axis=0)
        chosen_ref[...] = jnp.dot(bank_parts_ref[...], wanted, preferred_element_type=jnp.float32)
        for part in range(EDGES // LANES):
            lanes = slice(part * LANES, (part + 1) * LANES)
            features = gathered_ref[lanes, :].T
            for i in range(stalk):
                message = None
                for j in range(stalk):
                    factor = chosen_ref[i * stalk + j : i * stalk + j + 1, lanes]
                    term = factor * features[j * channels : (j + 1) * channels, :]
                    message = term if message is None else message + term
                turned_ref[i * channels : (i + 1) * channels, :] = message
            sent_ref[lanes, :] = turned_ref[...].T.astype(jnp.bfloat16)
        ids = lax.broadcasted_iota(jnp.int32, (EDGES, EDGES), 0).astype(jnp.bfloat16)
        one, zero = jnp.bfloat16(1), jnp.bfloat16(0)
        for start in range(0, nodes, 2 * EDGES):
            selectors = []
            for base in (start, start + EDGES):
                wanted_ids = (targets - base).astype(jnp.float32).astype(jnp.bfloat16)
                selectors.append(jnp.where(ids == wanted_ids, one, zero))
            selector = jnp.concatenate(selectors, axis=0)
            total_ref[start : start + 2 * EDGES, :] += jnp.dot(
                selector, sent_ref[...], preferred_element_type=jnp.float32
            )
        return 0

    lax.fori_loop(0, pl.cdiv(count, EDGES), add_block, 0)


def first_kernel(sizes, piece_count, ends_ref, words_ref, vector_words_ref, bank_ref, *refs):
    pieces, total_ref, (rows_ref, *scratch) = refs[:piece_count], refs[piece_count], refs[piece_count + 1 :]
    load_bank(bank_ref, scratch[0])
    load_rows(pieces, rows_ref)
    total_ref[...] = jnp.zeros_like(total_ref)
    add_edges(sizes, ends_ref[0], words_ref, vector_words_ref, rows_ref, total_ref, *scratch)


def second_kernel(sizes, piece_count, ends_ref, words_ref, vector_words_ref, bank_ref, before_ref, *refs):
    pieces, total_ref, (rows_ref, *scratch) = refs[:piece_count], refs[piece_count], refs[piece_count + 1 :]
    load_bank(bank_ref, scratch[0])
    load_rows(pieces, rows_ref)
    total_ref[...] = before_ref[...]
    add_edges(sizes, ends_ref[1], words_ref, vector_words_ref, rows_ref, total_ref, *scratch)


def last_kernel(sizes, piece_count, ends_ref, words_ref, vector_words_ref, bank_ref, before_ref, spread_ref, own_ref, *refs):
    pieces, out_ref, (total_ref, rows_ref, *scratch) = refs[:piece_count], refs[piece_count], refs[piece_count + 1 :]
    load_bank(bank_ref, scratch[0])
    load_rows(pieces, rows_ref)
    total_ref[...] = before_ref[...]
    add_edges(sizes, ends_ref[2], words_ref, vector_words_ref, rows_ref, total_ref, *scratch)
    spread_high, spread_low = two_parts(spread_ref[...])
    nodes = own_ref.shape[0]
    for start in range(0, nodes, 2 * EDGES):
        high, low = two_parts(total_ref[start : start + 2 * EDGES, :])
        mixed = jnp.dot(high, spread_high, preferred_element_type=jnp.float32)
        mixed += jnp.dot(high, spread_low, preferred_element_type=jnp.float32)
        mixed += jnp.dot(low, spread_high, preferred_element_type=jnp.float32)
        updated = own_ref[start : start + 2 * EDGES, :].astype(jnp.float32) + mixed
        out_ref[start : start + 2 * EDGES, :] = updated.astype(jnp.bfloat16)


def body(features, restriction, mixing, source_index, target_index, map_index, edge_counts):
    nodes, width = features.shape
    replicas = lax.axis_size("rep")
    near = replicas // 2
    half = nodes // 2
    maps, stalk, _ = restriction.shape
    channels = mixing.shape[0]
    capacity = source_index.shape[3]
    turns = source_index.shape[2]
    node_bits = bits_for(nodes)
    source_bits = bits_for(2 * near * nodes)
    assert replicas == 2 * near and near & (near - 1) == 0 and turns == 2
    assert nodes == 1 << node_bits and nodes % (2 * EDGES) == 0 and capacity % LANES == 0
    assert source_bits + node_bits + bits_for(maps) <= 30

    across = swapped(features, near)
    before = passed_along(features, "blk", 1)

    lists = [index[0, 0, turn].reshape(-1, LANES) for turn in range(turns) for index in (source_index, target_index, map_index)]
    counts = jnp.broadcast_to(edge_counts[0, 0][:, None], (turns, LANES))
    own_edges = jnp.concatenate(lists + [counts, jnp.zeros((8 - turns, LANES), jnp.int32)], axis=0)
    edges = [own_edges] + [swapped(own_edges, bit) for bit in range(1, replicas)]
    smem = pl.BlockSpec(memory_space=pltpu.SMEM)
    vmem = pl.BlockSpec(memory_space=pltpu.VMEM)
    rooms = [replicas * capacity + EDGES, turns * replicas * capacity + EDGES, replicas * capacity + EDGES]
    word_rows = turns * replicas * capacity // LANES
    *listed, ends = pl.pallas_call(
        functools.partial(pick_kernel, (source_bits, node_bits, node_bits, capacity), near),
        out_shape=[jax.ShapeDtypeStruct((room,), jnp.int32) for room in rooms] + [jax.ShapeDtypeStruct((3,), jnp.int32)],
        in_specs=[vmem] * replicas,
        out_specs=[smem] * 4,
        scratch_shapes=[
            pltpu.VMEM((word_rows, LANES), jnp.int32),
            pltpu.SMEM((word_rows, LANES), jnp.int32),
            pltpu.SMEM((8 * replicas, LANES), jnp.int32),
            pltpu.SemaphoreType.DMA((replicas + turns,)),
        ],
        cost_estimate=pl.CostEstimate(flops=0, bytes_accessed=40_000_000, transcendentals=0),
        name="pick_edges",
    )(*edges)

    sizes = (stalk, channels, maps, source_bits, node_bits, nodes)
    bank = restriction.reshape(maps, stalk * stalk).T
    spread = jnp.kron(jnp.eye(stalk, dtype=jnp.float32), mixing)

    def staged(number, kernel, operands, pieces, last=False):
        rows = sum(piece.shape[0] for piece in pieces)
        operands = [bank] + operands + pieces
        scratch = [pltpu.VMEM((nodes, width), jnp.float32)] if last else []
        return pl.pallas_call(
            functools.partial(kernel, sizes, len(pieces)),
            out_shape=jax.ShapeDtypeStruct((nodes, width), features.dtype if last else jnp.float32),
            in_specs=[smem, smem, vmem] + [vmem] * len(operands),
            out_specs=vmem,
            scratch_shapes=scratch
            + [
                pltpu.VMEM((rows, width), jnp.float32),
                pltpu.VMEM((stalk * stalk, 2 * maps), jnp.bfloat16),
                pltpu.VMEM((EDGES, width), jnp.float32),
                pltpu.VMEM((stalk * stalk, EDGES), jnp.float32),
                pltpu.VMEM((width, LANES), jnp.float32),
                pltpu.VMEM((EDGES, width), jnp.bfloat16),
            ],
            compiler_params=pltpu.CompilerParams(vmem_limit_bytes=VMEM_LIMIT),
            cost_estimate=pl.CostEstimate(flops=0, bytes_accessed=12_000_000, transcendentals=0),
            name=("first_edges", "second_edges", "last_edges")[number],
        )(ends, listed[number], listed[number].reshape(-1, EDGES), *operands)

    total = staged(0, first_kernel, [], spread_near(features, near))
    low, high = pl.pallas_call(
        cut_kernel,
        out_shape=[jax.ShapeDtypeStruct((half, width), features.dtype)] * 2,
        in_specs=[pl.BlockSpec(memory_space=pl.ANY), vmem, vmem],
        out_specs=[vmem] * 2,
        cost_estimate=pl.CostEstimate(flops=0, bytes_accessed=2_000_000, transcendentals=0),
        name="cut_halves",
    )(total, before, across)
    low = swapped(low, near)
    high = passed_along(high, "blk", 1)
    total = staged(1, second_kernel, [total], spread_near(across, near) + spread_near(before, near))
    joined = pl.pallas_call(
        join_kernel,
        out_shape=jax.ShapeDtypeStruct((nodes, width), features.dtype),
        in_specs=[pl.BlockSpec(memory_space=pl.ANY), vmem, vmem],
        out_specs=vmem,
        cost_estimate=pl.CostEstimate(flops=0, bytes_accessed=2_000_000, transcendentals=0),
        name="join_halves",
    )(total, low, high)
    return staged(2, last_kernel, [total, spread, features], spread_near(joined, near), last=True)


def solution(mesh):
    in_specs = (
        P(("blk", "rep"), None),
        P(),
        P(),
        P("blk", "rep", None, None),
        P("blk", "rep", None, None),
        P("blk", "rep", None, None),
        P("blk", "rep", None),
    )
    out_specs = P(("blk", "rep"), None)
    return jax.shard_map(body, mesh=mesh, in_specs=in_specs, out_specs=out_specs, check_vma=False)
```

```python
import functools

import jax
import jax.numpy as jnp
from jax import lax
from jax.experimental import pallas as pl
from jax.experimental.pallas import tpu as pltpu
from jax.sharding import PartitionSpec as P

EDGES = 256
LANES = 128
MIB = 1024 * 1024


def bits_for(count):
    return max(1, (count - 1).bit_length())


def passed_along(block, axis, distance):
    devices = range(lax.axis_size(axis))
    route = [((i - distance) % len(devices), i) for i in devices]
    return lax.ppermute(block, axis, route)


def swapped(block, bit):
    route = [(i, i ^ bit) for i in range(lax.axis_size("rep"))]
    return lax.ppermute(block, "rep", route)


def spread_near(piece, near):
    pieces = [piece]
    bit = 1
    while bit < near:
        pieces = pieces + [swapped(p, bit) for p in pieces]
        bit *= 2
    return pieces


def pack_kernel(counts_ref, *refs):
    index_refs, out_ref = refs[:-1], refs[-1]
    turns, capacity = index_refs[0].shape
    rows = capacity // LANES
    for turn in range(turns):
        for number, ref in enumerate(index_refs):
            start = (turn * len(index_refs) + number) * rows
            for row in range(rows):
                out_ref[start + row : start + row + 1, :] = ref[turn : turn + 1, row * LANES : (row + 1) * LANES]
    start = turns * len(index_refs) * rows
    out_ref[start:, :] = jnp.zeros((out_ref.shape[0] - start, LANES), jnp.int32)
    for turn in range(turns):
        out_ref[start + turn : start + turn + 1, :] = jnp.full((1, LANES), counts_ref[turn], jnp.int32)


def shifted_left(value, distance):
    rows = value.shape[0]
    if distance >= LANES:
        return pltpu.roll(value, rows - distance // LANES, 0)
    turned = pltpu.roll(value, LANES - distance, 1)
    lane = lax.broadcasted_iota(jnp.int32, value.shape, 1)
    return jnp.where(lane >= LANES - distance, pltpu.roll(turned, rows - 1, 0), turned)


def ones_where(condition):
    return jnp.where(condition, 1.0, 0.0).astype(jnp.bfloat16)


def closed_up(words):
    rows = words.shape[0]
    row = lax.broadcasted_iota(jnp.int32, (rows, LANES), 0)
    lane = lax.broadcasted_iota(jnp.int32, (rows, LANES), 1)
    used = ones_where(words != 0)
    upto = ones_where(lax.broadcasted_iota(jnp.int32, (LANES, LANES), 0) <= lax.broadcasted_iota(jnp.int32, (LANES, LANES), 1))
    above = ones_where(lax.broadcasted_iota(jnp.int32, (rows, rows), 1) < lax.broadcasted_iota(jnp.int32, (rows, rows), 0))
    every = jnp.ones((LANES, LANES), jnp.bfloat16)
    dot = functools.partial(jnp.dot, preferred_element_type=jnp.float32)
    earlier = dot(dot(above, used).astype(jnp.bfloat16), every)
    number = (earlier + dot(used, upto)).astype(jnp.int32)
    total = dot(dot(jnp.ones((8, rows), jnp.bfloat16), used).astype(jnp.bfloat16), every).astype(jnp.int32)
    way = jnp.where(words != 0, row * LANES + lane + 1 - number, 0)
    for bit in range(bits_for(rows * LANES)):
        moves = ((way >> bit) & 1) == 1
        moved_words = shifted_left(jnp.where(moves, words, 0), 1 << bit)
        moved_way = shifted_left(jnp.where(moves, way, 0), 1 << bit)
        words = jnp.where(moves, 0, words) | moved_words
        way = jnp.where(moves, 0, way) | moved_way
    return words, total


def pick_kernel(sizes, near, *refs):
    source_bits, target_bits, node_bits, capacity = sizes
    replicas = 2 * near
    edge_refs = refs[:replicas]
    word_refs, place_refs = refs[replicas : replicas + 3], refs[replicas + 3 : replicas + 6]
    candidates_ref = refs[replicas + 6]
    rows = capacity // LANES
    node_mask = (1 << node_bits) - 1
    me = lax.axis_index("rep")
    positions = lax.broadcasted_iota(jnp.int32, (rows, LANES), 0) * LANES + lax.broadcasted_iota(
        jnp.int32, (rows, LANES), 1
    )
    part = replicas * rows
    for turn in range(2):
        for k, edge_ref in enumerate(edge_refs):
            start = turn * 3 * rows
            source = edge_ref[start : start + rows, :]
            target = edge_ref[start + rows : start + 2 * rows, :]
            map_id = edge_ref[start + 2 * rows : start + 3 * rows, :]
            live = positions < edge_ref[6 * rows + turn : 6 * rows + turn + 1, :]
            mine = live & ((target >> node_bits) == me)
            slot = (source >> node_bits) ^ me
            far = slot >= near
            row = source & node_mask
            row += jnp.where(far, slot - near, slot + near * turn) << node_bits
            word = row | ((target & node_mask) << source_bits) | (map_id << (source_bits + target_bits)) | (1 << 30)
            at = k * rows
            candidates_ref[2 * turn * part + at : 2 * turn * part + at + rows, :] = jnp.where(mine & ~far, word, 0)
            candidates_ref[(2 * turn + 1) * part + at : (2 * turn + 1) * part + at + rows, :] = jnp.where(
                mine & far, word, 0
            )
    for number, (start, stop) in enumerate(((0, part), (part, 3 * part), (3 * part, 4 * part))):
        words, total = closed_up(candidates_ref[start:stop, :])
        word_refs[number][...] = words
        place_refs[number][: stop - start, :] = (words & ((1 << source_bits) - 1)) * 2
        place_refs[number][stop - start :, :] = total


def tables_kernel(bank_ref, mixing_ref, bank_parts_ref, spread_high_ref, spread_low_ref):
    maps = bank_ref.shape[1]
    channels = mixing_ref.shape[0]
    width = spread_high_ref.shape[0]
    high, low = two_parts(bank_ref[...])
    bank_parts_ref[:, :maps] = high
    bank_parts_ref[:, maps:] = low
    dot = functools.partial(jnp.dot, preferred_element_type=jnp.float32)
    down = ones_where(
        lax.broadcasted_iota(jnp.int32, (width, channels), 0) % channels
        == lax.broadcasted_iota(jnp.int32, (width, channels), 1)
    )
    across = ones_where(
        lax.broadcasted_iota(jnp.int32, (channels, width), 1) % channels
        == lax.broadcasted_iota(jnp.int32, (channels, width), 0)
    )
    same = lax.broadcasted_iota(jnp.int32, (width, width), 0) // channels == (
        lax.broadcasted_iota(jnp.int32, (width, width), 1) // channels
    )
    for part, ref in zip(two_parts(mixing_ref[...]), (spread_high_ref, spread_low_ref)):
        tiled = dot(dot(down, part).astype(jnp.bfloat16), across)
        ref[...] = jnp.where(same, tiled, 0.0).astype(jnp.bfloat16)


def after_kernel(earlier_ref, *refs):
    pass


def two_parts(value):
    high = value.astype(jnp.bfloat16)
    return high, (value - high.astype(jnp.float32)).astype(jnp.bfloat16)


def load_rows(piece_refs, rows_ref):
    start = 0
    for ref in piece_refs:
        rows = ref.shape[0]

        def widen(i, _, ref=ref, start=start):
            at = pl.multiple_of(i * EDGES, EDGES)
            value = ref[pl.ds(at, EDGES), :].astype(jnp.float32)
            for half in range(2):
                rows_ref[pl.ds(2 * (start + at) + half, EDGES, stride=2), :] = value[:, half * LANES : (half + 1) * LANES]
            return 0

        lax.fori_loop(0, rows // EDGES, widen, 0)
        start += rows


def add_edges(sizes, words_ref, rows_ref, places_ref, total_ref, bank_parts_ref, gathered_ref, turned_ref, chosen_ref, message_ref, sent_ref):
    stalk, channels, maps, source_bits, target_bits, nodes = sizes
    target_mask = (1 << target_bits) - 1
    map_mask = (1 << bits_for(maps)) - 1
    lists = EDGES // LANES
    blocks = words_ref.shape[0] // lists
    count = places_ref[words_ref.shape[0], 0]

    def gather(block):
        for u in range(EDGES):
            place = pl.multiple_of(places_ref[block * lists + u // LANES, u % LANES], 2)
            gathered_ref[2 * u : 2 * u + 2, :] = rows_ref[pl.ds(place, 2), :]

    def add_block(block, _):
        for part in range(lists):
            lanes = slice(part * LANES, (part + 1) * LANES)
            for half in range(2):
                values = gathered_ref[pl.ds(2 * part * LANES + half, LANES, stride=2), :]
                turned_ref[half * LANES : (half + 1) * LANES, lanes] = values.T
        gather(jnp.minimum(block + 1, blocks - 1))
        words = jnp.concatenate([words_ref[pl.ds(block * lists + part, 1), :] for part in range(lists)], axis=1)
        targets = jnp.where(words != 0, (words >> source_bits) & target_mask, -1)
        map_ids = (words >> (source_bits + target_bits)) & map_mask
        wanted = ones_where(lax.broadcasted_iota(jnp.int32, (maps, EDGES), 0) == map_ids)
        wanted = jnp.concatenate([wanted, wanted], axis=0)
        chosen_ref[...] = jnp.dot(bank_parts_ref[...], wanted, preferred_element_type=jnp.float32)
        for part in range(lists):
            lanes = slice(part * LANES, (part + 1) * LANES)
            features = turned_ref[:, lanes]
            for i in range(stalk):
                message = None
                for j in range(stalk):
                    factor = chosen_ref[i * stalk + j : i * stalk + j + 1, lanes]
                    term = factor * features[j * channels : (j + 1) * channels, :]
                    message = term if message is None else message + term
                message_ref[i * channels : (i + 1) * channels, lanes] = message
            sent_ref[lanes, :] = message_ref[:, lanes].T.astype(jnp.bfloat16)
        ids = lax.broadcasted_iota(jnp.int32, (EDGES, EDGES), 0).astype(jnp.bfloat16)
        one, zero = jnp.bfloat16(1), jnp.bfloat16(0)
        for start in range(0, nodes, 2 * EDGES):
            selectors = []
            for base in (start, start + EDGES):
                wanted_ids = (targets - base).astype(jnp.float32).astype(jnp.bfloat16)
                selectors.append(jnp.where(ids == wanted_ids, one, zero))
            selector = jnp.concatenate(selectors, axis=0)
            total_ref[start : start + 2 * EDGES, :] += jnp.dot(
                selector, sent_ref[...], preferred_element_type=jnp.float32
            )
        return 0

    gather(0)
    lax.fori_loop(0, pl.cdiv(count, EDGES), add_block, 0)


def stage_kernel(sizes, piece_count, stage, words_ref, listed_ref, bank_parts_ref, *refs):
    pieces, refs = refs[:piece_count], refs[piece_count:]
    if stage == "first":
        total_ref, *scratch = refs
    elif stage == "second":
        _, total_ref, *scratch = refs
    else:
        _, spread_high_ref, spread_low_ref, own_ref, out_ref, total_ref, *scratch = refs
    rows_ref, places_ref, sem, *scratch = scratch
    copy = pltpu.make_async_copy(listed_ref, places_ref, sem)
    copy.start()
    if stage == "first":
        total_ref[...] = jnp.zeros_like(total_ref)
    load_rows(pieces, rows_ref)
    copy.wait()
    add_edges(sizes, words_ref, rows_ref, places_ref, total_ref, bank_parts_ref, *scratch)
    if stage == "last":
        spread_high, spread_low = spread_high_ref[...], spread_low_ref[...]
        for start in range(0, own_ref.shape[0], 2 * EDGES):
            high, low = two_parts(total_ref[start : start + 2 * EDGES, :])
            mixed = jnp.dot(high, spread_high, preferred_element_type=jnp.float32)
            mixed += jnp.dot(high, spread_low, preferred_element_type=jnp.float32)
            mixed += jnp.dot(low, spread_high, preferred_element_type=jnp.float32)
            updated = own_ref[start : start + 2 * EDGES, :].astype(jnp.float32) + mixed
            out_ref[start : start + 2 * EDGES, :] = updated.astype(jnp.bfloat16)


def kernel_call(kernel, name, out_shape, in_specs, out_specs, cost, scratch=(), vmem=MIB, aliases=None):
    return pl.pallas_call(
        kernel,
        out_shape=out_shape,
        in_specs=in_specs,
        out_specs=out_specs,
        scratch_shapes=list(scratch),
        input_output_aliases=aliases or {},
        compiler_params=pltpu.CompilerParams(vmem_limit_bytes=vmem),
        cost_estimate=pl.CostEstimate(flops=0, bytes_accessed=cost, transcendentals=0),
        name=name,
    )


def body(features, restriction, mixing, source_index, target_index, map_index, edge_counts):
    nodes, width = features.shape
    replicas = lax.axis_size("rep")
    near = replicas // 2
    half = nodes // 2
    maps, stalk, _ = restriction.shape
    channels = mixing.shape[0]
    capacity = source_index.shape[3]
    turns = source_index.shape[2]
    node_bits = bits_for(nodes)
    source_bits = bits_for(2 * near * nodes)
    assert replicas == 2 * near and near & (near - 1) == 0 and turns == 2
    assert nodes == 1 << node_bits and nodes % (2 * EDGES) == 0 and capacity % LANES == 0
    assert source_bits + node_bits + bits_for(maps) <= 30

    across = swapped(features, near)
    before = passed_along(features, "blk", 1)

    smem = pl.BlockSpec(memory_space=pltpu.SMEM)
    vmem = pl.BlockSpec(memory_space=pltpu.VMEM)
    anywhere = pl.BlockSpec(memory_space=pl.ANY)
    own_edges = kernel_call(
        pack_kernel,
        "pack_edges",
        jax.ShapeDtypeStruct((3 * turns * capacity // LANES + 8, LANES), jnp.int32),
        [smem] + [vmem] * 3,
        vmem,
        1_000_000,
    )(edge_counts[0, 0], source_index[0, 0], target_index[0, 0], map_index[0, 0])
    edges = [own_edges] + [swapped(own_edges, bit) for bit in range(1, replicas)]
    part = replicas * capacity // LANES
    list_rows = (part, 2 * part, part)
    listed = kernel_call(
        functools.partial(pick_kernel, (source_bits, node_bits, node_bits, capacity), near),
        "pick_edges",
        [jax.ShapeDtypeStruct((rows, LANES), jnp.int32) for rows in list_rows]
        + [jax.ShapeDtypeStruct((rows + 8, LANES), jnp.int32) for rows in list_rows],
        [vmem] * replicas,
        [vmem] * 6,
        8_000_000,
        scratch=[pltpu.VMEM((4 * part, LANES), jnp.int32)],
        vmem=4 * MIB,
    )(*edges)
    table_shapes = [(stalk * stalk, 2 * maps), (width, width), (width, width)]
    bank_parts, spread_high, spread_low = kernel_call(
        tables_kernel,
        "tables",
        [jax.ShapeDtypeStruct(shape, jnp.bfloat16) for shape in table_shapes],
        [vmem] * 2,
        [vmem] * 3,
        1_000_000,
        vmem=4 * MIB,
    )(restriction.reshape(maps, stalk * stalk).T, mixing)

    sizes = (stalk, channels, maps, source_bits, node_bits, nodes)
    total_shape = jax.ShapeDtypeStruct((nodes, width), jnp.float32)

    def staged(number, stage, pieces, operands):
        rows = sum(piece.shape[0] for piece in pieces)
        operands = [listed[number], listed[number + 3], bank_parts] + pieces + operands
        aliases = {}
        out_shape = total_shape
        if stage != "first":
            aliases = {3 + len(pieces): 1 if stage == "last" else 0}
        if stage == "last":
            out_shape = [jax.ShapeDtypeStruct((nodes, width), features.dtype), total_shape]
        return kernel_call(
            functools.partial(stage_kernel, sizes, len(pieces), stage),
            stage + "_edges",
            out_shape,
            [vmem] * len(operands),
            [vmem] * 2 if stage == "last" else vmem,
            12_000_000,
            scratch=[
                pltpu.VMEM((2 * rows, LANES), jnp.float32),
                pltpu.SMEM((list_rows[number] + 8, LANES), jnp.int32),
                pltpu.SemaphoreType.DMA,
                pltpu.VMEM((2 * EDGES, LANES), jnp.float32),
                pltpu.VMEM((width, EDGES), jnp.float32),
                pltpu.VMEM((stalk * stalk, EDGES), jnp.float32),
                pltpu.VMEM((width, EDGES), jnp.float32),
                pltpu.VMEM((EDGES, width), jnp.bfloat16),
            ],
            vmem=rows * width * 4 + 6 * MIB,
            aliases=aliases,
        )(*operands)

    def after(earlier, *values):
        return kernel_call(
            after_kernel,
            "after",
            [jax.ShapeDtypeStruct(value.shape, value.dtype) for value in values],
            [anywhere] * (1 + len(values)),
            [anywhere] * len(values),
            100_000,
            aliases={1 + number: number for number in range(len(values))},
        )(earlier, *values)

    total = staged(0, "first", spread_near(features, near), [])
    across, before = after(total, across, before)
    low = swapped(before[:half], near)
    high = passed_along(across[half:], "blk", 1)
    total = staged(1, "second", spread_near(across, near) + spread_near(before, near), [total])
    low, high = after(total, low, high)
    far = [piece for pair in zip(spread_near(low, near), spread_near(high, near)) for piece in pair]
    updated, _ = staged(2, "last", far, [total, spread_high, spread_low, features])
    return updated


def solution(mesh):
    in_specs = (
        P(("blk", "rep"), None),
        P(),
        P(),
        P("blk", "rep", None, None),
        P("blk", "rep", None, None),
        P("blk", "rep", None, None),
        P("blk", "rep", None),
    )
    out_specs = P(("blk", "rep"), None)
    return jax.shard_map(body, mesh=mesh, in_specs=in_specs, out_specs=out_specs, check_vma=False)
```

```python
import functools

import jax
import jax.numpy as jnp
from jax import lax
from jax.experimental import pallas as pl
from jax.experimental.pallas import tpu as pltpu
from jax.sharding import PartitionSpec as P

EDGES = 256
LANES = 128
MIB = 1024 * 1024


def bits_for(count):
    return max(1, (count - 1).bit_length())


def passed_along(block, axis, distance):
    devices = range(lax.axis_size(axis))
    route = [((i - distance) % len(devices), i) for i in devices]
    return lax.ppermute(block, axis, route)


def swapped(block, bit):
    route = [(i, i ^ bit) for i in range(lax.axis_size("rep"))]
    return lax.ppermute(block, "rep", route)


def spread_near(piece, near):
    pieces = [piece]
    bit = 1
    while bit < near:
        pieces = pieces + [swapped(p, bit) for p in pieces]
        bit *= 2
    return pieces


def pack_kernel(counts_ref, source_ref, target_ref, map_ref, features_ref, out_ref, low_ref, high_ref, *scratch):
    *index_refs, counts_here, sems = scratch
    half = low_ref.shape[0]
    pairs = [
        (counts_ref, counts_here),
        (source_ref, index_refs[0]),
        (target_ref, index_refs[1]),
        (map_ref, index_refs[2]),
        (features_ref.at[pl.ds(0, half)], low_ref),
        (features_ref.at[pl.ds(half, half)], high_ref),
    ]
    copies = [pltpu.make_async_copy(start, end, sems.at[i]) for i, (start, end) in enumerate(pairs)]
    for copy in copies:
        copy.start()
    turns, capacity = index_refs[0].shape
    rows = capacity // LANES
    start = turns * len(index_refs) * rows
    out_ref[start:, :] = jnp.zeros((out_ref.shape[0] - start, LANES), jnp.int32)
    for copy in copies[:4]:
        copy.wait()
    for turn in range(turns):
        for number, ref in enumerate(index_refs):
            at = (turn * len(index_refs) + number) * rows
            for row in range(rows):
                out_ref[at + row : at + row + 1, :] = ref[turn : turn + 1, row * LANES : (row + 1) * LANES]
        out_ref[start + turn : start + turn + 1, :] = jnp.full((1, LANES), counts_here[turn], jnp.int32)
    for copy in copies[4:]:
        copy.wait()


def shifted_left(value, distance):
    rows = value.shape[0]
    if distance >= LANES:
        return pltpu.roll(value, rows - distance // LANES, 0)
    turned = pltpu.roll(value, LANES - distance, 1)
    lane = lax.broadcasted_iota(jnp.int32, value.shape, 1)
    return jnp.where(lane >= LANES - distance, pltpu.roll(turned, rows - 1, 0), turned)


def ones_where(condition):
    return jnp.where(condition, 1.0, 0.0).astype(jnp.bfloat16)


def closed_up(words):
    rows = words.shape[0]
    row = lax.broadcasted_iota(jnp.int32, (rows, LANES), 0)
    lane = lax.broadcasted_iota(jnp.int32, (rows, LANES), 1)
    used = ones_where(words != 0)
    upto = ones_where(lax.broadcasted_iota(jnp.int32, (LANES, LANES), 0) <= lax.broadcasted_iota(jnp.int32, (LANES, LANES), 1))
    above = ones_where(lax.broadcasted_iota(jnp.int32, (rows, rows), 1) < lax.broadcasted_iota(jnp.int32, (rows, rows), 0))
    every = jnp.ones((LANES, LANES), jnp.bfloat16)
    dot = functools.partial(jnp.dot, preferred_element_type=jnp.float32)
    earlier = dot(dot(above, used).astype(jnp.bfloat16), every)
    number = (earlier + dot(used, upto)).astype(jnp.int32)
    total = dot(dot(jnp.ones((8, rows), jnp.bfloat16), used).astype(jnp.bfloat16), every).astype(jnp.int32)
    way = jnp.where(words != 0, row * LANES + lane + 1 - number, 0)
    for bit in range(bits_for(rows * LANES)):
        moves = ((way >> bit) & 1) == 1
        moved_words = shifted_left(jnp.where(moves, words, 0), 1 << bit)
        moved_way = shifted_left(jnp.where(moves, way, 0), 1 << bit)
        words = jnp.where(moves, 0, words) | moved_words
        way = jnp.where(moves, 0, way) | moved_way
    return words, total


def pick_kernel(sizes, near, *refs):
    source_bits, target_bits, node_bits, capacity = sizes
    replicas = 2 * near
    edge_refs = refs[:replicas]
    word_refs, place_refs = refs[replicas : replicas + 3], refs[replicas + 3 : replicas + 6]
    candidates_ref = refs[replicas + 6]
    rows = capacity // LANES
    node_mask = (1 << node_bits) - 1
    me = lax.axis_index("rep")
    positions = lax.broadcasted_iota(jnp.int32, (rows, LANES), 0) * LANES + lax.broadcasted_iota(
        jnp.int32, (rows, LANES), 1
    )
    part = replicas * rows
    for turn in range(2):
        for k, edge_ref in enumerate(edge_refs):
            start = turn * 3 * rows
            source = edge_ref[start : start + rows, :]
            target = edge_ref[start + rows : start + 2 * rows, :]
            map_id = edge_ref[start + 2 * rows : start + 3 * rows, :]
            live = positions < edge_ref[6 * rows + turn : 6 * rows + turn + 1, :]
            mine = live & ((target >> node_bits) == me)
            slot = (source >> node_bits) ^ me
            far = slot >= near
            row = source & node_mask
            row += jnp.where(far, slot - near, slot + near * turn) << node_bits
            word = row | ((target & node_mask) << source_bits) | (map_id << (source_bits + target_bits)) | (1 << 30)
            at = k * rows
            candidates_ref[2 * turn * part + at : 2 * turn * part + at + rows, :] = jnp.where(mine & ~far, word, 0)
            candidates_ref[(2 * turn + 1) * part + at : (2 * turn + 1) * part + at + rows, :] = jnp.where(
                mine & far, word, 0
            )
    for number, (start, stop) in enumerate(((0, part), (part, 3 * part), (3 * part, 4 * part))):
        words, total = closed_up(candidates_ref[start:stop, :])
        word_refs[number][...] = words
        place_refs[number][: stop - start, :] = (words & ((1 << source_bits) - 1)) * 2
        place_refs[number][stop - start :, :] = total


def tables_kernel(bank_ref, mixing_ref, bank_parts_ref, spread_high_ref, spread_low_ref):
    maps = bank_ref.shape[1]
    channels = mixing_ref.shape[0]
    width = spread_high_ref.shape[0]
    high, low = two_parts(bank_ref[...])
    bank_parts_ref[:, :maps] = high
    bank_parts_ref[:, maps:] = low
    dot = functools.partial(jnp.dot, preferred_element_type=jnp.float32)
    down = ones_where(
        lax.broadcasted_iota(jnp.int32, (width, channels), 0) % channels
        == lax.broadcasted_iota(jnp.int32, (width, channels), 1)
    )
    across = ones_where(
        lax.broadcasted_iota(jnp.int32, (channels, width), 1) % channels
        == lax.broadcasted_iota(jnp.int32, (channels, width), 0)
    )
    same = lax.broadcasted_iota(jnp.int32, (width, width), 0) // channels == (
        lax.broadcasted_iota(jnp.int32, (width, width), 1) // channels
    )
    for part, ref in zip(two_parts(mixing_ref[...]), (spread_high_ref, spread_low_ref)):
        tiled = dot(dot(down, part).astype(jnp.bfloat16), across)
        ref[...] = jnp.where(same, tiled, 0.0).astype(jnp.bfloat16)


def after_kernel(*refs):
    pass


def two_parts(value):
    high = value.astype(jnp.bfloat16)
    return high, (value - high.astype(jnp.float32)).astype(jnp.bfloat16)


def load_rows(piece_refs, rows_ref):
    start = 0
    for ref in piece_refs:
        rows = ref.shape[0]

        def widen(i, _, ref=ref, start=start):
            at = pl.multiple_of(i * EDGES, EDGES)
            value = ref[pl.ds(at, EDGES), :].astype(jnp.float32)
            for half in range(2):
                rows_ref[pl.ds(2 * (start + at) + half, EDGES, stride=2), :] = value[:, half * LANES : (half + 1) * LANES]
            return 0

        lax.fori_loop(0, rows // EDGES, widen, 0)
        start += rows


def add_edges(sizes, words_ref, rows_ref, places_ref, total_ref, bank_parts_ref, gathered_ref, turned_ref, chosen_ref, message_ref, sent_ref):
    stalk, channels, maps, source_bits, target_bits, nodes = sizes
    target_mask = (1 << target_bits) - 1
    map_mask = (1 << bits_for(maps)) - 1
    lists = EDGES // LANES
    blocks = words_ref.shape[0] // lists
    count = places_ref[words_ref.shape[0], 0]

    def gather(block):
        for u in range(EDGES):
            place = pl.multiple_of(places_ref[block * lists + u // LANES, u % LANES], 2)
            gathered_ref[2 * u : 2 * u + 2, :] = rows_ref[pl.ds(place, 2), :]

    def add_block(block, _):
        for part in range(lists):
            lanes = slice(part * LANES, (part + 1) * LANES)
            for half in range(2):
                values = gathered_ref[pl.ds(2 * part * LANES + half, LANES, stride=2), :]
                turned_ref[half * LANES : (half + 1) * LANES, lanes] = values.T
        gather(jnp.minimum(block + 1, blocks - 1))
        words = jnp.concatenate([words_ref[pl.ds(block * lists + part, 1), :] for part in range(lists)], axis=1)
        targets = jnp.where(words != 0, (words >> source_bits) & target_mask, -1)
        map_ids = (words >> (source_bits + target_bits)) & map_mask
        wanted = ones_where(lax.broadcasted_iota(jnp.int32, (maps, EDGES), 0) == map_ids)
        wanted = jnp.concatenate([wanted, wanted], axis=0)
        chosen_ref[...] = jnp.dot(bank_parts_ref[...], wanted, preferred_element_type=jnp.float32)
        for part in range(lists):
            lanes = slice(part * LANES, (part + 1) * LANES)
            features = turned_ref[:, lanes]
            for i in range(stalk):
                message = None
                for j in range(stalk):
                    factor = chosen_ref[i * stalk + j : i * stalk + j + 1, lanes]
                    term = factor * features[j * channels : (j + 1) * channels, :]
                    message = term if message is None else message + term
                message_ref[i * channels : (i + 1) * channels, lanes] = message
            sent_ref[lanes, :] = message_ref[:, lanes].T.astype(jnp.bfloat16)
        ids = lax.broadcasted_iota(jnp.int32, (EDGES, EDGES), 0).astype(jnp.bfloat16)
        one, zero = jnp.bfloat16(1), jnp.bfloat16(0)
        for start in range(0, nodes, 2 * EDGES):
            selectors = []
            for base in (start, start + EDGES):
                wanted_ids = (targets - base).astype(jnp.float32).astype(jnp.bfloat16)
                selectors.append(jnp.where(ids == wanted_ids, one, zero))
            selector = jnp.concatenate(selectors, axis=0)
            total_ref[start : start + 2 * EDGES, :] += jnp.dot(
                selector, sent_ref[...], preferred_element_type=jnp.float32
            )
        return 0

    gather(0)
    lax.fori_loop(0, pl.cdiv(count, EDGES), add_block, 0)


def stage_kernel(sizes, piece_count, stage, words_ref, listed_ref, bank_parts_ref, *refs):
    pieces, refs = refs[:piece_count], refs[piece_count:]
    if stage == "first":
        total_ref, *scratch = refs
    elif stage == "second":
        _, total_ref, *scratch = refs
    else:
        _, spread_high_ref, spread_low_ref, own_ref, out_ref, total_ref, *scratch = refs
    rows_ref, places_ref, sem, *scratch = scratch
    copy = pltpu.make_async_copy(listed_ref, places_ref, sem)
    copy.start()
    if stage == "first":
        total_ref[...] = jnp.zeros_like(total_ref)
    load_rows(pieces, rows_ref)
    copy.wait()
    add_edges(sizes, words_ref, rows_ref, places_ref, total_ref, bank_parts_ref, *scratch)
    if stage == "last":
        spread_high, spread_low = spread_high_ref[...], spread_low_ref[...]
        for start in range(0, own_ref.shape[0], 2 * EDGES):
            high, low = two_parts(total_ref[start : start + 2 * EDGES, :])
            mixed = jnp.dot(high, spread_high, preferred_element_type=jnp.float32)
            mixed += jnp.dot(high, spread_low, preferred_element_type=jnp.float32)
            mixed += jnp.dot(low, spread_high, preferred_element_type=jnp.float32)
            updated = own_ref[start : start + 2 * EDGES, :].astype(jnp.float32) + mixed
            out_ref[start : start + 2 * EDGES, :] = updated.astype(jnp.bfloat16)


def kernel_call(kernel, name, out_shape, in_specs, out_specs, cost, scratch=(), vmem=MIB, aliases=None):
    return pl.pallas_call(
        kernel,
        out_shape=out_shape,
        in_specs=in_specs,
        out_specs=out_specs,
        scratch_shapes=list(scratch),
        input_output_aliases=aliases or {},
        compiler_params=pltpu.CompilerParams(vmem_limit_bytes=vmem),
        cost_estimate=pl.CostEstimate(flops=0, bytes_accessed=cost, transcendentals=0),
        name=name,
    )


def body(features, restriction, mixing, source_index, target_index, map_index, edge_counts):
    nodes, width = features.shape
    replicas = lax.axis_size("rep")
    near = replicas // 2
    half = nodes // 2
    maps, stalk, _ = restriction.shape
    channels = mixing.shape[0]
    capacity = source_index.shape[3]
    turns = source_index.shape[2]
    node_bits = bits_for(nodes)
    source_bits = bits_for(2 * near * nodes)
    assert replicas == 2 * near and near & (near - 1) == 0 and turns == 2
    assert nodes == 1 << node_bits and nodes % (2 * EDGES) == 0 and capacity % LANES == 0
    assert source_bits + node_bits + bits_for(maps) <= 30

    smem = pl.BlockSpec(memory_space=pltpu.SMEM)
    vmem = pl.BlockSpec(memory_space=pltpu.VMEM)
    anywhere = pl.BlockSpec(memory_space=pl.ANY)

    def after(earlier, *values):
        earlier = list(earlier)
        return kernel_call(
            after_kernel,
            "after",
            [jax.ShapeDtypeStruct(value.shape, value.dtype) for value in values],
            [anywhere] * (len(earlier) + len(values)),
            [anywhere] * len(values),
            100_000,
            aliases={len(earlier) + number: number for number in range(len(values))},
        )(*earlier, *values)

    half_shape = jax.ShapeDtypeStruct((half, width), features.dtype)
    own_edges, low, high = kernel_call(
        pack_kernel,
        "pack_edges",
        [jax.ShapeDtypeStruct((3 * turns * capacity // LANES + 8, LANES), jnp.int32), half_shape, half_shape],
        [anywhere] * 5,
        [vmem, anywhere, anywhere],
        1_000_000,
        scratch=[pltpu.VMEM((turns, capacity), jnp.int32)] * 3
        + [pltpu.SMEM((turns,), jnp.int32), pltpu.SemaphoreType.DMA((6,))],
        vmem=None,
    )(edge_counts[0, 0], source_index[0, 0], target_index[0, 0], map_index[0, 0], features)
    across_high = swapped(high, near)
    before_low = passed_along(low, "blk", 1)
    edges = [own_edges] + [swapped(own_edges, bit) for bit in range(1, replicas)]
    low, high = after(edges[1:2], low, high)
    across_low = swapped(low, near)
    before_high = passed_along(high, "blk", 1)
    across_high, before_low = after(edges[1:], across_high, before_low)
    far_low = swapped(before_low, near)
    far_high = passed_along(across_high, "blk", 1)
    part = replicas * capacity // LANES
    list_rows = (part, 2 * part, part)
    listed = kernel_call(
        functools.partial(pick_kernel, (source_bits, node_bits, node_bits, capacity), near),
        "pick_edges",
        [jax.ShapeDtypeStruct((rows, LANES), jnp.int32) for rows in list_rows]
        + [jax.ShapeDtypeStruct((rows + 8, LANES), jnp.int32) for rows in list_rows],
        [vmem] * replicas,
        [vmem] * 6,
        8_000_000,
        scratch=[pltpu.VMEM((4 * part, LANES), jnp.int32)],
        vmem=4 * MIB,
    )(*edges)
    table_shapes = [(stalk * stalk, 2 * maps), (width, width), (width, width)]
    bank_parts, spread_high, spread_low = kernel_call(
        tables_kernel,
        "tables",
        [jax.ShapeDtypeStruct(shape, jnp.bfloat16) for shape in table_shapes],
        [vmem] * 2,
        [vmem] * 3,
        1_000_000,
        vmem=4 * MIB,
    )(restriction.reshape(maps, stalk * stalk).T, mixing)

    sizes = (stalk, channels, maps, source_bits, node_bits, nodes)
    total_shape = jax.ShapeDtypeStruct((nodes, width), jnp.float32)

    def staged(number, stage, pieces, operands):
        rows = sum(piece.shape[0] for piece in pieces)
        operands = [listed[number], listed[number + 3], bank_parts] + pieces + operands
        aliases = {}
        out_shape = total_shape
        if stage != "first":
            aliases = {3 + len(pieces): 1 if stage == "last" else 0}
        if stage == "last":
            out_shape = [jax.ShapeDtypeStruct((nodes, width), features.dtype), total_shape]
        return kernel_call(
            functools.partial(stage_kernel, sizes, len(pieces), stage),
            stage + "_edges",
            out_shape,
            [vmem] * len(operands),
            [vmem] * 2 if stage == "last" else vmem,
            12_000_000,
            scratch=[
                pltpu.VMEM((2 * rows, LANES), jnp.float32),
                pltpu.SMEM((list_rows[number] + 8, LANES), jnp.int32),
                pltpu.SemaphoreType.DMA,
                pltpu.VMEM((2 * EDGES, LANES), jnp.float32),
                pltpu.VMEM((width, EDGES), jnp.float32),
                pltpu.VMEM((stalk * stalk, EDGES), jnp.float32),
                pltpu.VMEM((width, EDGES), jnp.float32),
                pltpu.VMEM((EDGES, width), jnp.bfloat16),
            ],
            vmem=rows * width * 4 + 6 * MIB,
            aliases=aliases,
        )(*operands)

    def joined(low, high):
        return [piece for pair in zip(spread_near(low, near), spread_near(high, near)) for piece in pair]

    total = staged(0, "first", spread_near(features, near), [])
    across_low, before_high = after([total], across_low, before_high)
    total = staged(1, "second", joined(across_low, across_high) + joined(before_low, before_high), [total])
    far_low, far_high = after([total], far_low, far_high)
    updated, _ = staged(2, "last", joined(far_low, far_high), [total, spread_high, spread_low, features])
    return updated


def solution(mesh):
    in_specs = (
        P(("blk", "rep"), None),
        P(),
        P(),
        P("blk", "rep", None, None),
        P("blk", "rep", None, None),
        P("blk", "rep", None, None),
        P("blk", "rep", None),
    )
    out_specs = P(("blk", "rep"), None)
    return jax.shard_map(body, mesh=mesh, in_specs=in_specs, out_specs=out_specs, check_vma=False)
```

```python
import functools

import jax
import jax.numpy as jnp
from jax import lax
from jax.experimental import pallas as pl
from jax.experimental.pallas import tpu as pltpu
from jax.sharding import PartitionSpec as P

EDGES = 256
LANES = 128
MIB = 1024 * 1024


def bits_for(count):
    return max(1, (count - 1).bit_length())


def passed_along(block, axis, distance):
    devices = range(lax.axis_size(axis))
    route = [((i - distance) % len(devices), i) for i in devices]
    return lax.ppermute(block, axis, route)


def swapped(block, bit):
    route = [(i, i ^ bit) for i in range(lax.axis_size("rep"))]
    return lax.ppermute(block, "rep", route)


def spread_near(piece, near):
    pieces = [piece]
    bit = 1
    while bit < near:
        pieces = pieces + [swapped(p, bit) for p in pieces]
        bit *= 2
    return pieces


def pack_kernel(counts_ref, _, *refs):
    index_refs, out_ref = refs[:-1], refs[-1]
    turns, capacity = index_refs[0].shape
    rows = capacity // LANES
    for turn in range(turns):
        for number, ref in enumerate(index_refs):
            start = (turn * len(index_refs) + number) * rows
            for row in range(rows):
                out_ref[start + row : start + row + 1, :] = ref[turn : turn + 1, row * LANES : (row + 1) * LANES]
    start = turns * len(index_refs) * rows
    out_ref[start:, :] = jnp.zeros((out_ref.shape[0] - start, LANES), jnp.int32)
    for turn in range(turns):
        out_ref[start + turn : start + turn + 1, :] = jnp.full((1, LANES), counts_ref[turn], jnp.int32)


def shifted_left(value, distance):
    rows = value.shape[0]
    if distance >= LANES:
        return pltpu.roll(value, rows - distance // LANES, 0)
    turned = pltpu.roll(value, LANES - distance, 1)
    lane = lax.broadcasted_iota(jnp.int32, value.shape, 1)
    return jnp.where(lane >= LANES - distance, pltpu.roll(turned, rows - 1, 0), turned)


def ones_where(condition):
    return jnp.where(condition, 1.0, 0.0).astype(jnp.bfloat16)


def closed_up(words):
    rows = words.shape[0]
    row = lax.broadcasted_iota(jnp.int32, (rows, LANES), 0)
    lane = lax.broadcasted_iota(jnp.int32, (rows, LANES), 1)
    used = ones_where(words != 0)
    upto = ones_where(lax.broadcasted_iota(jnp.int32, (LANES, LANES), 0) <= lax.broadcasted_iota(jnp.int32, (LANES, LANES), 1))
    above = ones_where(lax.broadcasted_iota(jnp.int32, (rows, rows), 1) < lax.broadcasted_iota(jnp.int32, (rows, rows), 0))
    every = jnp.ones((LANES, LANES), jnp.bfloat16)
    dot = functools.partial(jnp.dot, preferred_element_type=jnp.float32)
    earlier = dot(dot(above, used).astype(jnp.bfloat16), every)
    number = (earlier + dot(used, upto)).astype(jnp.int32)
    total = dot(dot(jnp.ones((8, rows), jnp.bfloat16), used).astype(jnp.bfloat16), every).astype(jnp.int32)
    way = jnp.where(words != 0, row * LANES + lane + 1 - number, 0)
    for bit in range(bits_for(rows * LANES)):
        moves = ((way >> bit) & 1) == 1
        moved_words = shifted_left(jnp.where(moves, words, 0), 1 << bit)
        moved_way = shifted_left(jnp.where(moves, way, 0), 1 << bit)
        words = jnp.where(moves, 0, words) | moved_words
        way = jnp.where(moves, 0, way) | moved_way
    return words, total


def pick_kernel(sizes, near, *refs):
    source_bits, target_bits, node_bits, capacity = sizes
    replicas = 2 * near
    edge_refs = refs[:replicas]
    word_refs, place_refs = refs[replicas : replicas + 3], refs[replicas + 3 : replicas + 6]
    candidates_ref = refs[replicas + 6]
    rows = capacity // LANES
    node_mask = (1 << node_bits) - 1
    me = lax.axis_index("rep")
    positions = lax.broadcasted_iota(jnp.int32, (rows, LANES), 0) * LANES + lax.broadcasted_iota(
        jnp.int32, (rows, LANES), 1
    )
    part = replicas * rows
    for turn in range(2):
        for k, edge_ref in enumerate(edge_refs):
            start = turn * 3 * rows
            source = edge_ref[start : start + rows, :]
            target = edge_ref[start + rows : start + 2 * rows, :]
            map_id = edge_ref[start + 2 * rows : start + 3 * rows, :]
            live = positions < edge_ref[6 * rows + turn : 6 * rows + turn + 1, :]
            mine = live & ((target >> node_bits) == me)
            slot = (source >> node_bits) ^ me
            far = slot >= near
            row = source & node_mask
            row += jnp.where(far, slot - near, slot + near * turn) << node_bits
            word = row | ((target & node_mask) << source_bits) | (map_id << (source_bits + target_bits)) | (1 << 30)
            at = k * rows
            candidates_ref[2 * turn * part + at : 2 * turn * part + at + rows, :] = jnp.where(mine & ~far, word, 0)
            candidates_ref[(2 * turn + 1) * part + at : (2 * turn + 1) * part + at + rows, :] = jnp.where(
                mine & far, word, 0
            )
    for number, (start, stop) in enumerate(((0, part), (part, 3 * part), (3 * part, 4 * part))):
        words, total = closed_up(candidates_ref[start:stop, :])
        word_refs[number][...] = words
        place_refs[number][: stop - start, :] = (words & ((1 << source_bits) - 1)) * 2
        place_refs[number][stop - start :, :] = total


def tables_kernel(bank_ref, mixing_ref, bank_parts_ref, spread_high_ref, spread_low_ref):
    maps = bank_ref.shape[1]
    channels = mixing_ref.shape[0]
    width = spread_high_ref.shape[0]
    high, low = two_parts(bank_ref[...])
    bank_parts_ref[:, :maps] = high
    bank_parts_ref[:, maps:] = low
    dot = functools.partial(jnp.dot, preferred_element_type=jnp.float32)
    down = ones_where(
        lax.broadcasted_iota(jnp.int32, (width, channels), 0) % channels
        == lax.broadcasted_iota(jnp.int32, (width, channels), 1)
    )
    across = ones_where(
        lax.broadcasted_iota(jnp.int32, (channels, width), 1) % channels
        == lax.broadcasted_iota(jnp.int32, (channels, width), 0)
    )
    same = lax.broadcasted_iota(jnp.int32, (width, width), 0) // channels == (
        lax.broadcasted_iota(jnp.int32, (width, width), 1) // channels
    )
    for part, ref in zip(two_parts(mixing_ref[...]), (spread_high_ref, spread_low_ref)):
        tiled = dot(dot(down, part).astype(jnp.bfloat16), across)
        ref[...] = jnp.where(same, tiled, 0.0).astype(jnp.bfloat16)


def after_kernel(*refs):
    pass


def two_parts(value):
    high = value.astype(jnp.bfloat16)
    return high, (value - high.astype(jnp.float32)).astype(jnp.bfloat16)


def load_rows(piece_refs, rows_ref):
    start = 0
    for ref in piece_refs:
        rows = ref.shape[0]

        def widen(i, _, ref=ref, start=start):
            at = pl.multiple_of(i * EDGES, EDGES)
            value = ref[pl.ds(at, EDGES), :].astype(jnp.float32)
            for half in range(2):
                rows_ref[pl.ds(2 * (start + at) + half, EDGES, stride=2), :] = value[:, half * LANES : (half + 1) * LANES]
            return 0

        lax.fori_loop(0, rows // EDGES, widen, 0)
        start += rows


def add_edges(sizes, words_ref, rows_ref, places_ref, total_ref, bank_parts_ref, gathered_ref, turned_ref, chosen_ref, message_ref, sent_ref):
    stalk, channels, maps, source_bits, target_bits, nodes = sizes
    target_mask = (1 << target_bits) - 1
    map_mask = (1 << bits_for(maps)) - 1
    lists = EDGES // LANES
    blocks = words_ref.shape[0] // lists
    count = places_ref[words_ref.shape[0], 0]

    def gather(block):
        for u in range(EDGES):
            place = pl.multiple_of(places_ref[block * lists + u // LANES, u % LANES], 2)
            gathered_ref[2 * u : 2 * u + 2, :] = rows_ref[pl.ds(place, 2), :]

    def add_block(block, _):
        for part in range(lists):
            lanes = slice(part * LANES, (part + 1) * LANES)
            for half in range(2):
                values = gathered_ref[pl.ds(2 * part * LANES + half, LANES, stride=2), :]
                turned_ref[half * LANES : (half + 1) * LANES, lanes] = values.T
        gather(jnp.minimum(block + 1, blocks - 1))
        words = jnp.concatenate([words_ref[pl.ds(block * lists + part, 1), :] for part in range(lists)], axis=1)
        targets = jnp.where(words != 0, (words >> source_bits) & target_mask, -1)
        map_ids = (words >> (source_bits + target_bits)) & map_mask
        wanted = ones_where(lax.broadcasted_iota(jnp.int32, (maps, EDGES), 0) == map_ids)
        wanted = jnp.concatenate([wanted, wanted], axis=0)
        chosen_ref[...] = jnp.dot(bank_parts_ref[...], wanted, preferred_element_type=jnp.float32)
        for part in range(lists):
            lanes = slice(part * LANES, (part + 1) * LANES)
            features = turned_ref[:, lanes]
            for i in range(stalk):
                message = None
                for j in range(stalk):
                    factor = chosen_ref[i * stalk + j : i * stalk + j + 1, lanes]
                    term = factor * features[j * channels : (j + 1) * channels, :]
                    message = term if message is None else message + term
                message_ref[i * channels : (i + 1) * channels, lanes] = message
            sent_ref[lanes, :] = message_ref[:, lanes].T.astype(jnp.bfloat16)
        ids = lax.broadcasted_iota(jnp.int32, (EDGES, EDGES), 0).astype(jnp.bfloat16)
        one, zero = jnp.bfloat16(1), jnp.bfloat16(0)
        for start in range(0, nodes, 2 * EDGES):
            selectors = []
            for base in (start, start + EDGES):
                wanted_ids = (targets - base).astype(jnp.float32).astype(jnp.bfloat16)
                selectors.append(jnp.where(ids == wanted_ids, one, zero))
            selector = jnp.concatenate(selectors, axis=0)
            total_ref[start : start + 2 * EDGES, :] += jnp.dot(
                selector, sent_ref[...], preferred_element_type=jnp.float32
            )
        return 0

    gather(0)
    lax.fori_loop(0, pl.cdiv(count, EDGES), add_block, 0)


def stage_kernel(sizes, piece_count, stage, words_ref, listed_ref, bank_parts_ref, *refs):
    pieces, refs = refs[:piece_count], refs[piece_count:]
    if stage == "first":
        total_ref, *scratch = refs
    elif stage == "second":
        _, total_ref, *scratch = refs
    else:
        _, spread_high_ref, spread_low_ref, own_ref, out_ref, total_ref, *scratch = refs
    rows_ref, places_ref, sem, *scratch = scratch
    copy = pltpu.make_async_copy(listed_ref, places_ref, sem)
    copy.start()
    if stage == "first":
        total_ref[...] = jnp.zeros_like(total_ref)
    load_rows(pieces, rows_ref)
    copy.wait()
    add_edges(sizes, words_ref, rows_ref, places_ref, total_ref, bank_parts_ref, *scratch)
    if stage == "last":
        spread_high, spread_low = spread_high_ref[...], spread_low_ref[...]
        for start in range(0, own_ref.shape[0], 2 * EDGES):
            high, low = two_parts(total_ref[start : start + 2 * EDGES, :])
            mixed = jnp.dot(high, spread_high, preferred_element_type=jnp.float32)
            mixed += jnp.dot(high, spread_low, preferred_element_type=jnp.float32)
            mixed += jnp.dot(low, spread_high, preferred_element_type=jnp.float32)
            updated = own_ref[start : start + 2 * EDGES, :].astype(jnp.float32) + mixed
            out_ref[start : start + 2 * EDGES, :] = updated.astype(jnp.bfloat16)


def kernel_call(kernel, name, out_shape, in_specs, out_specs, cost, scratch=(), vmem=MIB, aliases=None):
    return pl.pallas_call(
        kernel,
        out_shape=out_shape,
        in_specs=in_specs,
        out_specs=out_specs,
        scratch_shapes=list(scratch),
        input_output_aliases=aliases or {},
        compiler_params=pltpu.CompilerParams(vmem_limit_bytes=vmem),
        cost_estimate=pl.CostEstimate(flops=0, bytes_accessed=cost, transcendentals=0),
        name=name,
    )


def body(features, restriction, mixing, source_index, target_index, map_index, edge_counts):
    nodes, width = features.shape
    replicas = lax.axis_size("rep")
    near = replicas // 2
    half = nodes // 2
    maps, stalk, _ = restriction.shape
    channels = mixing.shape[0]
    capacity = source_index.shape[3]
    turns = source_index.shape[2]
    node_bits = bits_for(nodes)
    source_bits = bits_for(2 * near * nodes)
    assert replicas == 2 * near and near & (near - 1) == 0 and turns == 2
    assert nodes == 1 << node_bits and nodes % (2 * EDGES) == 0 and capacity % LANES == 0
    assert source_bits + node_bits + bits_for(maps) <= 30

    smem = pl.BlockSpec(memory_space=pltpu.SMEM)
    vmem = pl.BlockSpec(memory_space=pltpu.VMEM)
    anywhere = pl.BlockSpec(memory_space=pl.ANY)

    def after(earlier, *values):
        earlier = list(earlier)
        return kernel_call(
            after_kernel,
            "after",
            [jax.ShapeDtypeStruct(value.shape, value.dtype) for value in values],
            [anywhere] * (len(earlier) + len(values)),
            [anywhere] * len(values),
            100_000,
            aliases={len(earlier) + number: number for number in range(len(values))},
        )(*earlier, *values)

    before = passed_along(features, "blk", 1)
    low = features[:half]
    across_low = swapped(low, near)
    own_edges = kernel_call(
        pack_kernel,
        "pack_edges",
        jax.ShapeDtypeStruct((3 * turns * capacity // LANES + 8, LANES), jnp.int32),
        [smem, anywhere] + [vmem] * 3,
        vmem,
        1_000_000,
    )(edge_counts[0, 0], low, source_index[0, 0], target_index[0, 0], map_index[0, 0])
    edges = [own_edges] + [swapped(own_edges, bit) for bit in range(1, replicas)]
    *edges[1:], across_low, high = after([], *edges[1:], across_low, features[half:])
    across_high = swapped(high, near)
    far_low = passed_along(across_low, "blk", 1)
    part = replicas * capacity // LANES
    list_rows = (part, 2 * part, part)
    listed = kernel_call(
        functools.partial(pick_kernel, (source_bits, node_bits, node_bits, capacity), near),
        "pick_edges",
        [jax.ShapeDtypeStruct((rows, LANES), jnp.int32) for rows in list_rows]
        + [jax.ShapeDtypeStruct((rows + 8, LANES), jnp.int32) for rows in list_rows],
        [vmem] * replicas,
        [vmem] * 6,
        8_000_000,
        scratch=[pltpu.VMEM((4 * part, LANES), jnp.int32)],
        vmem=4 * MIB,
    )(*edges)
    table_shapes = [(stalk * stalk, 2 * maps), (width, width), (width, width)]
    bank_parts, spread_high, spread_low = kernel_call(
        tables_kernel,
        "tables",
        [jax.ShapeDtypeStruct(shape, jnp.bfloat16) for shape in table_shapes],
        [vmem] * 2,
        [vmem] * 3,
        1_000_000,
        vmem=4 * MIB,
    )(restriction.reshape(maps, stalk * stalk).T, mixing)

    sizes = (stalk, channels, maps, source_bits, node_bits, nodes)
    total_shape = jax.ShapeDtypeStruct((nodes, width), jnp.float32)

    def staged(number, stage, pieces, operands):
        rows = sum(piece.shape[0] for piece in pieces)
        operands = [listed[number], listed[number + 3], bank_parts] + pieces + operands
        aliases = {}
        out_shape = total_shape
        if stage != "first":
            aliases = {3 + len(pieces): 1 if stage == "last" else 0}
        if stage == "last":
            out_shape = [jax.ShapeDtypeStruct((nodes, width), features.dtype), total_shape]
        return kernel_call(
            functools.partial(stage_kernel, sizes, len(pieces), stage),
            stage + "_edges",
            out_shape,
            [vmem] * len(operands),
            [vmem] * 2 if stage == "last" else vmem,
            12_000_000,
            scratch=[
                pltpu.VMEM((2 * rows, LANES), jnp.float32),
                pltpu.SMEM((list_rows[number] + 8, LANES), jnp.int32),
                pltpu.SemaphoreType.DMA,
                pltpu.VMEM((2 * EDGES, LANES), jnp.float32),
                pltpu.VMEM((width, EDGES), jnp.float32),
                pltpu.VMEM((stalk * stalk, EDGES), jnp.float32),
                pltpu.VMEM((width, EDGES), jnp.float32),
                pltpu.VMEM((EDGES, width), jnp.bfloat16),
            ],
            vmem=rows * width * 4 + 6 * MIB,
            aliases=aliases,
        )(*operands)

    def joined(low, high):
        return [piece for pair in zip(spread_near(low, near), spread_near(high, near)) for piece in pair]

    total = staged(0, "first", spread_near(features, near), [])
    across_high, before = after([total], across_high, before)
    far_high = swapped(before[half:], near)
    total = staged(1, "second", joined(across_low, across_high) + spread_near(before, near), [total])
    far_low, far_high = after([total], far_low, far_high)
    updated, _ = staged(2, "last", joined(far_low, far_high), [total, spread_high, spread_low, features])
    return updated


def solution(mesh):
    in_specs = (
        P(("blk", "rep"), None),
        P(),
        P(),
        P("blk", "rep", None, None),
        P("blk", "rep", None, None),
        P("blk", "rep", None, None),
        P("blk", "rep", None),
    )
    out_specs = P(("blk", "rep"), None)
    return jax.shard_map(body, mesh=mesh, in_specs=in_specs, out_specs=out_specs, check_vma=False)
```

```python
import functools

import jax
import jax.numpy as jnp
from jax import lax
from jax.experimental import pallas as pl
from jax.experimental.pallas import tpu as pltpu
from jax.sharding import PartitionSpec as P

EDGES = 256
LANES = 128
MIB = 1024 * 1024


def bits_for(count):
    return max(1, (count - 1).bit_length())


def passed_along(block, axis, distance):
    devices = range(lax.axis_size(axis))
    route = [((i - distance) % len(devices), i) for i in devices]
    return lax.ppermute(block, axis, route)


def swapped(block, bit):
    route = [(i, i ^ bit) for i in range(lax.axis_size("rep"))]
    return lax.ppermute(block, "rep", route)


def spread_near(piece, near):
    pieces = [piece]
    bit = 1
    while bit < near:
        pieces = pieces + [swapped(p, bit) for p in pieces]
        bit *= 2
    return pieces


def pack_kernel(counts_ref, _, *refs):
    index_refs, out_ref = refs[:-1], refs[-1]
    turns, capacity = index_refs[0].shape
    rows = capacity // LANES
    for turn in range(turns):
        for number, ref in enumerate(index_refs):
            start = (turn * len(index_refs) + number) * rows
            for row in range(rows):
                out_ref[start + row : start + row + 1, :] = ref[turn : turn + 1, row * LANES : (row + 1) * LANES]
    start = turns * len(index_refs) * rows
    out_ref[start:, :] = jnp.zeros((out_ref.shape[0] - start, LANES), jnp.int32)
    for turn in range(turns):
        out_ref[start + turn : start + turn + 1, :] = jnp.full((1, LANES), counts_ref[turn], jnp.int32)


def shifted_left(value, distance):
    rows = value.shape[0]
    if distance >= LANES:
        return pltpu.roll(value, rows - distance // LANES, 0)
    turned = pltpu.roll(value, LANES - distance, 1)
    lane = lax.broadcasted_iota(jnp.int32, value.shape, 1)
    return jnp.where(lane >= LANES - distance, pltpu.roll(turned, rows - 1, 0), turned)


def ones_where(condition):
    return jnp.where(condition, 1.0, 0.0).astype(jnp.bfloat16)


def closed_up(words):
    rows = words.shape[0]
    row = lax.broadcasted_iota(jnp.int32, (rows, LANES), 0)
    lane = lax.broadcasted_iota(jnp.int32, (rows, LANES), 1)
    used = ones_where(words != 0)
    upto = ones_where(lax.broadcasted_iota(jnp.int32, (LANES, LANES), 0) <= lax.broadcasted_iota(jnp.int32, (LANES, LANES), 1))
    above = ones_where(lax.broadcasted_iota(jnp.int32, (rows, rows), 1) < lax.broadcasted_iota(jnp.int32, (rows, rows), 0))
    every = jnp.ones((LANES, LANES), jnp.bfloat16)
    dot = functools.partial(jnp.dot, preferred_element_type=jnp.float32)
    earlier = dot(dot(above, used).astype(jnp.bfloat16), every)
    number = (earlier + dot(used, upto)).astype(jnp.int32)
    total = dot(dot(jnp.ones((8, rows), jnp.bfloat16), used).astype(jnp.bfloat16), every).astype(jnp.int32)
    way = jnp.where(words != 0, row * LANES + lane + 1 - number, 0)
    for bit in range(bits_for(rows * LANES)):
        moves = ((way >> bit) & 1) == 1
        moved_words = shifted_left(jnp.where(moves, words, 0), 1 << bit)
        moved_way = shifted_left(jnp.where(moves, way, 0), 1 << bit)
        words = jnp.where(moves, 0, words) | moved_words
        way = jnp.where(moves, 0, way) | moved_way
    return words, total


def pick_kernel(sizes, near, *refs):
    source_bits, target_bits, node_bits, capacity = sizes
    replicas = 2 * near
    edge_refs, refs = refs[:replicas], refs[replicas:]
    word_refs, place_refs, candidates_ref = refs[:4], refs[4:8], refs[8]
    rows = capacity // LANES
    node_mask = (1 << node_bits) - 1
    me = lax.axis_index("rep")
    positions = lax.broadcasted_iota(jnp.int32, (rows, LANES), 0) * LANES + lax.broadcasted_iota(
        jnp.int32, (rows, LANES), 1
    )
    part = replicas * rows
    for turn in range(2):
        for k, edge_ref in enumerate(edge_refs):
            start = turn * 3 * rows
            source = edge_ref[start : start + rows, :]
            target = edge_ref[start + rows : start + 2 * rows, :]
            map_id = edge_ref[start + 2 * rows : start + 3 * rows, :]
            live = positions < edge_ref[6 * rows + turn : 6 * rows + turn + 1, :]
            mine = live & ((target >> node_bits) == me)
            slot = (source >> node_bits) ^ me
            far = slot >= near
            slot = slot & (near - 1)
            straight = slot == 0
            rest = (source & node_mask) | ((target & node_mask) << source_bits)
            rest |= (map_id << (source_bits + target_bits)) | (1 << 30)
            in_own = rest | (slot << node_bits)
            in_straight = rest | (turn << node_bits)
            in_turned = rest | ((turn * (near - 1) + slot - 1) << node_bits)
            ends = mine & ~far if turn == 0 else mine & far
            others = mine & far if turn == 0 else mine & ~far
            at = k * rows
            choices = (
                (0 if turn == 0 else 5 * part, ends, in_own),
                (part + turn * part, others & straight, in_straight),
                (3 * part + turn * part, others & ~straight, in_turned),
            )
            for first, chosen, word in choices:
                candidates_ref[first + at : first + at + rows, :] = jnp.where(chosen, word, 0)
    for number, (start, stop) in enumerate(((0, part), (part, 3 * part), (3 * part, 5 * part), (5 * part, 6 * part))):
        words, total = closed_up(candidates_ref[start:stop, :])
        word_refs[number][...] = words
        place_refs[number][: stop - start, :] = (words & ((1 << source_bits) - 1)) * 2
        place_refs[number][stop - start :, :] = total


def tables_kernel(bank_ref, mixing_ref, bank_parts_ref, spread_high_ref, spread_low_ref):
    maps = bank_ref.shape[1]
    channels = mixing_ref.shape[0]
    width = spread_high_ref.shape[0]
    high, low = two_parts(bank_ref[...])
    bank_parts_ref[:, :maps] = high
    bank_parts_ref[:, maps:] = low
    dot = functools.partial(jnp.dot, preferred_element_type=jnp.float32)
    down = ones_where(
        lax.broadcasted_iota(jnp.int32, (width, channels), 0) % channels
        == lax.broadcasted_iota(jnp.int32, (width, channels), 1)
    )
    across = ones_where(
        lax.broadcasted_iota(jnp.int32, (channels, width), 1) % channels
        == lax.broadcasted_iota(jnp.int32, (channels, width), 0)
    )
    same = lax.broadcasted_iota(jnp.int32, (width, width), 0) // channels == (
        lax.broadcasted_iota(jnp.int32, (width, width), 1) // channels
    )
    for part, ref in zip(two_parts(mixing_ref[...]), (spread_high_ref, spread_low_ref)):
        tiled = dot(dot(down, part).astype(jnp.bfloat16), across)
        ref[...] = jnp.where(same, tiled, 0.0).astype(jnp.bfloat16)


def after_kernel(*refs):
    pass


def two_parts(value):
    high = value.astype(jnp.bfloat16)
    return high, (value - high.astype(jnp.float32)).astype(jnp.bfloat16)


def load_rows(piece_refs, rows_ref):
    start = 0
    for ref in piece_refs:
        rows = ref.shape[0]

        def widen(i, _, ref=ref, start=start):
            at = pl.multiple_of(i * EDGES, EDGES)
            value = ref[pl.ds(at, EDGES), :].astype(jnp.float32)
            for half in range(2):
                rows_ref[pl.ds(2 * (start + at) + half, EDGES, stride=2), :] = value[:, half * LANES : (half + 1) * LANES]
            return 0

        lax.fori_loop(0, rows // EDGES, widen, 0)
        start += rows


def add_edges(sizes, words_ref, rows_ref, places_ref, total_ref, bank_parts_ref, gathered_ref, turned_ref, chosen_ref, message_ref, sent_ref):
    stalk, channels, maps, source_bits, target_bits, nodes = sizes
    target_mask = (1 << target_bits) - 1
    map_mask = (1 << bits_for(maps)) - 1
    lists = EDGES // LANES
    blocks = words_ref.shape[0] // lists
    count = places_ref[words_ref.shape[0], 0]

    def gather(block):
        for u in range(EDGES):
            place = pl.multiple_of(places_ref[block * lists + u // LANES, u % LANES], 2)
            gathered_ref[2 * u : 2 * u + 2, :] = rows_ref[pl.ds(place, 2), :]

    def add_block(block, _):
        for part in range(lists):
            lanes = slice(part * LANES, (part + 1) * LANES)
            for half in range(2):
                values = gathered_ref[pl.ds(2 * part * LANES + half, LANES, stride=2), :]
                turned_ref[half * LANES : (half + 1) * LANES, lanes] = values.T
        gather(jnp.minimum(block + 1, blocks - 1))
        words = jnp.concatenate([words_ref[pl.ds(block * lists + part, 1), :] for part in range(lists)], axis=1)
        targets = jnp.where(words != 0, (words >> source_bits) & target_mask, -1)
        map_ids = (words >> (source_bits + target_bits)) & map_mask
        wanted = ones_where(lax.broadcasted_iota(jnp.int32, (maps, EDGES), 0) == map_ids)
        wanted = jnp.concatenate([wanted, wanted], axis=0)
        chosen_ref[...] = jnp.dot(bank_parts_ref[...], wanted, preferred_element_type=jnp.float32)
        for part in range(lists):
            lanes = slice(part * LANES, (part + 1) * LANES)
            features = turned_ref[:, lanes]
            for i in range(stalk):
                message = None
                for j in range(stalk):
                    factor = chosen_ref[i * stalk + j : i * stalk + j + 1, lanes]
                    term = factor * features[j * channels : (j + 1) * channels, :]
                    message = term if message is None else message + term
                message_ref[i * channels : (i + 1) * channels, lanes] = message
            sent_ref[lanes, :] = message_ref[:, lanes].T.astype(jnp.bfloat16)
        ids = lax.broadcasted_iota(jnp.int32, (EDGES, EDGES), 0).astype(jnp.bfloat16)
        one, zero = jnp.bfloat16(1), jnp.bfloat16(0)
        for start in range(0, nodes, 2 * EDGES):
            selectors = []
            for base in (start, start + EDGES):
                wanted_ids = (targets - base).astype(jnp.float32).astype(jnp.bfloat16)
                selectors.append(jnp.where(ids == wanted_ids, one, zero))
            selector = jnp.concatenate(selectors, axis=0)
            total_ref[start : start + 2 * EDGES, :] += jnp.dot(
                selector, sent_ref[...], preferred_element_type=jnp.float32
            )
        return 0

    gather(0)
    lax.fori_loop(0, pl.cdiv(count, EDGES), add_block, 0)


def stage_kernel(sizes, piece_count, stage, words_ref, listed_ref, bank_parts_ref, *refs):
    pieces, refs = refs[:piece_count], refs[piece_count:]
    if stage == "first":
        total_ref, *scratch = refs
    elif stage != "last":
        _, total_ref, *scratch = refs
    else:
        _, spread_high_ref, spread_low_ref, own_ref, out_ref, total_ref, *scratch = refs
    rows_ref, places_ref, sem, *scratch = scratch
    copy = pltpu.make_async_copy(listed_ref, places_ref, sem)
    copy.start()
    if stage == "first":
        total_ref[...] = jnp.zeros_like(total_ref)
    load_rows(pieces, rows_ref)
    copy.wait()
    add_edges(sizes, words_ref, rows_ref, places_ref, total_ref, bank_parts_ref, *scratch)
    if stage == "last":
        spread_high, spread_low = spread_high_ref[...], spread_low_ref[...]
        for start in range(0, own_ref.shape[0], 2 * EDGES):
            high, low = two_parts(total_ref[start : start + 2 * EDGES, :])
            mixed = jnp.dot(high, spread_high, preferred_element_type=jnp.float32)
            mixed += jnp.dot(high, spread_low, preferred_element_type=jnp.float32)
            mixed += jnp.dot(low, spread_high, preferred_element_type=jnp.float32)
            updated = own_ref[start : start + 2 * EDGES, :].astype(jnp.float32) + mixed
            out_ref[start : start + 2 * EDGES, :] = updated.astype(jnp.bfloat16)


def kernel_call(kernel, name, out_shape, in_specs, out_specs, scratch=(), vmem=MIB, aliases=None):
    return pl.pallas_call(
        kernel,
        out_shape=out_shape,
        in_specs=in_specs,
        out_specs=out_specs,
        scratch_shapes=list(scratch),
        input_output_aliases=aliases or {},
        compiler_params=pltpu.CompilerParams(vmem_limit_bytes=vmem),
        cost_estimate=pl.CostEstimate(flops=0, bytes_accessed=1_000, transcendentals=0),
        name=name,
    )


def body(features, restriction, mixing, source_index, target_index, map_index, edge_counts):
    nodes, width = features.shape
    replicas = lax.axis_size("rep")
    near = replicas // 2
    split = nodes // 2
    maps, stalk, _ = restriction.shape
    channels = mixing.shape[0]
    capacity = source_index.shape[3]
    turns = source_index.shape[2]
    node_bits = bits_for(nodes)
    source_bits = bits_for(2 * near * nodes)
    assert replicas == 2 * near and near > 1 and near & (near - 1) == 0 and turns == 2
    assert nodes == 1 << node_bits and nodes % (8 * EDGES) == 0 and capacity % LANES == 0
    assert source_bits + node_bits + bits_for(maps) <= 30

    smem = pl.BlockSpec(memory_space=pltpu.SMEM)
    vmem = pl.BlockSpec(memory_space=pltpu.VMEM)
    anywhere = pl.BlockSpec(memory_space=pl.ANY)

    def after(earlier, *values):
        earlier = list(earlier)
        return kernel_call(
            after_kernel,
            "after",
            [jax.ShapeDtypeStruct(value.shape, value.dtype) for value in values],
            [anywhere] * (len(earlier) + len(values)),
            [anywhere] * len(values),
            aliases={len(earlier) + number: number for number in range(len(values))},
        )(*earlier, *values)

    low, high = features[:split], features[split:]
    before_high = passed_along(high, "blk", 1)
    across_low = swapped(low, near)
    before_low = passed_along(low, "blk", 1)
    own_edges = kernel_call(
        pack_kernel,
        "pack_edges",
        jax.ShapeDtypeStruct((3 * turns * capacity // LANES + 8, LANES), jnp.int32),
        [smem, anywhere] + [vmem] * 3,
        vmem,
    )(edge_counts[0, 0], low, source_index[0, 0], target_index[0, 0], map_index[0, 0])
    edges = [own_edges] + [swapped(own_edges, bit) for bit in range(1, replicas)]
    *edges[1:], across_low, before_high, high = after([], *edges[1:], across_low, before_high, high)
    across_high = swapped(high, near)
    far_low = passed_along(across_low, "blk", 1)
    far_high = swapped(before_high, near)
    part = replicas * capacity // LANES
    list_rows = (part, 2 * part, 2 * part, part)
    listed = kernel_call(
        functools.partial(pick_kernel, (source_bits, node_bits, node_bits, capacity), near),
        "pick_edges",
        [jax.ShapeDtypeStruct((rows, LANES), jnp.int32) for rows in list_rows]
        + [jax.ShapeDtypeStruct((rows + 8, LANES), jnp.int32) for rows in list_rows],
        [vmem] * replicas,
        [vmem] * 8,
        scratch=[pltpu.VMEM((6 * part, LANES), jnp.int32)],
        vmem=4 * MIB,
    )(*edges)
    table_shapes = [(stalk * stalk, 2 * maps), (width, width), (width, width)]
    bank_parts, spread_high, spread_low = kernel_call(
        tables_kernel,
        "tables",
        [jax.ShapeDtypeStruct(shape, jnp.bfloat16) for shape in table_shapes],
        [vmem] * 2,
        [vmem] * 3,
        vmem=4 * MIB,
    )(restriction.reshape(maps, stalk * stalk).T, mixing)

    sizes = (stalk, channels, maps, source_bits, node_bits, nodes)
    total_shape = jax.ShapeDtypeStruct((nodes, width), jnp.float32)

    def staged(number, stage, pieces, operands):
        rows = sum(piece.shape[0] for piece in pieces)
        operands = [listed[number], listed[number + 4], bank_parts] + pieces + operands
        aliases = {}
        out_shape = total_shape
        if stage != "first":
            aliases = {3 + len(pieces): 1 if stage == "last" else 0}
        if stage == "last":
            out_shape = [jax.ShapeDtypeStruct((nodes, width), features.dtype), total_shape]
        return kernel_call(
            functools.partial(stage_kernel, sizes, len(pieces), stage),
            stage + "_edges",
            out_shape,
            [vmem] * len(operands),
            [vmem] * 2 if stage == "last" else vmem,
            scratch=[
                pltpu.VMEM((2 * rows, LANES), jnp.float32),
                pltpu.SMEM((list_rows[number] + 8, LANES), jnp.int32),
                pltpu.SemaphoreType.DMA,
                pltpu.VMEM((2 * EDGES, LANES), jnp.float32),
                pltpu.VMEM((width, EDGES), jnp.float32),
                pltpu.VMEM((stalk * stalk, EDGES), jnp.float32),
                pltpu.VMEM((width, EDGES), jnp.float32),
                pltpu.VMEM((EDGES, width), jnp.bfloat16),
            ],
            vmem=rows * width * 4 + 6 * MIB,
            aliases=aliases,
        )(*operands)

    def near_halves(low, high):
        return [list(pair) for pair in zip(spread_near(low, near), spread_near(high, near))]

    total = staged(0, "first", spread_near(features, near), [])
    across_high, before_low = after([total], across_high, before_low)
    across = near_halves(across_low, across_high)
    before = near_halves(before_low, before_high)
    total = staged(1, "second", across[0] + before[0], [total])
    far_low, far_high = after([total], far_low, far_high)
    turned = [piece for pair in across[1:] + before[1:] for piece in pair]
    total = staged(2, "third", turned, [total])
    far = [piece for pair in near_halves(far_low, far_high) for piece in pair]
    updated, _ = staged(3, "last", far, [total, spread_high, spread_low, features])
    return updated


def solution(mesh):
    in_specs = (
        P(("blk", "rep"), None),
        P(),
        P(),
        P("blk", "rep", None, None),
        P("blk", "rep", None, None),
        P("blk", "rep", None, None),
        P("blk", "rep", None),
    )
    out_specs = P(("blk", "rep"), None)
    return jax.shard_map(body, mesh=mesh, in_specs=in_specs, out_specs=out_specs, check_vma=False)
```

```python
import functools

import jax
import jax.numpy as jnp
from jax import lax
from jax.experimental import pallas as pl
from jax.experimental.pallas import tpu as pltpu
from jax.sharding import PartitionSpec as P

EDGES = 256
LANES = 128
MIB = 1024 * 1024
COUNT_ROWS = 8
EARLY_ROWS = 24


def bits_for(count):
    return max(1, (count - 1).bit_length())


def passed_along(block, axis, distance):
    devices = range(lax.axis_size(axis))
    route = [((i - distance) % len(devices), i) for i in devices]
    return lax.ppermute(block, axis, route)


def swapped(block, bit):
    route = [(i, i ^ bit) for i in range(lax.axis_size("rep"))]
    return lax.ppermute(block, "rep", route)


def spread_near(piece, near):
    pieces = [piece]
    bit = 1
    while bit < near:
        pieces = pieces + [swapped(p, bit) for p in pieces]
        bit *= 2
    return pieces


def pack_kernel(counts_ref, _, *refs):
    index_refs, out_ref = refs[:-1], refs[-1]
    turns, capacity = index_refs[0].shape
    rows = capacity // LANES
    for turn in range(turns):
        for number, ref in enumerate(index_refs):
            start = (turn * len(index_refs) + number) * rows
            for row in range(rows):
                out_ref[start + row : start + row + 1, :] = ref[turn : turn + 1, row * LANES : (row + 1) * LANES]
    start = turns * len(index_refs) * rows
    out_ref[start:, :] = jnp.zeros((out_ref.shape[0] - start, LANES), jnp.int32)
    for turn in range(turns):
        out_ref[start + turn : start + turn + 1, :] = jnp.full((1, LANES), counts_ref[turn], jnp.int32)


def shifted_left(value, distance):
    rows = value.shape[0]
    if distance >= LANES:
        return pltpu.roll(value, rows - distance // LANES, 0)
    turned = pltpu.roll(value, LANES - distance, 1)
    lane = lax.broadcasted_iota(jnp.int32, value.shape, 1)
    return jnp.where(lane >= LANES - distance, pltpu.roll(turned, rows - 1, 0), turned)


def ones_where(condition):
    return jnp.where(condition, 1.0, 0.0).astype(jnp.bfloat16)


def closed_up(words):
    rows = words.shape[0]
    row = lax.broadcasted_iota(jnp.int32, (rows, LANES), 0)
    lane = lax.broadcasted_iota(jnp.int32, (rows, LANES), 1)
    used = ones_where(words != 0)
    upto = ones_where(lax.broadcasted_iota(jnp.int32, (LANES, LANES), 0) <= lax.broadcasted_iota(jnp.int32, (LANES, LANES), 1))
    above = ones_where(lax.broadcasted_iota(jnp.int32, (rows, rows), 1) < lax.broadcasted_iota(jnp.int32, (rows, rows), 0))
    every = jnp.ones((LANES, LANES), jnp.bfloat16)
    dot = functools.partial(jnp.dot, preferred_element_type=jnp.float32)
    earlier = dot(dot(above, used).astype(jnp.bfloat16), every)
    number = (earlier + dot(used, upto)).astype(jnp.int32)
    total = dot(dot(jnp.ones((8, rows), jnp.bfloat16), used).astype(jnp.bfloat16), every).astype(jnp.int32)
    way = jnp.where(words != 0, row * LANES + lane + 1 - number, 0)
    for bit in range(bits_for(rows * LANES)):
        moves = ((way >> bit) & 1) == 1
        moved_words = shifted_left(jnp.where(moves, words, 0), 1 << bit)
        moved_way = shifted_left(jnp.where(moves, way, 0), 1 << bit)
        words = jnp.where(moves, 0, words) | moved_words
        way = jnp.where(moves, 0, way) | moved_way
    return words, total


def pick_kernel(sizes, near, *refs):
    source_bits, target_bits, node_bits, capacity = sizes
    replicas = 2 * near
    edge_refs, refs = refs[:replicas], refs[replicas:]
    word_refs, place_refs, candidates_ref = refs[:4], refs[4:8], refs[8]
    rows = capacity // LANES
    node_mask = (1 << node_bits) - 1
    me = lax.axis_index("rep")
    positions = lax.broadcasted_iota(jnp.int32, (rows, LANES), 0) * LANES + lax.broadcasted_iota(
        jnp.int32, (rows, LANES), 1
    )
    part = replicas * rows
    for turn in range(2):
        for k, edge_ref in enumerate(edge_refs):
            start = turn * 3 * rows
            source = edge_ref[start : start + rows, :]
            target = edge_ref[start + rows : start + 2 * rows, :]
            map_id = edge_ref[start + 2 * rows : start + 3 * rows, :]
            live = positions < edge_ref[6 * rows + turn : 6 * rows + turn + 1, :]
            mine = live & ((target >> node_bits) == me)
            slot = (source >> node_bits) ^ me
            far = slot >= near
            slot = slot & (near - 1)
            straight = slot == 0
            rest = (source & node_mask) | ((target & node_mask) << source_bits)
            rest |= (map_id << (source_bits + target_bits)) | (1 << 30)
            in_own = rest | (slot << node_bits)
            in_straight = rest | (turn << node_bits)
            in_turned = rest | ((turn * (near - 1) + slot - 1) << node_bits)
            ends = mine & ~far if turn == 0 else mine & far
            others = mine & far if turn == 0 else mine & ~far
            at = k * rows
            choices = (
                (0 if turn == 0 else 5 * part, ends, in_own),
                (part + turn * part, others & straight, in_straight),
                (3 * part + turn * part, others & ~straight, in_turned),
            )
            for first, chosen, word in choices:
                candidates_ref[first + at : first + at + rows, :] = jnp.where(chosen, word, 0)
    for number, (start, stop) in enumerate(((0, part), (part, 3 * part), (3 * part, 5 * part), (5 * part, 6 * part))):
        words, total = closed_up(candidates_ref[start:stop, :])
        word_refs[number][...] = words
        place_refs[number][:COUNT_ROWS, :] = total
        place_refs[number][COUNT_ROWS:, :] = (words & ((1 << source_bits) - 1)) * 2


def tables_kernel(bank_ref, mixing_ref, bank_parts_ref, spread_high_ref, spread_low_ref):
    maps = bank_ref.shape[1]
    channels = mixing_ref.shape[0]
    width = spread_high_ref.shape[0]
    high, low = two_parts(bank_ref[...])
    bank_parts_ref[:, :maps] = high
    bank_parts_ref[:, maps:] = low
    dot = functools.partial(jnp.dot, preferred_element_type=jnp.float32)
    down = ones_where(
        lax.broadcasted_iota(jnp.int32, (width, channels), 0) % channels
        == lax.broadcasted_iota(jnp.int32, (width, channels), 1)
    )
    across = ones_where(
        lax.broadcasted_iota(jnp.int32, (channels, width), 1) % channels
        == lax.broadcasted_iota(jnp.int32, (channels, width), 0)
    )
    same = lax.broadcasted_iota(jnp.int32, (width, width), 0) // channels == (
        lax.broadcasted_iota(jnp.int32, (width, width), 1) // channels
    )
    for part, ref in zip(two_parts(mixing_ref[...]), (spread_high_ref, spread_low_ref)):
        tiled = dot(dot(down, part).astype(jnp.bfloat16), across)
        ref[...] = jnp.where(same, tiled, 0.0).astype(jnp.bfloat16)


def after_kernel(*refs):
    pass


def two_parts(value):
    high = value.astype(jnp.bfloat16)
    return high, (value - high.astype(jnp.float32)).astype(jnp.bfloat16)


def load_rows(piece_refs, rows_ref):
    start = 0
    for ref in piece_refs:
        rows = ref.shape[0]

        def widen(i, _, ref=ref, start=start):
            at = pl.multiple_of(i * LANES, LANES)
            value = ref[pl.ds(at, LANES), :].astype(jnp.float32)
            for half in range(2):
                rows_ref[pl.ds(2 * (start + at) + half, LANES, stride=2), :] = value[:, half * LANES : (half + 1) * LANES]
            return 0

        lax.fori_loop(0, rows // LANES, widen, 0, unroll=2)
        start += rows


def add_edges(sizes, words_ref, rows_ref, places_ref, total_ref, bank_parts_ref, gathered_ref, turned_ref, chosen_ref, message_ref, sent_ref):
    stalk, channels, maps, source_bits, target_bits, nodes = sizes
    target_mask = (1 << target_bits) - 1
    map_mask = (1 << bits_for(maps)) - 1
    lists = EDGES // LANES
    blocks = words_ref.shape[0] // lists
    count = places_ref[0, 0]

    def gather(block):
        for u in range(EDGES):
            place = pl.multiple_of(places_ref[COUNT_ROWS + block * lists + u // LANES, u % LANES], 2)
            gathered_ref[2 * u : 2 * u + 2, :] = rows_ref[pl.ds(place, 2), :]

    def words_of(block):
        return jnp.concatenate([words_ref[pl.ds(block * lists + part, 1), :] for part in range(lists)], axis=1)

    def turn_rows():
        for part in range(lists):
            lanes = slice(part * LANES, (part + 1) * LANES)
            for half in range(2):
                values = gathered_ref[pl.ds(2 * part * LANES + half, LANES, stride=2), :]
                turned_ref[half * LANES : (half + 1) * LANES, lanes] = values.T

    def choose(block):
        map_ids = (words_of(block) >> (source_bits + target_bits)) & map_mask
        wanted = ones_where(lax.broadcasted_iota(jnp.int32, (maps, EDGES), 0) == map_ids)
        wanted = jnp.concatenate([wanted, wanted], axis=0)
        chosen_ref[...] = jnp.dot(bank_parts_ref[...], wanted, preferred_element_type=jnp.float32)

    def make_messages():
        for part in range(lists):
            lanes = slice(part * LANES, (part + 1) * LANES)
            features = turned_ref[:, lanes]
            for i in range(stalk):
                message = None
                for j in range(stalk):
                    factor = chosen_ref[i * stalk + j : i * stalk + j + 1, lanes]
                    term = factor * features[j * channels : (j + 1) * channels, :]
                    message = term if message is None else message + term
                message_ref[i * channels : (i + 1) * channels, lanes] = message

    def turn_messages():
        for part in range(lists):
            lanes = slice(part * LANES, (part + 1) * LANES)
            sent_ref[lanes, :] = message_ref[:, lanes].T.astype(jnp.bfloat16)

    def scatter(block):
        words = words_of(block)
        targets = jnp.where(words != 0, (words >> source_bits) & target_mask, -1)
        ids = lax.broadcasted_iota(jnp.int32, (EDGES, EDGES), 0).astype(jnp.bfloat16)
        one, zero = jnp.bfloat16(1), jnp.bfloat16(0)
        for start in range(0, nodes, 2 * EDGES):
            selectors = []
            for base in (start, start + EDGES):
                wanted_ids = (targets - base).astype(jnp.float32).astype(jnp.bfloat16)
                selectors.append(jnp.where(ids == wanted_ids, one, zero))
            selector = jnp.concatenate(selectors, axis=0)
            total_ref[start : start + 2 * EDGES, :] += jnp.dot(
                selector, sent_ref[...], preferred_element_type=jnp.float32
            )

    def step(block, _):
        turn_rows()
        choose(block)
        gather(jnp.minimum(block + 1, blocks - 1))
        scatter(block - 1)
        make_messages()
        turn_messages()
        return 0

    last = jnp.maximum(pl.cdiv(count, EDGES), 1) - 1
    gather(0)
    turn_rows()
    choose(0)
    gather(jnp.minimum(1, blocks - 1))
    make_messages()
    turn_messages()
    lax.fori_loop(1, last + 1, step, 0)
    scatter(last)


def stage_kernel(sizes, piece_count, stage, words_ref, listed_ref, bank_parts_ref, *refs):
    pieces, refs = refs[:piece_count], refs[piece_count:]
    if stage == "first":
        total_ref, *scratch = refs
    elif stage != "last":
        _, total_ref, *scratch = refs
    else:
        _, spread_high_ref, spread_low_ref, own_ref, out_ref, total_ref, *scratch, made_ref, out_sems = refs
    rows_ref, places_ref, sem, *scratch = scratch
    early = pl.ds(0, EARLY_ROWS)
    copy = pltpu.make_async_copy(listed_ref.at[early], places_ref.at[early], sem)
    copy.start()
    if stage == "first":
        total_ref[...] = jnp.zeros_like(total_ref)
    load_rows(pieces, rows_ref)
    copy.wait()

    @pl.when(places_ref[0, 0] > (EARLY_ROWS - COUNT_ROWS) * LANES)
    def _():
        rest = pl.ds(EARLY_ROWS, listed_ref.shape[0] - EARLY_ROWS)
        rest_copy = pltpu.make_async_copy(listed_ref.at[rest], places_ref.at[rest], sem)
        rest_copy.start()
        rest_copy.wait()

    add_edges(sizes, words_ref, rows_ref, places_ref, total_ref, bank_parts_ref, *scratch)
    if stage == "last":
        spread_high, spread_low = spread_high_ref[...], spread_low_ref[...]
        copies = []
        for number, start in enumerate(range(0, own_ref.shape[0], 2 * EDGES)):
            here = pl.ds(start, 2 * EDGES)
            high, low = two_parts(total_ref[here, :])
            mixed = jnp.dot(high, spread_high, preferred_element_type=jnp.float32)
            mixed += jnp.dot(high, spread_low, preferred_element_type=jnp.float32)
            mixed += jnp.dot(low, spread_high, preferred_element_type=jnp.float32)
            made_ref[here, :] = (own_ref[here, :].astype(jnp.float32) + mixed).astype(jnp.bfloat16)
            copies.append(pltpu.make_async_copy(made_ref.at[here], out_ref.at[here], out_sems.at[number]))
            copies[-1].start()
        for copy in copies:
            copy.wait()


def kernel_call(kernel, name, out_shape, in_specs, out_specs, scratch=(), vmem=MIB, aliases=None, cost=1_000):
    return pl.pallas_call(
        kernel,
        out_shape=out_shape,
        in_specs=in_specs,
        out_specs=out_specs,
        scratch_shapes=list(scratch),
        input_output_aliases=aliases or {},
        compiler_params=pltpu.CompilerParams(vmem_limit_bytes=vmem),
        cost_estimate=pl.CostEstimate(flops=0, bytes_accessed=cost, transcendentals=0),
        name=name,
    )


def body(features, restriction, mixing, source_index, target_index, map_index, edge_counts):
    nodes, width = features.shape
    replicas = lax.axis_size("rep")
    near = replicas // 2
    split = nodes * 9 // 16 // LANES * LANES
    maps, stalk, _ = restriction.shape
    channels = mixing.shape[0]
    capacity = source_index.shape[3]
    turns = source_index.shape[2]
    node_bits = bits_for(nodes)
    source_bits = bits_for(2 * near * nodes)
    assert replicas == 2 * near and near > 1 and near & (near - 1) == 0 and turns == 2
    assert nodes == 1 << node_bits and nodes % (2 * EDGES) == 0 and capacity % LANES == 0
    assert source_bits + node_bits + bits_for(maps) <= 30

    smem = pl.BlockSpec(memory_space=pltpu.SMEM)
    vmem = pl.BlockSpec(memory_space=pltpu.VMEM)
    anywhere = pl.BlockSpec(memory_space=pl.ANY)

    def after(earlier, *values):
        earlier = list(earlier)
        return kernel_call(
            after_kernel,
            "after",
            [jax.ShapeDtypeStruct(value.shape, value.dtype) for value in values],
            [anywhere] * (len(earlier) + len(values)),
            [anywhere] * len(values),
            aliases={len(earlier) + number: number for number in range(len(values))},
        )(*earlier, *values)

    low, high = features[:split], features[split:]
    before_high = passed_along(high, "blk", 1)
    across_low = swapped(low, near)
    before_low = passed_along(low, "blk", 1)
    own_edges = kernel_call(
        pack_kernel,
        "pack_edges",
        jax.ShapeDtypeStruct((3 * turns * capacity // LANES + 8, LANES), jnp.int32),
        [smem, anywhere] + [vmem] * 3,
        vmem,
    )(edge_counts[0, 0], low, source_index[0, 0], target_index[0, 0], map_index[0, 0])
    far_edges = swapped(own_edges, near)
    near_edges = spread_near(own_edges, near)
    near_pieces = spread_near(features, near)
    *meeting, far_edges, across_low, before_high, high = after(
        [], *near_edges[1:], *near_pieces[1:], far_edges, across_low, before_high, high
    )
    near_edges[1:], near_pieces[1:] = meeting[: near - 1], meeting[near - 1 :]
    across_high = swapped(high, near)
    far_low = passed_along(across_low, "blk", 1)
    far_high = swapped(before_high, near)
    part = replicas * capacity // LANES
    list_rows = (part, 2 * part, 2 * part, part)
    listed = kernel_call(
        functools.partial(pick_kernel, (source_bits, node_bits, node_bits, capacity), near),
        "pick_edges",
        [jax.ShapeDtypeStruct((rows, LANES), jnp.int32) for rows in list_rows]
        + [jax.ShapeDtypeStruct((rows + COUNT_ROWS, LANES), jnp.int32) for rows in list_rows],
        [vmem] * replicas,
        [vmem] * 8,
        scratch=[pltpu.VMEM((6 * part, LANES), jnp.int32)],
        vmem=4 * MIB,
    )(*near_edges, *spread_near(far_edges, near))
    table_shapes = [(stalk * stalk, 2 * maps), (width, width), (width, width)]
    bank_parts, spread_high, spread_low = kernel_call(
        tables_kernel,
        "tables",
        [jax.ShapeDtypeStruct(shape, jnp.bfloat16) for shape in table_shapes],
        [vmem] * 2,
        [vmem] * 3,
        vmem=4 * MIB,
    )(restriction.reshape(maps, stalk * stalk).T, mixing)

    sizes = (stalk, channels, maps, source_bits, node_bits, nodes)
    total_shape = jax.ShapeDtypeStruct((nodes, width), jnp.float32)

    def staged(number, stage, pieces, operands):
        rows = sum(piece.shape[0] for piece in pieces)
        operands = [listed[number], listed[number + 4], bank_parts] + pieces + operands
        aliases = {}
        out_shape = total_shape
        if stage != "first":
            aliases = {3 + len(pieces): 1 if stage == "last" else 0}
        if stage == "last":
            out_shape = [jax.ShapeDtypeStruct((nodes, width), features.dtype), total_shape]
        return kernel_call(
            functools.partial(stage_kernel, sizes, len(pieces), stage),
            stage + "_edges",
            out_shape,
            [vmem] * len(operands),
            [anywhere, vmem] if stage == "last" else vmem,
            scratch=[
                pltpu.VMEM((2 * rows, LANES), jnp.float32),
                pltpu.SMEM((list_rows[number] + COUNT_ROWS, LANES), jnp.int32),
                pltpu.SemaphoreType.DMA,
                pltpu.VMEM((2 * EDGES, LANES), jnp.float32),
                pltpu.VMEM((width, EDGES), jnp.float32),
                pltpu.VMEM((stalk * stalk, EDGES), jnp.float32),
                pltpu.VMEM((width, EDGES), jnp.float32),
                pltpu.VMEM((EDGES, width), jnp.bfloat16),
            ]
            + (
                [pltpu.VMEM((nodes, width), jnp.bfloat16), pltpu.SemaphoreType.DMA((nodes // (2 * EDGES),))]
                if stage == "last"
                else []
            ),
            vmem=rows * width * 4 + 6 * MIB,
            cost=2_000_000 if stage == "third" else 1_000,
            aliases=aliases,
        )(*operands)

    def near_halves(low, high):
        return [list(pair) for pair in zip(spread_near(low, near), spread_near(high, near))]

    total = staged(0, "first", near_pieces, [])
    across_high, before_low = after([total], across_high, before_low)
    across = near_halves(across_low, across_high)
    before = near_halves(before_low, before_high)
    total = staged(1, "second", across[0] + before[0], [total])
    far_low, far_high = after([total], far_low, far_high)
    turned = [piece for pair in across[1:] + before[1:] for piece in pair]
    total = staged(2, "third", turned, [total])
    far = [piece for pair in near_halves(far_low, far_high) for piece in pair]
    updated, _ = staged(3, "last", far, [total, spread_high, spread_low, features])
    return updated


def solution(mesh):
    in_specs = (
        P(("blk", "rep"), None),
        P(),
        P(),
        P("blk", "rep", None, None),
        P("blk", "rep", None, None),
        P("blk", "rep", None, None),
        P("blk", "rep", None),
    )
    out_specs = P(("blk", "rep"), None)
    return jax.shard_map(body, mesh=mesh, in_specs=in_specs, out_specs=out_specs, check_vma=False)
```

```python
import functools

import jax
import jax.numpy as jnp
from jax import lax
from jax.experimental import pallas as pl
from jax.experimental.pallas import tpu as pltpu
from jax.sharding import PartitionSpec as P

EDGES = 256
LANES = 128
MIB = 1024 * 1024
COUNT_ROWS = 8
EARLY_ROWS = 24


def bits_for(count):
    return max(1, (count - 1).bit_length())


def passed_along(block, axis, distance):
    devices = range(lax.axis_size(axis))
    route = [((i - distance) % len(devices), i) for i in devices]
    return lax.ppermute(block, axis, route)


def swapped(block, bit):
    route = [(i, i ^ bit) for i in range(lax.axis_size("rep"))]
    return lax.ppermute(block, "rep", route)


def spread_near(piece, near):
    pieces = [piece]
    bit = 1
    while bit < near:
        pieces = pieces + [swapped(p, bit) for p in pieces]
        bit *= 2
    return pieces


def pack_kernel(counts_ref, *refs):
    index_refs, out_ref = refs[:-1], refs[-1]
    turns, capacity = index_refs[0].shape
    rows = capacity // LANES
    for turn in range(turns):
        for number, ref in enumerate(index_refs):
            start = (turn * len(index_refs) + number) * rows
            for row in range(rows):
                out_ref[start + row : start + row + 1, :] = ref[turn : turn + 1, row * LANES : (row + 1) * LANES]
    start = turns * len(index_refs) * rows
    out_ref[start:, :] = jnp.zeros((out_ref.shape[0] - start, LANES), jnp.int32)
    for turn in range(turns):
        out_ref[start + turn : start + turn + 1, :] = jnp.full((1, LANES), counts_ref[turn], jnp.int32)


def shifted_left(value, distance):
    rows = value.shape[0]
    if distance >= LANES:
        return pltpu.roll(value, rows - distance // LANES, 0)
    turned = pltpu.roll(value, LANES - distance, 1)
    lane = lax.broadcasted_iota(jnp.int32, value.shape, 1)
    return jnp.where(lane >= LANES - distance, pltpu.roll(turned, rows - 1, 0), turned)


def ones_where(condition):
    return jnp.where(condition, 1.0, 0.0).astype(jnp.bfloat16)


def closed_up(words):
    rows = words.shape[0]
    row = lax.broadcasted_iota(jnp.int32, (rows, LANES), 0)
    lane = lax.broadcasted_iota(jnp.int32, (rows, LANES), 1)
    used = ones_where(words != 0)
    upto = ones_where(lax.broadcasted_iota(jnp.int32, (LANES, LANES), 0) <= lax.broadcasted_iota(jnp.int32, (LANES, LANES), 1))
    above = ones_where(lax.broadcasted_iota(jnp.int32, (rows, rows), 1) < lax.broadcasted_iota(jnp.int32, (rows, rows), 0))
    every = jnp.ones((LANES, LANES), jnp.bfloat16)
    dot = functools.partial(jnp.dot, preferred_element_type=jnp.float32)
    earlier = dot(dot(above, used).astype(jnp.bfloat16), every)
    number = (earlier + dot(used, upto)).astype(jnp.int32)
    total = dot(dot(jnp.ones((8, rows), jnp.bfloat16), used).astype(jnp.bfloat16), every).astype(jnp.int32)
    way = jnp.where(words != 0, row * LANES + lane + 1 - number, 0)
    for bit in range(bits_for(rows * LANES)):
        moves = ((way >> bit) & 1) == 1
        moved_words = shifted_left(jnp.where(moves, words, 0), 1 << bit)
        moved_way = shifted_left(jnp.where(moves, way, 0), 1 << bit)
        words = jnp.where(moves, 0, words) | moved_words
        way = jnp.where(moves, 0, way) | moved_way
    return words, total


def pick_kernel(sizes, near, *refs):
    source_bits, target_bits, node_bits, capacity = sizes
    replicas = 2 * near
    edge_refs, refs = refs[:replicas], refs[replicas:]
    word_refs, place_refs, candidates_ref = refs[:4], refs[4:8], refs[8]
    rows = capacity // LANES
    node_mask = (1 << node_bits) - 1
    me = lax.axis_index("rep")
    positions = lax.broadcasted_iota(jnp.int32, (rows, LANES), 0) * LANES + lax.broadcasted_iota(
        jnp.int32, (rows, LANES), 1
    )
    part = replicas * rows
    for turn in range(2):
        for k, edge_ref in enumerate(edge_refs):
            start = turn * 3 * rows
            source = edge_ref[start : start + rows, :]
            target = edge_ref[start + rows : start + 2 * rows, :]
            map_id = edge_ref[start + 2 * rows : start + 3 * rows, :]
            live = positions < edge_ref[6 * rows + turn : 6 * rows + turn + 1, :]
            mine = live & ((target >> node_bits) == me)
            slot = (source >> node_bits) ^ me
            far = slot >= near
            slot = slot & (near - 1)
            straight = slot == 0
            rest = (source & node_mask) | ((target & node_mask) << source_bits)
            rest |= (map_id << (source_bits + target_bits)) | (1 << 30)
            in_own = rest | (slot << node_bits)
            in_straight = rest | (turn << node_bits)
            in_turned = rest | ((turn * (near - 1) + slot - 1) << node_bits)
            ends = mine & ~far if turn == 0 else mine & far
            others = mine & far if turn == 0 else mine & ~far
            at = k * rows
            choices = (
                (0 if turn == 0 else 5 * part, ends, in_own),
                (part + turn * part, others & straight, in_straight),
                (3 * part + turn * part, others & ~straight, in_turned),
            )
            for first, chosen, word in choices:
                candidates_ref[first + at : first + at + rows, :] = jnp.where(chosen, word, 0)
    for number, (start, stop) in enumerate(((0, part), (part, 3 * part), (3 * part, 5 * part), (5 * part, 6 * part))):
        words, total = closed_up(candidates_ref[start:stop, :])
        word_refs[number][...] = words
        place_refs[number][:COUNT_ROWS, :] = total
        place_refs[number][COUNT_ROWS:, :] = (words & ((1 << source_bits) - 1)) * 2


def tables_kernel(bank_ref, mixing_ref, bank_parts_ref, spread_high_ref, spread_low_ref):
    maps = bank_ref.shape[1]
    channels = mixing_ref.shape[0]
    width = spread_high_ref.shape[0]
    high, low = two_parts(bank_ref[...])
    bank_parts_ref[:, :maps] = high
    bank_parts_ref[:, maps:] = low
    dot = functools.partial(jnp.dot, preferred_element_type=jnp.float32)
    down = ones_where(
        lax.broadcasted_iota(jnp.int32, (width, channels), 0) % channels
        == lax.broadcasted_iota(jnp.int32, (width, channels), 1)
    )
    across = ones_where(
        lax.broadcasted_iota(jnp.int32, (channels, width), 1) % channels
        == lax.broadcasted_iota(jnp.int32, (channels, width), 0)
    )
    same = lax.broadcasted_iota(jnp.int32, (width, width), 0) // channels == (
        lax.broadcasted_iota(jnp.int32, (width, width), 1) // channels
    )
    for part, ref in zip(two_parts(mixing_ref[...]), (spread_high_ref, spread_low_ref)):
        tiled = dot(dot(down, part).astype(jnp.bfloat16), across)
        ref[...] = jnp.where(same, tiled, 0.0).astype(jnp.bfloat16)


def after_kernel(*refs):
    pass


def two_parts(value):
    high = value.astype(jnp.bfloat16)
    return high, (value - high.astype(jnp.float32)).astype(jnp.bfloat16)


def load_rows(piece_refs, rows_ref):
    start = 0
    for ref in piece_refs:
        rows = ref.shape[0]

        def widen(i, _, ref=ref, start=start):
            at = pl.multiple_of(i * LANES, LANES)
            value = ref[pl.ds(at, LANES), :].astype(jnp.float32)
            for half in range(2):
                rows_ref[pl.ds(2 * (start + at) + half, LANES, stride=2), :] = value[:, half * LANES : (half + 1) * LANES]
            return 0

        lax.fori_loop(0, rows // LANES, widen, 0, unroll=2)
        start += rows


def add_edges(sizes, words_ref, rows_ref, places_ref, total_ref, bank_parts_ref, gathered_ref, turned_ref, chosen_ref, message_ref, sent_ref):
    stalk, channels, maps, source_bits, target_bits, nodes = sizes
    target_mask = (1 << target_bits) - 1
    map_mask = (1 << bits_for(maps)) - 1
    lists = EDGES // LANES
    blocks = words_ref.shape[0] // lists
    count = places_ref[0, 0]

    def gather(block):
        for u in range(EDGES):
            place = pl.multiple_of(places_ref[COUNT_ROWS + block * lists + u // LANES, u % LANES], 2)
            gathered_ref[2 * u : 2 * u + 2, :] = rows_ref[pl.ds(place, 2), :]

    def words_of(block):
        return jnp.concatenate([words_ref[pl.ds(block * lists + part, 1), :] for part in range(lists)], axis=1)

    def turn_rows():
        for part in range(lists):
            lanes = slice(part * LANES, (part + 1) * LANES)
            for half in range(2):
                values = gathered_ref[pl.ds(2 * part * LANES + half, LANES, stride=2), :]
                turned_ref[half * LANES : (half + 1) * LANES, lanes] = values.T

    def choose(block):
        map_ids = (words_of(block) >> (source_bits + target_bits)) & map_mask
        wanted = ones_where(lax.broadcasted_iota(jnp.int32, (maps, EDGES), 0) == map_ids)
        wanted = jnp.concatenate([wanted, wanted], axis=0)
        chosen_ref[...] = jnp.dot(bank_parts_ref[...], wanted, preferred_element_type=jnp.float32)

    def make_messages():
        for part in range(lists):
            lanes = slice(part * LANES, (part + 1) * LANES)
            features = turned_ref[:, lanes]
            for i in range(stalk):
                message = None
                for j in range(stalk):
                    factor = chosen_ref[i * stalk + j : i * stalk + j + 1, lanes]
                    term = factor * features[j * channels : (j + 1) * channels, :]
                    message = term if message is None else message + term
                message_ref[i * channels : (i + 1) * channels, lanes] = message

    def turn_messages():
        for part in range(lists):
            lanes = slice(part * LANES, (part + 1) * LANES)
            sent_ref[lanes, :] = message_ref[:, lanes].T.astype(jnp.bfloat16)

    def scatter(block):
        words = words_of(block)
        targets = jnp.where(words != 0, (words >> source_bits) & target_mask, -1)
        ids = lax.broadcasted_iota(jnp.int32, (EDGES, EDGES), 0).astype(jnp.bfloat16)
        one, zero = jnp.bfloat16(1), jnp.bfloat16(0)
        for start in range(0, nodes, 2 * EDGES):
            selectors = []
            for base in (start, start + EDGES):
                wanted_ids = (targets - base).astype(jnp.float32).astype(jnp.bfloat16)
                selectors.append(jnp.where(ids == wanted_ids, one, zero))
            selector = jnp.concatenate(selectors, axis=0)
            total_ref[start : start + 2 * EDGES, :] += jnp.dot(
                selector, sent_ref[...], preferred_element_type=jnp.float32
            )

    def step(block, _):
        turn_rows()
        choose(block)
        gather(jnp.minimum(block + 1, blocks - 1))
        scatter(block - 1)
        make_messages()
        turn_messages()
        return 0

    last = jnp.maximum(pl.cdiv(count, EDGES), 1) - 1
    gather(0)
    turn_rows()
    choose(0)
    gather(jnp.minimum(1, blocks - 1))
    make_messages()
    turn_messages()
    lax.fori_loop(1, last + 1, step, 0)
    scatter(last)


def stage_kernel(sizes, piece_count, stage, words_ref, listed_ref, bank_parts_ref, *refs):
    pieces, refs = refs[:piece_count], refs[piece_count:]
    if stage == "first":
        total_ref, *scratch = refs
    elif stage != "last":
        _, total_ref, *scratch = refs
    else:
        _, spread_high_ref, spread_low_ref, own_ref, out_ref, total_ref, *scratch, made_ref, out_sems = refs
    rows_ref, places_ref, sem, *scratch = scratch
    early = pl.ds(0, EARLY_ROWS)
    copy = pltpu.make_async_copy(listed_ref.at[early], places_ref.at[early], sem)
    copy.start()
    if stage == "first":
        total_ref[...] = jnp.zeros_like(total_ref)
    load_rows(pieces, rows_ref)
    copy.wait()

    @pl.when(places_ref[0, 0] > (EARLY_ROWS - COUNT_ROWS) * LANES)
    def _():
        rest = pl.ds(EARLY_ROWS, listed_ref.shape[0] - EARLY_ROWS)
        rest_copy = pltpu.make_async_copy(listed_ref.at[rest], places_ref.at[rest], sem)
        rest_copy.start()
        rest_copy.wait()

    add_edges(sizes, words_ref, rows_ref, places_ref, total_ref, bank_parts_ref, *scratch)
    if stage == "last":
        spread_high, spread_low = spread_high_ref[...], spread_low_ref[...]
        copies = []
        for number, start in enumerate(range(0, own_ref.shape[0], 2 * EDGES)):
            here = pl.ds(start, 2 * EDGES)
            high, low = two_parts(total_ref[here, :])
            mixed = jnp.dot(high, spread_high, preferred_element_type=jnp.float32)
            mixed += jnp.dot(high, spread_low, preferred_element_type=jnp.float32)
            mixed += jnp.dot(low, spread_high, preferred_element_type=jnp.float32)
            made_ref[here, :] = (own_ref[here, :].astype(jnp.float32) + mixed).astype(jnp.bfloat16)
            copies.append(pltpu.make_async_copy(made_ref.at[here], out_ref.at[here], out_sems.at[number]))
            copies[-1].start()
        for copy in copies:
            copy.wait()


def kernel_call(kernel, name, out_shape, in_specs, out_specs, scratch=(), vmem=MIB, aliases=None):
    return pl.pallas_call(
        kernel,
        out_shape=out_shape,
        in_specs=in_specs,
        out_specs=out_specs,
        scratch_shapes=list(scratch),
        input_output_aliases=aliases or {},
        compiler_params=pltpu.CompilerParams(vmem_limit_bytes=vmem),
        cost_estimate=pl.CostEstimate(flops=0, bytes_accessed=1_000, transcendentals=0),
        name=name,
    )


def body(features, restriction, mixing, source_index, target_index, map_index, edge_counts):
    nodes, width = features.shape
    replicas = lax.axis_size("rep")
    near = replicas // 2
    split = nodes // 2
    maps, stalk, _ = restriction.shape
    channels = mixing.shape[0]
    capacity = source_index.shape[3]
    turns = source_index.shape[2]
    node_bits = bits_for(nodes)
    source_bits = bits_for(2 * near * nodes)
    assert replicas == 2 * near and near > 1 and near & (near - 1) == 0 and turns == 2
    assert nodes == 1 << node_bits and nodes % (2 * EDGES) == 0 and capacity % LANES == 0
    assert source_bits + node_bits + bits_for(maps) <= 30

    smem = pl.BlockSpec(memory_space=pltpu.SMEM)
    vmem = pl.BlockSpec(memory_space=pltpu.VMEM)
    anywhere = pl.BlockSpec(memory_space=pl.ANY)

    def after(earlier, *values):
        earlier = list(earlier)
        return kernel_call(
            after_kernel,
            "after",
            [jax.ShapeDtypeStruct(value.shape, value.dtype) for value in values],
            [anywhere] * (len(earlier) + len(values)),
            [anywhere] * len(values),
            aliases={len(earlier) + number: number for number in range(len(values))},
        )(*earlier, *values)

    before = passed_along(features, "blk", 1)
    across = swapped(features, near)
    own_edges = kernel_call(
        pack_kernel,
        "pack_edges",
        jax.ShapeDtypeStruct((3 * turns * capacity // LANES + 8, LANES), jnp.int32),
        [smem] + [vmem] * 3,
        vmem,
    )(edge_counts[0, 0], source_index[0, 0], target_index[0, 0], map_index[0, 0])
    edges = [own_edges] + [swapped(own_edges, bit) for bit in range(1, replicas)]
    across, before = after(edges[1:], across, before)
    far_low = passed_along(across[:split], "blk", 1)
    far_high = swapped(before[split:], near)
    part = replicas * capacity // LANES
    list_rows = (part, 2 * part, 2 * part, part)
    listed = kernel_call(
        functools.partial(pick_kernel, (source_bits, node_bits, node_bits, capacity), near),
        "pick_edges",
        [jax.ShapeDtypeStruct((rows, LANES), jnp.int32) for rows in list_rows]
        + [jax.ShapeDtypeStruct((rows + COUNT_ROWS, LANES), jnp.int32) for rows in list_rows],
        [vmem] * replicas,
        [vmem] * 8,
        scratch=[pltpu.VMEM((6 * part, LANES), jnp.int32)],
        vmem=4 * MIB,
    )(*edges)
    table_shapes = [(stalk * stalk, 2 * maps), (width, width), (width, width)]
    bank_parts, spread_high, spread_low = kernel_call(
        tables_kernel,
        "tables",
        [jax.ShapeDtypeStruct(shape, jnp.bfloat16) for shape in table_shapes],
        [vmem] * 2,
        [vmem] * 3,
        vmem=4 * MIB,
    )(restriction.reshape(maps, stalk * stalk).T, mixing)

    sizes = (stalk, channels, maps, source_bits, node_bits, nodes)
    total_shape = jax.ShapeDtypeStruct((nodes, width), jnp.float32)

    def staged(number, stage, pieces, operands):
        rows = sum(piece.shape[0] for piece in pieces)
        operands = [listed[number], listed[number + 4], bank_parts] + pieces + operands
        aliases = {}
        out_shape = total_shape
        if stage != "first":
            aliases = {3 + len(pieces): 1 if stage == "last" else 0}
        if stage == "last":
            out_shape = [jax.ShapeDtypeStruct((nodes, width), features.dtype), total_shape]
        return kernel_call(
            functools.partial(stage_kernel, sizes, len(pieces), stage),
            stage + "_edges",
            out_shape,
            [vmem] * len(operands),
            [anywhere, vmem] if stage == "last" else vmem,
            scratch=[
                pltpu.VMEM((2 * rows, LANES), jnp.float32),
                pltpu.SMEM((list_rows[number] + COUNT_ROWS, LANES), jnp.int32),
                pltpu.SemaphoreType.DMA,
                pltpu.VMEM((2 * EDGES, LANES), jnp.float32),
                pltpu.VMEM((width, EDGES), jnp.float32),
                pltpu.VMEM((stalk * stalk, EDGES), jnp.float32),
                pltpu.VMEM((width, EDGES), jnp.float32),
                pltpu.VMEM((EDGES, width), jnp.bfloat16),
            ]
            + (
                [pltpu.VMEM((nodes, width), jnp.bfloat16), pltpu.SemaphoreType.DMA((nodes // (2 * EDGES),))]
                if stage == "last"
                else []
            ),
            vmem=rows * width * 4 + 6 * MIB,
            aliases=aliases,
        )(*operands)

    total = staged(0, "first", spread_near(features, near), [])
    across, before = spread_near(across, near), spread_near(before, near)
    total = staged(1, "second", [across[0], before[0]], [total])
    total = staged(2, "third", across[1:] + before[1:], [total])
    far_low, far_high = after([total], far_low, far_high)
    far = [piece for pair in zip(spread_near(far_low, near), spread_near(far_high, near)) for piece in pair]
    updated, _ = staged(3, "last", far, [total, spread_high, spread_low, features])
    return updated


def solution(mesh):
    in_specs = (
        P(("blk", "rep"), None),
        P(),
        P(),
        P("blk", "rep", None, None),
        P("blk", "rep", None, None),
        P("blk", "rep", None, None),
        P("blk", "rep", None),
    )
    out_specs = P(("blk", "rep"), None)
    return jax.shard_map(body, mesh=mesh, in_specs=in_specs, out_specs=out_specs, check_vma=False)
```

```python
import functools

import jax
import jax.numpy as jnp
from jax import lax
from jax.experimental import pallas as pl
from jax.experimental.pallas import tpu as pltpu
from jax.sharding import PartitionSpec as P

EDGES = 256
LANES = 128
MIB = 1024 * 1024
COUNT_ROWS = 8
EARLY_ROWS = 24


def bits_for(count):
    return max(1, (count - 1).bit_length())


def passed_along(block, axis, distance):
    devices = range(lax.axis_size(axis))
    route = [((i - distance) % len(devices), i) for i in devices]
    return lax.ppermute(block, axis, route)


def swapped(block, bit):
    route = [(i, i ^ bit) for i in range(lax.axis_size("rep"))]
    return lax.ppermute(block, "rep", route)


def spread_near(piece, near):
    pieces = [piece]
    bit = 1
    while bit < near:
        pieces = pieces + [swapped(p, bit) for p in pieces]
        bit *= 2
    return pieces


def pack_kernel(counts_ref, *refs):
    index_refs, out_ref = refs[:-1], refs[-1]
    turns, capacity = index_refs[0].shape
    rows = capacity // LANES
    for turn in range(turns):
        for number, ref in enumerate(index_refs):
            start = (turn * len(index_refs) + number) * rows
            for row in range(rows):
                out_ref[start + row : start + row + 1, :] = ref[turn : turn + 1, row * LANES : (row + 1) * LANES]
    start = turns * len(index_refs) * rows
    out_ref[start:, :] = jnp.zeros((out_ref.shape[0] - start, LANES), jnp.int32)
    for turn in range(turns):
        out_ref[start + turn : start + turn + 1, :] = jnp.full((1, LANES), counts_ref[turn], jnp.int32)


def shifted_left(value, distance):
    rows = value.shape[0]
    if distance >= LANES:
        return pltpu.roll(value, rows - distance // LANES, 0)
    turned = pltpu.roll(value, LANES - distance, 1)
    lane = lax.broadcasted_iota(jnp.int32, value.shape, 1)
    return jnp.where(lane >= LANES - distance, pltpu.roll(turned, rows - 1, 0), turned)


def ones_where(condition):
    return jnp.where(condition, 1.0, 0.0).astype(jnp.bfloat16)


def closed_up(words):
    rows = words.shape[0]
    row = lax.broadcasted_iota(jnp.int32, (rows, LANES), 0)
    lane = lax.broadcasted_iota(jnp.int32, (rows, LANES), 1)
    used = ones_where(words != 0)
    upto = ones_where(lax.broadcasted_iota(jnp.int32, (LANES, LANES), 0) <= lax.broadcasted_iota(jnp.int32, (LANES, LANES), 1))
    above = ones_where(lax.broadcasted_iota(jnp.int32, (rows, rows), 1) < lax.broadcasted_iota(jnp.int32, (rows, rows), 0))
    every = jnp.ones((LANES, LANES), jnp.bfloat16)
    dot = functools.partial(jnp.dot, preferred_element_type=jnp.float32)
    earlier = dot(dot(above, used).astype(jnp.bfloat16), every)
    number = (earlier + dot(used, upto)).astype(jnp.int32)
    total = dot(dot(jnp.ones((8, rows), jnp.bfloat16), used).astype(jnp.bfloat16), every).astype(jnp.int32)
    way = jnp.where(words != 0, row * LANES + lane + 1 - number, 0)
    for bit in range(bits_for(rows * LANES)):
        moves = ((way >> bit) & 1) == 1
        moved_words = shifted_left(jnp.where(moves, words, 0), 1 << bit)
        moved_way = shifted_left(jnp.where(moves, way, 0), 1 << bit)
        words = jnp.where(moves, 0, words) | moved_words
        way = jnp.where(moves, 0, way) | moved_way
    return words, total


def pick_kernel(sizes, near, *refs):
    source_bits, target_bits, node_bits, capacity = sizes
    replicas = 2 * near
    edge_refs, refs = refs[:replicas], refs[replicas:]
    word_refs, place_refs, candidates_ref = refs[:3], refs[3:6], refs[6]
    rows = capacity // LANES
    node_mask = (1 << node_bits) - 1
    me = lax.axis_index("rep")
    positions = lax.broadcasted_iota(jnp.int32, (rows, LANES), 0) * LANES + lax.broadcasted_iota(
        jnp.int32, (rows, LANES), 1
    )
    part = replicas * rows
    for turn in range(2):
        for k, edge_ref in enumerate(edge_refs):
            start = turn * 3 * rows
            source = edge_ref[start : start + rows, :]
            target = edge_ref[start + rows : start + 2 * rows, :]
            map_id = edge_ref[start + 2 * rows : start + 3 * rows, :]
            live = positions < edge_ref[6 * rows + turn : 6 * rows + turn + 1, :]
            mine = live & ((target >> node_bits) == me)
            slot = (source >> node_bits) ^ me
            rest = (source & node_mask) | ((target & node_mask) << source_bits)
            rest |= (map_id << (source_bits + target_bits)) | jnp.int32(-(1 << 31))
            at = k * rows
            if turn == 0:
                candidates_ref[at : at + rows, :] = jnp.where(mine, rest | (slot << node_bits), 0)
                continue
            far = slot >= near
            column = slot & (near - 1)
            choices = (
                (part, ~far, rest | ((slot + replicas) << node_bits)),
                (2 * part, far & (column == 0), rest),
                (3 * part, far & (column != 0), rest | ((column - 1) << node_bits)),
            )
            for first, chosen, word in choices:
                candidates_ref[first + at : first + at + rows, :] = jnp.where(mine & chosen, word, 0)
    for number, (start, stop) in enumerate(((0, 2 * part), (2 * part, 3 * part), (3 * part, 4 * part))):
        words, total = closed_up(candidates_ref[start:stop, :])
        word_refs[number][...] = words
        place_refs[number][:COUNT_ROWS, :] = total
        place_refs[number][COUNT_ROWS:, :] = (words & ((1 << source_bits) - 1)) * 2


def tables_kernel(bank_ref, mixing_ref, bank_parts_ref, spread_high_ref, spread_low_ref):
    maps = bank_ref.shape[1]
    channels = mixing_ref.shape[0]
    width = spread_high_ref.shape[0]
    high, low = two_parts(bank_ref[...])
    bank_parts_ref[:, :maps] = high
    bank_parts_ref[:, maps:] = low
    dot = functools.partial(jnp.dot, preferred_element_type=jnp.float32)
    down = ones_where(
        lax.broadcasted_iota(jnp.int32, (width, channels), 0) % channels
        == lax.broadcasted_iota(jnp.int32, (width, channels), 1)
    )
    across = ones_where(
        lax.broadcasted_iota(jnp.int32, (channels, width), 1) % channels
        == lax.broadcasted_iota(jnp.int32, (channels, width), 0)
    )
    same = lax.broadcasted_iota(jnp.int32, (width, width), 0) // channels == (
        lax.broadcasted_iota(jnp.int32, (width, width), 1) // channels
    )
    for part, ref in zip(two_parts(mixing_ref[...]), (spread_high_ref, spread_low_ref)):
        tiled = dot(dot(down, part).astype(jnp.bfloat16), across)
        ref[...] = jnp.where(same, tiled, 0.0).astype(jnp.bfloat16)


def after_kernel(*refs):
    pass


def two_parts(value):
    high = value.astype(jnp.bfloat16)
    return high, (value - high.astype(jnp.float32)).astype(jnp.bfloat16)


def load_rows(piece_refs, rows_ref):
    start = 0
    for ref in piece_refs:
        rows = ref.shape[0]

        def widen(i, _, ref=ref, start=start):
            at = pl.multiple_of(i * LANES, LANES)
            value = ref[pl.ds(at, LANES), :].astype(jnp.float32)
            for half in range(2):
                rows_ref[pl.ds(2 * (start + at) + half, LANES, stride=2), :] = value[:, half * LANES : (half + 1) * LANES]
            return 0

        lax.fori_loop(0, rows // LANES, widen, 0, unroll=2)
        start += rows


def add_edges(sizes, words_ref, rows_ref, places_ref, total_ref, bank_parts_ref, gathered_ref, turned_ref, chosen_ref, message_ref, sent_ref, spread_refs=(), finish=None):
    stalk, channels, maps, source_bits, target_bits, nodes = sizes
    target_mask = (1 << target_bits) - 1
    map_mask = (1 << bits_for(maps)) - 1
    lists = EDGES // LANES
    blocks = words_ref.shape[0] // lists
    count = places_ref[0, 0]

    def gather(block):
        for u in range(EDGES):
            place = pl.multiple_of(places_ref[COUNT_ROWS + block * lists + u // LANES, u % LANES], 2)
            gathered_ref[2 * u : 2 * u + 2, :] = rows_ref[pl.ds(place, 2), :]

    def words_of(block):
        return jnp.concatenate([words_ref[pl.ds(block * lists + part, 1), :] for part in range(lists)], axis=1)

    def turn_rows():
        for part in range(lists):
            lanes = slice(part * LANES, (part + 1) * LANES)
            for half in range(2):
                values = gathered_ref[pl.ds(2 * part * LANES + half, LANES, stride=2), :]
                turned_ref[half * LANES : (half + 1) * LANES, lanes] = values.T

    def choose(block):
        map_ids = (words_of(block) >> (source_bits + target_bits)) & map_mask
        wanted = ones_where(lax.broadcasted_iota(jnp.int32, (maps, EDGES), 0) == map_ids)
        wanted = jnp.concatenate([wanted, wanted], axis=0)
        chosen_ref[...] = jnp.dot(bank_parts_ref[...], wanted, preferred_element_type=jnp.float32)

    def make_messages():
        for part in range(lists):
            lanes = slice(part * LANES, (part + 1) * LANES)
            features = turned_ref[:, lanes]
            for i in range(stalk):
                message = None
                for j in range(stalk):
                    factor = chosen_ref[i * stalk + j : i * stalk + j + 1, lanes]
                    term = factor * features[j * channels : (j + 1) * channels, :]
                    message = term if message is None else message + term
                message_ref[i * channels : (i + 1) * channels, lanes] = message

    def turn_messages():
        for part in range(lists):
            lanes = slice(part * LANES, (part + 1) * LANES)
            sent_ref[lanes, :] = message_ref[:, lanes].T.astype(jnp.bfloat16)
        if spread_refs:
            mixed = sum(jnp.dot(sent_ref[:EDGES, :], ref[...], preferred_element_type=jnp.float32) for ref in spread_refs)
            sent_ref[:EDGES, :], sent_ref[EDGES:, :] = two_parts(mixed)

    def scatter(block, finish=None):
        words = words_of(block)
        targets = jnp.where(words != 0, (words >> source_bits) & target_mask, -1)
        ids = lax.broadcasted_iota(jnp.int32, (EDGES, EDGES), 0).astype(jnp.bfloat16)
        one, zero = jnp.bfloat16(1), jnp.bfloat16(0)
        for start in range(0, nodes, 2 * EDGES):
            selectors = []
            for base in (start, start + EDGES):
                wanted_ids = (targets - base).astype(jnp.float32).astype(jnp.bfloat16)
                selectors.append(jnp.where(ids == wanted_ids, one, zero))
            selector = jnp.concatenate(selectors, axis=0)
            here = slice(start, start + 2 * EDGES)
            added = total_ref[here, :]
            for part in range(0, sent_ref.shape[0], EDGES):
                added += jnp.dot(selector, sent_ref[part : part + EDGES, :], preferred_element_type=jnp.float32)
            if finish is None:
                total_ref[here, :] = added
            else:
                finish(start, added)

    def step(block, _):
        turn_rows()
        choose(block)
        gather(jnp.minimum(block + 1, blocks - 1))
        scatter(block - 1)
        make_messages()
        turn_messages()
        return 0

    last = jnp.maximum(pl.cdiv(count, EDGES), 1) - 1
    gather(0)
    turn_rows()
    choose(0)
    gather(jnp.minimum(1, blocks - 1))
    make_messages()
    turn_messages()
    lax.fori_loop(1, last + 1, step, 0)
    scatter(last, finish)


def stage_kernel(sizes, piece_count, stage, words_ref, listed_ref, bank_parts_ref, *refs):
    pieces, refs = refs[:piece_count], refs[piece_count:]
    if stage == "soon":
        total_ref, *scratch = refs
    elif stage == "straight":
        _, spread_high_ref, spread_low_ref, own_ref, total_ref, *scratch = refs
    else:
        _, spread_high_ref, spread_low_ref, out_ref, total_ref, *scratch, made_ref, out_sems = refs
    rows_ref, places_ref, sem, *scratch = scratch
    early = pl.ds(0, EARLY_ROWS)
    copy = pltpu.make_async_copy(listed_ref.at[early], places_ref.at[early], sem)
    copy.start()
    if stage == "soon":
        total_ref[...] = jnp.zeros_like(total_ref)
    load_rows(pieces, rows_ref)
    copy.wait()

    @pl.when(places_ref[0, 0] > (EARLY_ROWS - COUNT_ROWS) * LANES)
    def _():
        rest = pl.ds(EARLY_ROWS, listed_ref.shape[0] - EARLY_ROWS)
        rest_copy = pltpu.make_async_copy(listed_ref.at[rest], places_ref.at[rest], sem)
        rest_copy.start()
        rest_copy.wait()

    add = functools.partial(add_edges, sizes, words_ref, rows_ref, places_ref, total_ref, bank_parts_ref, *scratch)
    if stage == "soon":
        add()
    elif stage == "straight":

        def mix(start, summed):
            here = pl.ds(start, 2 * EDGES)
            high, low = two_parts(summed)
            mixed = jnp.dot(high, spread_high_ref[...], preferred_element_type=jnp.float32)
            mixed += jnp.dot(high, spread_low_ref[...], preferred_element_type=jnp.float32)
            mixed += jnp.dot(low, spread_high_ref[...], preferred_element_type=jnp.float32)
            total_ref[here, :] = own_ref[here, :].astype(jnp.float32) + mixed

        add(finish=mix)
    else:
        copies = []

        def give(start, updated):
            here = pl.ds(start, 2 * EDGES)
            made_ref[here, :] = updated.astype(jnp.bfloat16)
            copies.append(pltpu.make_async_copy(made_ref.at[here], out_ref.at[here], out_sems.at[len(copies)]))
            copies[-1].start()

        add(spread_refs=(spread_high_ref, spread_low_ref), finish=give)
        for copy in copies:
            copy.wait()


def kernel_call(kernel, name, out_shape, in_specs, out_specs, scratch=(), vmem=MIB, aliases=None):
    return pl.pallas_call(
        kernel,
        out_shape=out_shape,
        in_specs=in_specs,
        out_specs=out_specs,
        scratch_shapes=list(scratch),
        input_output_aliases=aliases or {},
        compiler_params=pltpu.CompilerParams(vmem_limit_bytes=vmem),
        cost_estimate=pl.CostEstimate(flops=0, bytes_accessed=1_000, transcendentals=0),
        name=name,
    )


def body(features, restriction, mixing, source_index, target_index, map_index, edge_counts):
    nodes, width = features.shape
    replicas = lax.axis_size("rep")
    near = replicas // 2
    split = nodes // 2
    maps, stalk, _ = restriction.shape
    channels = mixing.shape[0]
    capacity = source_index.shape[3]
    turns = source_index.shape[2]
    node_bits = bits_for(nodes)
    source_bits = bits_for((replicas + near) * nodes)
    assert replicas == 2 * near and near > 1 and near & (near - 1) == 0 and turns == 2
    assert nodes == 1 << node_bits and nodes % (2 * EDGES) == 0 and capacity % LANES == 0
    assert source_bits + node_bits + bits_for(maps) <= 31

    smem = pl.BlockSpec(memory_space=pltpu.SMEM)
    vmem = pl.BlockSpec(memory_space=pltpu.VMEM)
    anywhere = pl.BlockSpec(memory_space=pl.ANY)

    def after(earlier, *values):
        earlier = list(earlier)
        return kernel_call(
            after_kernel,
            "after",
            [jax.ShapeDtypeStruct(value.shape, value.dtype) for value in values],
            [anywhere] * (len(earlier) + len(values)),
            [anywhere] * len(values),
            aliases={len(earlier) + number: number for number in range(len(values))},
        )(*earlier, *values)

    before = passed_along(features, "blk", 1)
    across = swapped(features, near)
    own_edges = kernel_call(
        pack_kernel,
        "pack_edges",
        jax.ShapeDtypeStruct((3 * turns * capacity // LANES + 8, LANES), jnp.int32),
        [smem] + [vmem] * 3,
        vmem,
    )(edge_counts[0, 0], source_index[0, 0], target_index[0, 0], map_index[0, 0])
    edges = [own_edges] + [swapped(own_edges, bit) for bit in range(1, replicas)]
    near_pieces = spread_near(features, near)
    across, before = after(edges[1:] + near_pieces[1:], across, before)
    far_low = passed_along(across[:split], "blk", 1)
    far_high = swapped(before[split:], near)
    part = replicas * capacity // LANES
    list_rows = (2 * part, part, part)
    listed = kernel_call(
        functools.partial(pick_kernel, (source_bits, node_bits, node_bits, capacity), near),
        "pick_edges",
        [jax.ShapeDtypeStruct((rows, LANES), jnp.int32) for rows in list_rows]
        + [jax.ShapeDtypeStruct((rows + COUNT_ROWS, LANES), jnp.int32) for rows in list_rows],
        [vmem] * replicas,
        [vmem] * 6,
        scratch=[pltpu.VMEM((4 * part, LANES), jnp.int32)],
        vmem=4 * MIB,
    )(*edges)
    table_shapes = [(stalk * stalk, 2 * maps), (width, width), (width, width)]
    bank_parts, spread_high, spread_low = kernel_call(
        tables_kernel,
        "tables",
        [jax.ShapeDtypeStruct(shape, jnp.bfloat16) for shape in table_shapes],
        [vmem] * 2,
        [vmem] * 3,
        vmem=4 * MIB,
    )(restriction.reshape(maps, stalk * stalk).T, mixing)

    sizes = (stalk, channels, maps, source_bits, node_bits, nodes)
    total_shape = jax.ShapeDtypeStruct((nodes, width), jnp.float32)

    def staged(number, stage, pieces, operands):
        rows = sum(piece.shape[0] for piece in pieces)
        operands = [listed[number], listed[number + 3], bank_parts] + pieces + operands
        aliases = {}
        out_shape = total_shape
        if stage != "soon":
            aliases = {3 + len(pieces): 1 if stage == "last" else 0}
        if stage == "last":
            out_shape = [jax.ShapeDtypeStruct((nodes, width), features.dtype), total_shape]
        return kernel_call(
            functools.partial(stage_kernel, sizes, len(pieces), stage),
            stage + "_edges",
            out_shape,
            [vmem] * len(operands),
            [anywhere, vmem] if stage == "last" else vmem,
            scratch=[
                pltpu.VMEM((2 * rows, LANES), jnp.float32),
                pltpu.SMEM((list_rows[number] + COUNT_ROWS, LANES), jnp.int32),
                pltpu.SemaphoreType.DMA,
                pltpu.VMEM((2 * EDGES, LANES), jnp.float32),
                pltpu.VMEM((width, EDGES), jnp.float32),
                pltpu.VMEM((stalk * stalk, EDGES), jnp.float32),
                pltpu.VMEM((width, EDGES), jnp.float32),
                pltpu.VMEM((2 * EDGES if stage == "last" else EDGES, width), jnp.bfloat16),
            ]
            + (
                [pltpu.VMEM((nodes, width), jnp.bfloat16), pltpu.SemaphoreType.DMA((nodes // (2 * EDGES),))]
                if stage == "last"
                else []
            ),
            vmem=rows * width * 4 + 6 * MIB,
            aliases=aliases,
        )(*operands)

    pieces = near_pieces + spread_near(across, near) + spread_near(before, near)
    total = staged(0, "soon", pieces, [])
    far_low, far_high = after([total], far_low, far_high)
    far = [list(pair) for pair in zip(spread_near(far_low, near), spread_near(far_high, near))]
    total = staged(1, "straight", far[0], [total, spread_high, spread_low, features])
    turned = [piece for pair in far[1:] for piece in pair]
    updated, _ = staged(2, "last", turned, [total, spread_high, spread_low])
    return updated


def solution(mesh):
    in_specs = (
        P(("blk", "rep"), None),
        P(),
        P(),
        P("blk", "rep", None, None),
        P("blk", "rep", None, None),
        P("blk", "rep", None, None),
        P("blk", "rep", None),
    )
    out_specs = P(("blk", "rep"), None)
    return jax.shard_map(body, mesh=mesh, in_specs=in_specs, out_specs=out_specs, check_vma=False)
```

```python
import functools

import jax
import jax.numpy as jnp
from jax import lax
from jax.experimental import pallas as pl
from jax.experimental.pallas import tpu as pltpu
from jax.sharding import PartitionSpec as P

EDGES = 256
LANES = 128
MIB = 1024 * 1024
COUNT_ROWS = 8
EARLY_ROWS = 24


def bits_for(count):
    return max(1, (count - 1).bit_length())


def passed_along(block, axis, distance):
    devices = range(lax.axis_size(axis))
    route = [((i - distance) % len(devices), i) for i in devices]
    return lax.ppermute(block, axis, route)


def swapped(block, bit):
    route = [(i, i ^ bit) for i in range(lax.axis_size("rep"))]
    return lax.ppermute(block, "rep", route)


def pack_kernel(counts_ref, *refs):
    index_refs, out_ref = refs[:-1], refs[-1]
    turns, capacity = index_refs[0].shape
    rows = capacity // LANES
    for turn in range(turns):
        for number, ref in enumerate(index_refs):
            start = (turn * len(index_refs) + number) * rows
            for row in range(rows):
                out_ref[start + row : start + row + 1, :] = ref[turn : turn + 1, row * LANES : (row + 1) * LANES]
    start = turns * len(index_refs) * rows
    out_ref[start:, :] = jnp.zeros((out_ref.shape[0] - start, LANES), jnp.int32)
    for turn in range(turns):
        out_ref[start + turn : start + turn + 1, :] = jnp.full((1, LANES), counts_ref[turn], jnp.int32)


def shifted_left(value, distance):
    rows = value.shape[0]
    if distance >= LANES:
        return pltpu.roll(value, rows - distance // LANES, 0)
    turned = pltpu.roll(value, LANES - distance, 1)
    lane = lax.broadcasted_iota(jnp.int32, value.shape, 1)
    return jnp.where(lane >= LANES - distance, pltpu.roll(turned, rows - 1, 0), turned)


def ones_where(condition):
    return jnp.where(condition, 1.0, 0.0).astype(jnp.bfloat16)


def closed_up(words):
    rows = words.shape[0]
    row = lax.broadcasted_iota(jnp.int32, (rows, LANES), 0)
    lane = lax.broadcasted_iota(jnp.int32, (rows, LANES), 1)
    used = ones_where(words != 0)
    upto = ones_where(lax.broadcasted_iota(jnp.int32, (LANES, LANES), 0) <= lax.broadcasted_iota(jnp.int32, (LANES, LANES), 1))
    above = ones_where(lax.broadcasted_iota(jnp.int32, (rows, rows), 1) < lax.broadcasted_iota(jnp.int32, (rows, rows), 0))
    every = jnp.ones((LANES, LANES), jnp.bfloat16)
    dot = functools.partial(jnp.dot, preferred_element_type=jnp.float32)
    earlier = dot(dot(above, used).astype(jnp.bfloat16), every)
    number = (earlier + dot(used, upto)).astype(jnp.int32)
    total = dot(dot(jnp.ones((8, rows), jnp.bfloat16), used).astype(jnp.bfloat16), every).astype(jnp.int32)
    way = jnp.where(words != 0, row * LANES + lane + 1 - number, 0)
    for bit in range(bits_for(rows * LANES)):
        moves = ((way >> bit) & 1) == 1
        moved_words = shifted_left(jnp.where(moves, words, 0), 1 << bit)
        moved_way = shifted_left(jnp.where(moves, way, 0), 1 << bit)
        words = jnp.where(moves, 0, words) | moved_words
        way = jnp.where(moves, 0, way) | moved_way
    return words, total


def pick_kernel(sizes, near, *refs):
    source_bits, target_bits, node_bits, capacity = sizes
    replicas = 2 * near
    edge_refs, refs = refs[:replicas], refs[replicas:]
    word_refs, place_refs, candidates_ref = refs[:4], refs[4:8], refs[8]
    rows = capacity // LANES
    node_mask = (1 << node_bits) - 1
    me = lax.axis_index("rep")
    positions = lax.broadcasted_iota(jnp.int32, (rows, LANES), 0) * LANES + lax.broadcasted_iota(
        jnp.int32, (rows, LANES), 1
    )
    part = replicas * rows
    for turn in range(2):
        for k, edge_ref in enumerate(edge_refs):
            start = turn * 3 * rows
            source = edge_ref[start : start + rows, :]
            target = edge_ref[start + rows : start + 2 * rows, :]
            map_id = edge_ref[start + 2 * rows : start + 3 * rows, :]
            live = positions < edge_ref[6 * rows + turn : 6 * rows + turn + 1, :]
            slot = (source >> node_bits) ^ me
            owner = (target >> node_bits) ^ me
            held = live & ((slot & (near - 1)) == 0)
            far = slot >= near
            word = (source & node_mask) | ((target & node_mask) << source_bits)
            word |= (map_id << (source_bits + target_bits)) | jnp.int32(1 << 30)
            soon = word | (jnp.where(far, 1, 0) << node_bits) if turn == 0 else word | (2 << node_bits)
            at = k * rows
            for other in range(2):
                wanted = held & (owner == other)
                first = 2 * other * part + turn * part + at
                candidates_ref[first : first + rows, :] = jnp.where(wanted if turn == 0 else wanted & ~far, soon, 0)
                if turn == 1:
                    first = (4 + other) * part + at
                    candidates_ref[first : first + rows, :] = jnp.where(wanted & far, word, 0)
    for number, (start, stop) in enumerate(((0, 2 * part), (2 * part, 4 * part), (4 * part, 5 * part), (5 * part, 6 * part))):
        words, total = closed_up(candidates_ref[start:stop, :])
        word_refs[number][...] = words
        place_refs[number][:COUNT_ROWS, :] = total
        place_refs[number][COUNT_ROWS:, :] = (words & ((1 << source_bits) - 1)) * 2


def tables_kernel(bank_ref, mixing_ref, bank_parts_ref, spread_high_ref, spread_low_ref):
    maps = bank_ref.shape[1]
    channels = mixing_ref.shape[0]
    width = spread_high_ref.shape[0]
    high, low = two_parts(bank_ref[...])
    bank_parts_ref[:, :maps] = high
    bank_parts_ref[:, maps:] = low
    dot = functools.partial(jnp.dot, preferred_element_type=jnp.float32)
    down = ones_where(
        lax.broadcasted_iota(jnp.int32, (width, channels), 0) % channels
        == lax.broadcasted_iota(jnp.int32, (width, channels), 1)
    )
    across = ones_where(
        lax.broadcasted_iota(jnp.int32, (channels, width), 1) % channels
        == lax.broadcasted_iota(jnp.int32, (channels, width), 0)
    )
    same = lax.broadcasted_iota(jnp.int32, (width, width), 0) // channels == (
        lax.broadcasted_iota(jnp.int32, (width, width), 1) // channels
    )
    for part, ref in zip(two_parts(mixing_ref[...]), (spread_high_ref, spread_low_ref)):
        tiled = dot(dot(down, part).astype(jnp.bfloat16), across)
        ref[...] = jnp.where(same, tiled, 0.0).astype(jnp.bfloat16)


def after_kernel(*refs):
    pass


def two_parts(value):
    high = value.astype(jnp.bfloat16)
    return high, (value - high.astype(jnp.float32)).astype(jnp.bfloat16)


def load_rows(piece_refs, rows_ref):
    start = 0
    for ref in piece_refs:
        rows = ref.shape[0]

        def widen(i, _, ref=ref, start=start):
            at = pl.multiple_of(i * LANES, LANES)
            value = ref[pl.ds(at, LANES), :].astype(jnp.float32)
            for half in range(2):
                rows_ref[pl.ds(2 * (start + at) + half, LANES, stride=2), :] = value[:, half * LANES : (half + 1) * LANES]
            return 0

        lax.fori_loop(0, rows // LANES, widen, 0, unroll=2)
        start += rows


def add_edges(sizes, words_ref, rows_ref, places_ref, total_ref, bank_parts_ref, gathered_ref, turned_ref, chosen_ref, message_ref, sent_ref, spread_refs=(), finish=None):
    stalk, channels, maps, source_bits, target_bits, nodes = sizes
    target_mask = (1 << target_bits) - 1
    map_mask = (1 << bits_for(maps)) - 1
    lists = EDGES // LANES
    blocks = words_ref.shape[0] // lists
    count = places_ref[0, 0]

    def gather(block):
        for u in range(EDGES):
            place = pl.multiple_of(places_ref[COUNT_ROWS + block * lists + u // LANES, u % LANES], 2)
            gathered_ref[2 * u : 2 * u + 2, :] = rows_ref[pl.ds(place, 2), :]

    def words_of(block):
        return jnp.concatenate([words_ref[pl.ds(block * lists + part, 1), :] for part in range(lists)], axis=1)

    def turn_rows():
        for part in range(lists):
            lanes = slice(part * LANES, (part + 1) * LANES)
            for half in range(2):
                values = gathered_ref[pl.ds(2 * part * LANES + half, LANES, stride=2), :]
                turned_ref[half * LANES : (half + 1) * LANES, lanes] = values.T

    def choose(block):
        map_ids = (words_of(block) >> (source_bits + target_bits)) & map_mask
        wanted = ones_where(lax.broadcasted_iota(jnp.int32, (maps, EDGES), 0) == map_ids)
        wanted = jnp.concatenate([wanted, wanted], axis=0)
        chosen_ref[...] = jnp.dot(bank_parts_ref[...], wanted, preferred_element_type=jnp.float32)

    def make_messages():
        for part in range(lists):
            lanes = slice(part * LANES, (part + 1) * LANES)
            features = turned_ref[:, lanes]
            for i in range(stalk):
                message = None
                for j in range(stalk):
                    factor = chosen_ref[i * stalk + j : i * stalk + j + 1, lanes]
                    term = factor * features[j * channels : (j + 1) * channels, :]
                    message = term if message is None else message + term
                message_ref[i * channels : (i + 1) * channels, lanes] = message

    def turn_messages():
        for part in range(lists):
            lanes = slice(part * LANES, (part + 1) * LANES)
            sent_ref[lanes, :] = message_ref[:, lanes].T.astype(jnp.bfloat16)
        if spread_refs:
            mixed = sum(jnp.dot(sent_ref[:EDGES, :], ref[...], preferred_element_type=jnp.float32) for ref in spread_refs)
            sent_ref[:EDGES, :], sent_ref[EDGES:, :] = two_parts(mixed)

    def scatter(block, finish=None):
        words = words_of(block)
        targets = jnp.where(words != 0, (words >> source_bits) & target_mask, -1)
        ids = lax.broadcasted_iota(jnp.int32, (EDGES, EDGES), 0).astype(jnp.bfloat16)
        one, zero = jnp.bfloat16(1), jnp.bfloat16(0)
        for start in range(0, nodes, 2 * EDGES):
            selectors = []
            for base in (start, start + EDGES):
                wanted_ids = (targets - base).astype(jnp.float32).astype(jnp.bfloat16)
                selectors.append(jnp.where(ids == wanted_ids, one, zero))
            selector = jnp.concatenate(selectors, axis=0)
            here = slice(start, start + 2 * EDGES)
            added = total_ref[here, :]
            for part in range(0, sent_ref.shape[0], EDGES):
                added += jnp.dot(selector, sent_ref[part : part + EDGES, :], preferred_element_type=jnp.float32)
            if finish is None:
                total_ref[here, :] = added
            else:
                finish(start, added)

    def step(block, _):
        turn_rows()
        choose(block)
        gather(jnp.minimum(block + 1, blocks - 1))
        scatter(block - 1)
        make_messages()
        turn_messages()
        return 0

    last = jnp.maximum(pl.cdiv(count, EDGES), 1) - 1
    gather(0)
    turn_rows()
    choose(0)
    gather(jnp.minimum(1, blocks - 1))
    make_messages()
    turn_messages()
    lax.fori_loop(1, last + 1, step, 0)
    scatter(last, finish)


def early_places(listed_ref, places_ref, sem):
    early = pl.ds(0, EARLY_ROWS)
    return pltpu.make_async_copy(listed_ref.at[early], places_ref.at[early], sem)


def late_places(listed_ref, places_ref, sem):
    @pl.when(places_ref[0, 0] > (EARLY_ROWS - COUNT_ROWS) * LANES)
    def _():
        rest = pl.ds(EARLY_ROWS, listed_ref.shape[0] - EARLY_ROWS)
        copy = pltpu.make_async_copy(listed_ref.at[rest], places_ref.at[rest], sem)
        copy.start()
        copy.wait()


def soon_kernel(sizes, piece_count, *refs):
    word_refs, listed_refs, (bank_parts_ref, spread_high_ref, spread_low_ref), refs = refs[:2], refs[2:4], refs[4:7], refs[7:]
    pieces, total_refs, refs = refs[:piece_count], refs[piece_count : piece_count + 2], refs[piece_count + 2 :]
    rows_ref, place_refs, sems, scratch = refs[0], refs[1:3], refs[3], refs[4:]
    copies = [early_places(listed_refs[i], place_refs[i], sems.at[i]) for i in range(2)]
    for copy in copies:
        copy.start()
    for total_ref in total_refs:
        total_ref[...] = jnp.zeros_like(total_ref)
    load_rows(pieces, rows_ref)
    for copy in copies:
        copy.wait()
    for i, total_ref in enumerate(total_refs):

        def mix(start, summed):
            here = pl.ds(start, 2 * EDGES)
            high, low = two_parts(summed)
            mixed = jnp.dot(high, spread_high_ref[...], preferred_element_type=jnp.float32)
            mixed += jnp.dot(high, spread_low_ref[...], preferred_element_type=jnp.float32)
            mixed += jnp.dot(low, spread_high_ref[...], preferred_element_type=jnp.float32)
            total_ref[here, :] = mixed if i == 1 else pieces[0][here, :].astype(jnp.float32) + mixed

        late_places(listed_refs[i], place_refs[i], sems.at[i])
        add_edges(sizes, word_refs[i], rows_ref, place_refs[i], total_ref, bank_parts_ref, *scratch, finish=mix)


def last_kernel(sizes, piece_count, gives, words_ref, listed_ref, bank_parts_ref, spread_high_ref, spread_low_ref, *refs):
    pieces, refs = refs[:piece_count], refs[piece_count + 1 :]
    total_ref, refs = refs[0], refs[1:]
    if gives:
        given_ref, refs = refs[0], refs[1:]
    rows_ref, places_ref, sem, *scratch = refs
    copy = early_places(listed_ref, places_ref, sem)
    copy.start()
    load_rows(pieces, rows_ref)
    copy.wait()
    late_places(listed_ref, places_ref, sem)

    def give(start, summed):
        given_ref[pl.ds(start, 2 * EDGES), :] = summed.astype(jnp.bfloat16)

    add_edges(
        sizes,
        words_ref,
        rows_ref,
        places_ref,
        total_ref,
        bank_parts_ref,
        *scratch,
        spread_refs=(spread_high_ref, spread_low_ref),
        finish=give if gives else None,
    )


def kernel_call(kernel, name, out_shape, in_specs, out_specs, scratch=(), vmem=MIB, aliases=None):
    return pl.pallas_call(
        kernel,
        out_shape=out_shape,
        in_specs=in_specs,
        out_specs=out_specs,
        scratch_shapes=list(scratch),
        input_output_aliases=aliases or {},
        compiler_params=pltpu.CompilerParams(vmem_limit_bytes=vmem),
        cost_estimate=pl.CostEstimate(flops=0, bytes_accessed=1_000, transcendentals=0),
        name=name,
    )


def body(features, restriction, mixing, source_index, target_index, map_index, edge_counts):
    nodes, width = features.shape
    replicas = lax.axis_size("rep")
    near = replicas // 2
    split = nodes // 2
    maps, stalk, _ = restriction.shape
    channels = mixing.shape[0]
    capacity = source_index.shape[3]
    turns = source_index.shape[2]
    node_bits = bits_for(nodes)
    source_bits = bits_for(3 * nodes)
    assert replicas == 4 and turns == 2
    assert nodes == 1 << node_bits and nodes % (2 * EDGES) == 0 and capacity % LANES == 0
    assert source_bits + node_bits + bits_for(maps) <= 30

    smem = pl.BlockSpec(memory_space=pltpu.SMEM)
    vmem = pl.BlockSpec(memory_space=pltpu.VMEM)
    anywhere = pl.BlockSpec(memory_space=pl.ANY)

    def after(earlier, *values):
        earlier = list(earlier)
        return kernel_call(
            after_kernel,
            "after",
            [jax.ShapeDtypeStruct(value.shape, value.dtype) for value in values],
            [anywhere] * (len(earlier) + len(values)),
            [anywhere] * len(values),
            aliases={len(earlier) + number: number for number in range(len(values))},
        )(*earlier, *values)

    before = passed_along(features, "blk", 1)
    across = swapped(features, near)
    own_edges = kernel_call(
        pack_kernel,
        "pack_edges",
        jax.ShapeDtypeStruct((3 * turns * capacity // LANES + 8, LANES), jnp.int32),
        [smem] + [vmem] * 3,
        vmem,
    )(edge_counts[0, 0], source_index[0, 0], target_index[0, 0], map_index[0, 0])
    edges = [own_edges] + [swapped(own_edges, bit) for bit in range(1, replicas)]
    across, before = after(edges[1:], across, before)
    far_low = passed_along(across[:split], "blk", 1)
    far_high = swapped(before[split:], near)
    part = replicas * capacity // LANES
    list_rows = (2 * part, 2 * part, part, part)
    listed = kernel_call(
        functools.partial(pick_kernel, (source_bits, node_bits, node_bits, capacity), near),
        "pick_edges",
        [jax.ShapeDtypeStruct((rows, LANES), jnp.int32) for rows in list_rows]
        + [jax.ShapeDtypeStruct((rows + COUNT_ROWS, LANES), jnp.int32) for rows in list_rows],
        [vmem] * replicas,
        [vmem] * 8,
        scratch=[pltpu.VMEM((6 * part, LANES), jnp.int32)],
        vmem=4 * MIB,
    )(*edges)
    table_shapes = [(stalk * stalk, 2 * maps), (width, width), (width, width)]
    bank_parts, spread_high, spread_low = kernel_call(
        tables_kernel,
        "tables",
        [jax.ShapeDtypeStruct(shape, jnp.bfloat16) for shape in table_shapes],
        [vmem] * 2,
        [vmem] * 3,
        vmem=4 * MIB,
    )(restriction.reshape(maps, stalk * stalk).T, mixing)

    sizes = (stalk, channels, maps, source_bits, node_bits, nodes)
    total_shape = jax.ShapeDtypeStruct((nodes, width), jnp.float32)

    def work_space(message_parts):
        return [
            pltpu.VMEM((2 * EDGES, LANES), jnp.float32),
            pltpu.VMEM((width, EDGES), jnp.float32),
            pltpu.VMEM((stalk * stalk, EDGES), jnp.float32),
            pltpu.VMEM((width, EDGES), jnp.float32),
            pltpu.VMEM((message_parts * EDGES, width), jnp.bfloat16),
        ]

    def places_of(number):
        return pltpu.SMEM((list_rows[number] + COUNT_ROWS, LANES), jnp.int32)

    tables = [bank_parts, spread_high, spread_low]
    pieces = [features, across, before]
    rows = len(pieces) * nodes
    own, other = kernel_call(
        functools.partial(soon_kernel, sizes, len(pieces)),
        "soon_edges",
        [total_shape] * 2,
        [vmem] * (7 + len(pieces)),
        [vmem] * 2,
        scratch=[pltpu.VMEM((2 * rows, LANES), jnp.float32), places_of(0), places_of(1), pltpu.SemaphoreType.DMA((2,))]
        + work_space(1),
        vmem=rows * width * 4 + 6 * MIB,
    )(*listed[:2], *listed[4:6], *tables, *pieces)

    def with_far(number, pieces, total, gives):
        given = [jax.ShapeDtypeStruct((nodes, width), jnp.bfloat16)] if gives else []
        return kernel_call(
            functools.partial(last_kernel, sizes, len(pieces), gives),
            "last_edges",
            [total_shape] + given,
            [vmem] * (6 + len(pieces)),
            [vmem] * (1 + len(given)),
            scratch=[pltpu.VMEM((2 * nodes, LANES), jnp.float32), places_of(number), pltpu.SemaphoreType.DMA]
            + work_space(2),
            vmem=nodes * width * 4 + 6 * MIB,
            aliases={5 + len(pieces): 0},
        )(listed[number], listed[number + 4], *tables, *pieces, total)

    far = after([own, other], far_low, far_high)
    _, given = with_far(3, far, other, True)
    taken = swapped(given, 1)
    (own,) = with_far(2, far, own, False)
    return (own + taken.astype(jnp.float32)).astype(features.dtype)


def solution(mesh):
    in_specs = (
        P(("blk", "rep"), None),
        P(),
        P(),
        P("blk", "rep", None, None),
        P("blk", "rep", None, None),
        P("blk", "rep", None, None),
        P("blk", "rep", None),
    )
    out_specs = P(("blk", "rep"), None)
    return jax.shard_map(body, mesh=mesh, in_specs=in_specs, out_specs=out_specs, check_vma=False)
```

```python
import functools

import jax
import jax.numpy as jnp
from jax import lax
from jax.experimental import pallas as pl
from jax.experimental.pallas import tpu as pltpu
from jax.sharding import PartitionSpec as P

EDGES = 256
LANES = 128
MIB = 1024 * 1024
COUNT_ROWS = 8
EARLY_ROWS = 24


def bits_for(count):
    return max(1, (count - 1).bit_length())


def passed_along(block, axis, distance):
    devices = range(lax.axis_size(axis))
    route = [((i - distance) % len(devices), i) for i in devices]
    return lax.ppermute(block, axis, route)


def swapped(block, bit):
    route = [(i, i ^ bit) for i in range(lax.axis_size("rep"))]
    return lax.ppermute(block, "rep", route)


def pack_kernel(counts_ref, *refs):
    index_refs, out_ref = refs[:-1], refs[-1]
    turns, capacity = index_refs[0].shape
    rows = capacity // LANES
    for turn in range(turns):
        for number, ref in enumerate(index_refs):
            start = (turn * len(index_refs) + number) * rows
            for row in range(rows):
                out_ref[start + row : start + row + 1, :] = ref[turn : turn + 1, row * LANES : (row + 1) * LANES]
    start = turns * len(index_refs) * rows
    out_ref[start:, :] = jnp.zeros((out_ref.shape[0] - start, LANES), jnp.int32)
    for turn in range(turns):
        out_ref[start + turn : start + turn + 1, :] = jnp.full((1, LANES), counts_ref[turn], jnp.int32)


def shifted_left(value, distance):
    rows = value.shape[0]
    if distance >= LANES:
        return pltpu.roll(value, rows - distance // LANES, 0)
    turned = pltpu.roll(value, LANES - distance, 1)
    lane = lax.broadcasted_iota(jnp.int32, value.shape, 1)
    return jnp.where(lane >= LANES - distance, pltpu.roll(turned, rows - 1, 0), turned)


def ones_where(condition):
    return jnp.where(condition, 1.0, 0.0).astype(jnp.bfloat16)


def closed_up(words):
    rows = words.shape[0]
    row = lax.broadcasted_iota(jnp.int32, (rows, LANES), 0)
    lane = lax.broadcasted_iota(jnp.int32, (rows, LANES), 1)
    used = ones_where(words != 0)
    upto = ones_where(lax.broadcasted_iota(jnp.int32, (LANES, LANES), 0) <= lax.broadcasted_iota(jnp.int32, (LANES, LANES), 1))
    above = ones_where(lax.broadcasted_iota(jnp.int32, (rows, rows), 1) < lax.broadcasted_iota(jnp.int32, (rows, rows), 0))
    every = jnp.ones((LANES, LANES), jnp.bfloat16)
    dot = functools.partial(jnp.dot, preferred_element_type=jnp.float32)
    earlier = dot(dot(above, used).astype(jnp.bfloat16), every)
    number = (earlier + dot(used, upto)).astype(jnp.int32)
    total = dot(dot(jnp.ones((8, rows), jnp.bfloat16), used).astype(jnp.bfloat16), every).astype(jnp.int32)
    way = jnp.where(words != 0, row * LANES + lane + 1 - number, 0)
    for bit in range(bits_for(rows * LANES)):
        moves = ((way >> bit) & 1) == 1
        moved_words = shifted_left(jnp.where(moves, words, 0), 1 << bit)
        moved_way = shifted_left(jnp.where(moves, way, 0), 1 << bit)
        words = jnp.where(moves, 0, words) | moved_words
        way = jnp.where(moves, 0, way) | moved_way
    return words, total


def pick_kernel(sizes, near, *refs):
    source_bits, target_bits, node_bits, capacity = sizes
    replicas = 2 * near
    edge_refs, refs = refs[:replicas], refs[replicas:]
    word_refs, place_refs, candidates_ref = refs[:4], refs[4:8], refs[8]
    rows = capacity // LANES
    node_mask = (1 << node_bits) - 1
    me = lax.axis_index("rep")
    positions = lax.broadcasted_iota(jnp.int32, (rows, LANES), 0) * LANES + lax.broadcasted_iota(
        jnp.int32, (rows, LANES), 1
    )
    part = replicas * rows
    for turn in range(2):
        for k, edge_ref in enumerate(edge_refs):
            start = turn * 3 * rows
            source = edge_ref[start : start + rows, :]
            target = edge_ref[start + rows : start + 2 * rows, :]
            map_id = edge_ref[start + 2 * rows : start + 3 * rows, :]
            live = positions < edge_ref[6 * rows + turn : 6 * rows + turn + 1, :]
            slot = (source >> node_bits) ^ me
            owner = (target >> node_bits) ^ me
            held = live & ((slot & (near - 1)) == 0)
            far = slot >= near
            word = (source & node_mask) | ((target & node_mask) << source_bits)
            word |= (map_id << (source_bits + target_bits)) | jnp.int32(1 << 30)
            soon = word | (jnp.where(far, 1, 0) << node_bits) if turn == 0 else word | (2 << node_bits)
            at = k * rows
            for other in range(2):
                wanted = held & (owner == other)
                first = 2 * other * part + turn * part + at
                candidates_ref[first : first + rows, :] = jnp.where(wanted if turn == 0 else wanted & ~far, soon, 0)
                if turn == 1:
                    wanted = live & far & (owner == 0) & ((slot & (near - 1)) == other)
                    first = (4 + other) * part + at
                    candidates_ref[first : first + rows, :] = jnp.where(wanted, word, 0)
    for number, (start, stop) in enumerate(((0, 2 * part), (2 * part, 4 * part), (4 * part, 5 * part), (5 * part, 6 * part))):
        words, total = closed_up(candidates_ref[start:stop, :])
        word_refs[number][...] = words
        place_refs[number][:COUNT_ROWS, :] = total
        place_refs[number][COUNT_ROWS:, :] = (words & ((1 << source_bits) - 1)) * 2


def tables_kernel(bank_ref, mixing_ref, bank_parts_ref, spread_high_ref, spread_low_ref):
    maps = bank_ref.shape[1]
    channels = mixing_ref.shape[0]
    width = spread_high_ref.shape[0]
    high, low = two_parts(bank_ref[...])
    bank_parts_ref[:, :maps] = high
    bank_parts_ref[:, maps:] = low
    dot = functools.partial(jnp.dot, preferred_element_type=jnp.float32)
    down = ones_where(
        lax.broadcasted_iota(jnp.int32, (width, channels), 0) % channels
        == lax.broadcasted_iota(jnp.int32, (width, channels), 1)
    )
    across = ones_where(
        lax.broadcasted_iota(jnp.int32, (channels, width), 1) % channels
        == lax.broadcasted_iota(jnp.int32, (channels, width), 0)
    )
    same = lax.broadcasted_iota(jnp.int32, (width, width), 0) // channels == (
        lax.broadcasted_iota(jnp.int32, (width, width), 1) // channels
    )
    for part, ref in zip(two_parts(mixing_ref[...]), (spread_high_ref, spread_low_ref)):
        tiled = dot(dot(down, part).astype(jnp.bfloat16), across)
        ref[...] = jnp.where(same, tiled, 0.0).astype(jnp.bfloat16)


def after_kernel(*refs):
    pass


def two_parts(value):
    high = value.astype(jnp.bfloat16)
    return high, (value - high.astype(jnp.float32)).astype(jnp.bfloat16)


def load_rows(piece_refs, rows_ref):
    start = 0
    for ref in piece_refs:
        rows = ref.shape[0]

        def widen(i, _, ref=ref, start=start):
            at = pl.multiple_of(i * LANES, LANES)
            value = ref[pl.ds(at, LANES), :].astype(jnp.float32)
            for half in range(2):
                rows_ref[pl.ds(2 * (start + at) + half, LANES, stride=2), :] = value[:, half * LANES : (half + 1) * LANES]
            return 0

        lax.fori_loop(0, rows // LANES, widen, 0, unroll=2)
        start += rows


def add_edges(sizes, words_ref, rows_ref, places_ref, total_ref, bank_parts_ref, gathered_ref, turned_ref, chosen_ref, message_ref, sent_ref, spread_refs=(), finish=None):
    stalk, channels, maps, source_bits, target_bits, nodes = sizes
    target_mask = (1 << target_bits) - 1
    map_mask = (1 << bits_for(maps)) - 1
    lists = EDGES // LANES
    blocks = words_ref.shape[0] // lists
    count = places_ref[0, 0]

    def gather(block):
        for u in range(EDGES):
            place = pl.multiple_of(places_ref[COUNT_ROWS + block * lists + u // LANES, u % LANES], 2)
            gathered_ref[2 * u : 2 * u + 2, :] = rows_ref[pl.ds(place, 2), :]

    def words_of(block):
        return jnp.concatenate([words_ref[pl.ds(block * lists + part, 1), :] for part in range(lists)], axis=1)

    def turn_rows():
        for part in range(lists):
            lanes = slice(part * LANES, (part + 1) * LANES)
            for half in range(2):
                values = gathered_ref[pl.ds(2 * part * LANES + half, LANES, stride=2), :]
                turned_ref[half * LANES : (half + 1) * LANES, lanes] = values.T

    def choose(block):
        map_ids = (words_of(block) >> (source_bits + target_bits)) & map_mask
        wanted = ones_where(lax.broadcasted_iota(jnp.int32, (maps, EDGES), 0) == map_ids)
        wanted = jnp.concatenate([wanted, wanted], axis=0)
        chosen_ref[...] = jnp.dot(bank_parts_ref[...], wanted, preferred_element_type=jnp.float32)

    def make_messages():
        for part in range(lists):
            lanes = slice(part * LANES, (part + 1) * LANES)
            features = turned_ref[:, lanes]
            for i in range(stalk):
                message = None
                for j in range(stalk):
                    factor = chosen_ref[i * stalk + j : i * stalk + j + 1, lanes]
                    term = factor * features[j * channels : (j + 1) * channels, :]
                    message = term if message is None else message + term
                message_ref[i * channels : (i + 1) * channels, lanes] = message

    def turn_messages():
        for part in range(lists):
            lanes = slice(part * LANES, (part + 1) * LANES)
            sent_ref[lanes, :] = message_ref[:, lanes].T.astype(jnp.bfloat16)
        if spread_refs:
            mixed = sum(jnp.dot(sent_ref[:EDGES, :], ref[...], preferred_element_type=jnp.float32) for ref in spread_refs)
            sent_ref[:EDGES, :], sent_ref[EDGES:, :] = two_parts(mixed)

    def scatter(block, finish=None):
        words = words_of(block)
        targets = jnp.where(words != 0, (words >> source_bits) & target_mask, -1)
        ids = lax.broadcasted_iota(jnp.int32, (EDGES, EDGES), 0).astype(jnp.bfloat16)
        one, zero = jnp.bfloat16(1), jnp.bfloat16(0)
        for start in range(0, nodes, 2 * EDGES):
            selectors = []
            for base in (start, start + EDGES):
                wanted_ids = (targets - base).astype(jnp.float32).astype(jnp.bfloat16)
                selectors.append(jnp.where(ids == wanted_ids, one, zero))
            selector = jnp.concatenate(selectors, axis=0)
            here = slice(start, start + 2 * EDGES)
            added = total_ref[here, :]
            for part in range(0, sent_ref.shape[0], EDGES):
                added += jnp.dot(selector, sent_ref[part : part + EDGES, :], preferred_element_type=jnp.float32)
            if finish is None:
                total_ref[here, :] = added
            else:
                finish(start, added)

    def step(block, _):
        turn_rows()
        choose(block)
        gather(jnp.minimum(block + 1, blocks - 1))
        scatter(block - 1)
        make_messages()
        turn_messages()
        return 0

    last = jnp.maximum(pl.cdiv(count, EDGES), 1) - 1
    gather(0)
    turn_rows()
    choose(0)
    gather(jnp.minimum(1, blocks - 1))
    make_messages()
    turn_messages()
    lax.fori_loop(1, last + 1, step, 0)
    scatter(last, finish)


def early_places(listed_ref, places_ref, sem):
    early = pl.ds(0, EARLY_ROWS)
    return pltpu.make_async_copy(listed_ref.at[early], places_ref.at[early], sem)


def late_places(listed_ref, places_ref, sem):
    @pl.when(places_ref[0, 0] > (EARLY_ROWS - COUNT_ROWS) * LANES)
    def _():
        rest = pl.ds(EARLY_ROWS, listed_ref.shape[0] - EARLY_ROWS)
        copy = pltpu.make_async_copy(listed_ref.at[rest], places_ref.at[rest], sem)
        copy.start()
        copy.wait()


def soon_kernel(sizes, piece_count, *refs):
    word_refs, listed_refs, (bank_parts_ref, spread_high_ref, spread_low_ref), refs = refs[:2], refs[2:4], refs[4:7], refs[7:]
    pieces, (own_ref, *given_refs), refs = refs[:piece_count], refs[piece_count : piece_count + 3], refs[piece_count + 3 :]
    other_ref, rows_ref, place_refs, sems, scratch = refs[0], refs[1], refs[2:4], refs[4], refs[5:]
    copies = [early_places(listed_refs[i], place_refs[i], sems.at[i]) for i in range(2)]
    for copy in copies:
        copy.start()
    for total_ref in (own_ref, other_ref):
        total_ref[...] = jnp.zeros_like(total_ref)
    load_rows(pieces, rows_ref)
    for copy in copies:
        copy.wait()

    def mixed(summed):
        high, low = two_parts(summed)
        result = jnp.dot(high, spread_high_ref[...], preferred_element_type=jnp.float32)
        result += jnp.dot(high, spread_low_ref[...], preferred_element_type=jnp.float32)
        return result + jnp.dot(low, spread_high_ref[...], preferred_element_type=jnp.float32)

    def give(start, summed):
        first = given_refs[0].shape[0]
        number, start = (0, start) if start < first else (1, start - first)
        given_refs[number][pl.ds(start, 2 * EDGES), :] = mixed(summed).astype(jnp.bfloat16)

    def keep(start, summed):
        here = pl.ds(start, 2 * EDGES)
        own_ref[here, :] = pieces[0][here, :].astype(jnp.float32) + mixed(summed)

    for i, total_ref, finish in ((1, other_ref, give), (0, own_ref, keep)):
        late_places(listed_refs[i], place_refs[i], sems.at[i])
        add_edges(sizes, word_refs[i], rows_ref, place_refs[i], total_ref, bank_parts_ref, *scratch, finish=finish)


def far_kernel(sizes, piece_count, last, words_ref, listed_ref, bank_parts_ref, spread_high_ref, spread_low_ref, *refs):
    pieces, refs = refs[:piece_count], refs[piece_count + 1 :]
    if last:
        *taken_refs, total_ref, out_ref, made_ref, out_sems = refs[:6]
        refs = refs[6:]
    else:
        total_ref, refs = refs[0], refs[1:]
    rows_ref, places_ref, sem, *scratch = refs
    copy = early_places(listed_ref, places_ref, sem)
    copy.start()
    load_rows(pieces, rows_ref)
    copy.wait()
    late_places(listed_ref, places_ref, sem)
    copies = []

    def give(start, summed):
        here = pl.ds(start, 2 * EDGES)
        first = taken_refs[0].shape[0]
        number, start = (0, start) if start < first else (1, start - first)
        taken = taken_refs[number][pl.ds(start, 2 * EDGES), :].astype(jnp.float32)
        made_ref[here, :] = (summed + taken).astype(jnp.bfloat16)
        copies.append(pltpu.make_async_copy(made_ref.at[here], out_ref.at[here], out_sems.at[len(copies)]))
        copies[-1].start()

    add_edges(
        sizes,
        words_ref,
        rows_ref,
        places_ref,
        total_ref,
        bank_parts_ref,
        *scratch,
        spread_refs=(spread_high_ref, spread_low_ref),
        finish=give if last else None,
    )
    for copy in copies:
        copy.wait()


def kernel_call(kernel, name, out_shape, in_specs, out_specs, scratch=(), vmem=MIB, aliases=None):
    return pl.pallas_call(
        kernel,
        out_shape=out_shape,
        in_specs=in_specs,
        out_specs=out_specs,
        scratch_shapes=list(scratch),
        input_output_aliases=aliases or {},
        compiler_params=pltpu.CompilerParams(vmem_limit_bytes=vmem),
        cost_estimate=pl.CostEstimate(flops=0, bytes_accessed=1_000, transcendentals=0),
        name=name,
    )


def body(features, restriction, mixing, source_index, target_index, map_index, edge_counts):
    nodes, width = features.shape
    replicas = lax.axis_size("rep")
    near = replicas // 2
    split = nodes * 7 // 16 // LANES * LANES
    maps, stalk, _ = restriction.shape
    channels = mixing.shape[0]
    capacity = source_index.shape[3]
    turns = source_index.shape[2]
    node_bits = bits_for(nodes)
    source_bits = bits_for(3 * nodes)
    assert replicas == 4 and turns == 2
    assert nodes == 1 << node_bits and nodes % (2 * EDGES) == 0 and nodes > 2 * EDGES and capacity % LANES == 0
    assert source_bits + node_bits + bits_for(maps) <= 30

    smem = pl.BlockSpec(memory_space=pltpu.SMEM)
    vmem = pl.BlockSpec(memory_space=pltpu.VMEM)
    anywhere = pl.BlockSpec(memory_space=pl.ANY)

    def after(earlier, *values):
        earlier = list(earlier)
        return kernel_call(
            after_kernel,
            "after",
            [jax.ShapeDtypeStruct(value.shape, value.dtype) for value in values],
            [anywhere] * (len(earlier) + len(values)),
            [anywhere] * len(values),
            aliases={len(earlier) + number: number for number in range(len(values))},
        )(*earlier, *values)

    before = passed_along(features, "blk", 1)
    across = swapped(features, near)
    own_edges = kernel_call(
        pack_kernel,
        "pack_edges",
        jax.ShapeDtypeStruct((3 * turns * capacity // LANES + 8, LANES), jnp.int32),
        [smem] + [vmem] * 3,
        vmem,
    )(edge_counts[0, 0], source_index[0, 0], target_index[0, 0], map_index[0, 0])
    edges = [own_edges] + [swapped(own_edges, bit) for bit in range(1, replicas)]
    part = replicas * capacity // LANES
    list_rows = (2 * part, 2 * part, part, part)
    listed = kernel_call(
        functools.partial(pick_kernel, (source_bits, node_bits, node_bits, capacity), near),
        "pick_edges",
        [jax.ShapeDtypeStruct((rows, LANES), jnp.int32) for rows in list_rows]
        + [jax.ShapeDtypeStruct((rows + COUNT_ROWS, LANES), jnp.int32) for rows in list_rows],
        [vmem] * replicas,
        [vmem] * 8,
        scratch=[pltpu.VMEM((6 * part, LANES), jnp.int32)],
        vmem=4 * MIB,
    )(*edges)
    table_shapes = [(stalk * stalk, 2 * maps), (width, width), (width, width)]
    bank_parts, spread_high, spread_low = kernel_call(
        tables_kernel,
        "tables",
        [jax.ShapeDtypeStruct(shape, jnp.bfloat16) for shape in table_shapes],
        [vmem] * 2,
        [vmem] * 3,
        vmem=4 * MIB,
    )(restriction.reshape(maps, stalk * stalk).T, mixing)

    (across,) = after(edges[1:], across)
    far_low = passed_along(across[:split], "blk", 1)
    (before,) = after(edges[1:] + [bank_parts], before)
    far_high = swapped(before[split:], near)

    sizes = (stalk, channels, maps, source_bits, node_bits, nodes)
    total_shape = jax.ShapeDtypeStruct((nodes, width), jnp.float32)

    def work_space(message_parts):
        return [
            pltpu.VMEM((2 * EDGES, LANES), jnp.float32),
            pltpu.VMEM((width, EDGES), jnp.float32),
            pltpu.VMEM((stalk * stalk, EDGES), jnp.float32),
            pltpu.VMEM((width, EDGES), jnp.float32),
            pltpu.VMEM((message_parts * EDGES, width), jnp.bfloat16),
        ]

    def places_of(number):
        return pltpu.SMEM((list_rows[number] + COUNT_ROWS, LANES), jnp.int32)

    tables = [bank_parts, spread_high, spread_low]
    pieces = [features, across, before]
    rows = len(pieces) * nodes
    first = nodes * 3 // 4 // (2 * EDGES) * (2 * EDGES)
    given_shapes = [jax.ShapeDtypeStruct((count, width), jnp.bfloat16) for count in (first, nodes - first)]
    own, *given = kernel_call(
        functools.partial(soon_kernel, sizes, len(pieces)),
        "soon_edges",
        [total_shape] + given_shapes,
        [vmem] * (7 + len(pieces)),
        [vmem] * 3,
        scratch=[
            pltpu.VMEM((nodes, width), jnp.float32),
            pltpu.VMEM((2 * rows, LANES), jnp.float32),
            places_of(0),
            places_of(1),
            pltpu.SemaphoreType.DMA((2,)),
        ]
        + work_space(1),
        vmem=(rows + nodes) * width * 4 + 6 * MIB,
    )(*listed[:2], *listed[4:6], *tables, *pieces)

    def with_far(number, pieces, total, taken=()):
        result = [jax.ShapeDtypeStruct((nodes, width), features.dtype)] if taken else []
        room = [pltpu.VMEM((nodes, width), features.dtype), pltpu.SemaphoreType.DMA((nodes // (2 * EDGES),))] if taken else []
        return kernel_call(
            functools.partial(far_kernel, sizes, len(pieces), bool(taken)),
            "last_edges" if taken else "straight_edges",
            [total_shape] + result,
            [vmem] * (6 + len(pieces) + len(taken)),
            [vmem] + [anywhere] * len(result),
            scratch=room
            + [pltpu.VMEM((2 * nodes, LANES), jnp.float32), places_of(number), pltpu.SemaphoreType.DMA]
            + work_space(2),
            vmem=nodes * width * 4 + 7 * MIB,
            aliases={5 + len(pieces): 0},
        )(listed[number], listed[number + 4], *tables, *pieces, total, *taken)

    taken = [swapped(part, 1) for part in given]
    far_low, far_high = after([own], far_low, far_high)
    (own,) = with_far(2, [far_low, far_high], own)
    _, updated = with_far(3, [swapped(far_low, 1), swapped(far_high, 1)], own, taken)
    return updated


def solution(mesh):
    in_specs = (
        P(("blk", "rep"), None),
        P(),
        P(),
        P("blk", "rep", None, None),
        P("blk", "rep", None, None),
        P("blk", "rep", None, None),
        P("blk", "rep", None),
    )
    out_specs = P(("blk", "rep"), None)
    return jax.shard_map(body, mesh=mesh, in_specs=in_specs, out_specs=out_specs, check_vma=False)
```

```python
import functools

import jax
import jax.numpy as jnp
from jax import lax
from jax.experimental import pallas as pl
from jax.experimental.pallas import tpu as pltpu
from jax.sharding import PartitionSpec as P

EDGES = 256
FAR_EDGES = 384
ROWS = 512
LANES = 128
MIB = 1024 * 1024
COUNT_ROWS = 8
EARLY_ROWS = 24


def bits_for(count):
    return max(1, (count - 1).bit_length())


def passed_along(block, axis, distance):
    devices = range(lax.axis_size(axis))
    route = [((i - distance) % len(devices), i) for i in devices]
    return lax.ppermute(block, axis, route)


def swapped(block, bit):
    route = [(i, i ^ bit) for i in range(lax.axis_size("rep"))]
    return lax.ppermute(block, "rep", route)


def shifted_left(value, distance):
    rows = value.shape[0]
    if distance >= LANES:
        return pltpu.roll(value, rows - distance // LANES, 0)
    turned = pltpu.roll(value, LANES - distance, 1)
    lane = lax.broadcasted_iota(jnp.int32, value.shape, 1)
    return jnp.where(lane >= LANES - distance, pltpu.roll(turned, rows - 1, 0), turned)


def ones_where(condition):
    return jnp.where(condition, 1.0, 0.0).astype(jnp.bfloat16)


def closed_up(words):
    rows = words.shape[0]
    row = lax.broadcasted_iota(jnp.int32, (rows, LANES), 0)
    lane = lax.broadcasted_iota(jnp.int32, (rows, LANES), 1)
    used = ones_where(words != 0)
    upto = ones_where(lax.broadcasted_iota(jnp.int32, (LANES, LANES), 0) <= lax.broadcasted_iota(jnp.int32, (LANES, LANES), 1))
    above = ones_where(lax.broadcasted_iota(jnp.int32, (rows, rows), 1) < lax.broadcasted_iota(jnp.int32, (rows, rows), 0))
    every = jnp.ones((LANES, LANES), jnp.bfloat16)
    dot = functools.partial(jnp.dot, preferred_element_type=jnp.float32)
    earlier = dot(dot(above, used).astype(jnp.bfloat16), every)
    number = (earlier + dot(used, upto)).astype(jnp.int32)
    total = dot(dot(jnp.ones((8, rows), jnp.bfloat16), used).astype(jnp.bfloat16), every).astype(jnp.int32)
    way = jnp.where(words != 0, row * LANES + lane + 1 - number, 0)
    for bit in range(bits_for(rows * LANES)):
        moves = ((way >> bit) & 1) == 1
        moved_words = shifted_left(jnp.where(moves, words, 0), 1 << bit)
        moved_way = shifted_left(jnp.where(moves, way, 0), 1 << bit)
        words = jnp.where(moves, 0, words) | moved_words
        way = jnp.where(moves, 0, way) | moved_way
    return words, total


def pick_kernel(sizes, near, *refs):
    source_bits, target_bits, node_bits, capacity = sizes
    replicas = 2 * near
    edge_refs, refs = refs[:replicas], refs[replicas:]
    word_refs, place_refs, candidates_ref, unpacked_ref = refs[:6], refs[6:12], refs[12], refs[13]
    rows = capacity // LANES
    node_mask = (1 << node_bits) - 1
    me = lax.axis_index("rep")
    positions = lax.broadcasted_iota(jnp.int32, (rows, LANES), 0) * LANES + lax.broadcasted_iota(
        jnp.int32, (rows, LANES), 1
    )
    part = replicas * rows
    for turn in range(2):
        for k, edge_ref in enumerate(edge_refs):
            for number in range(3):
                for row in range(rows):
                    at = number * rows + row
                    index_row = 2 * number + turn
                    unpacked_ref[at : at + 1, :] = edge_ref[index_row : index_row + 1, row * LANES : (row + 1) * LANES]
            source, target, map_id = (unpacked_ref[number * rows : (number + 1) * rows, :] for number in range(3))
            live = positions < edge_ref[6 + turn : 7 + turn, :LANES]
            slot = (source >> node_bits) ^ me
            owner = (target >> node_bits) ^ me
            held = live & ((slot & (near - 1)) == 0)
            far = slot >= near
            word = (source & node_mask) | ((target & node_mask) << source_bits)
            word |= (map_id << (source_bits + target_bits)) | jnp.int32(1 << 30)
            at = k * rows
            for other in range(2):
                wanted = held & (owner == other)
                choices = [((2 + 2 * other + turn) * part, wanted & (far if turn == 0 else ~far), word | (turn << node_bits))]
                if turn == 0:
                    choices.append((other * part, wanted & ~far, word))
                else:
                    turned = live & far & (owner == 0) & ((slot & (near - 1)) == other)
                    choices.append(((6 + other) * part, turned, word))
                for first, chosen, chosen_word in choices:
                    candidates_ref[first + at : first + at + rows, :] = jnp.where(chosen, chosen_word, 0)
    stops = [count * part for count in (0, 1, 2, 4, 6, 7, 8)]
    for number, (start, stop) in enumerate(zip(stops[:-1], stops[1:])):
        words, total = closed_up(candidates_ref[start:stop, :])
        count = stop - start
        for ref, head, values in ((word_refs[number], 0, words), (place_refs[number], COUNT_ROWS, (words & ((1 << source_bits) - 1)) * 2)):
            ref[head : head + count, :] = values
            if ref.shape[0] > head + count:
                ref[head + count :, :] = jnp.zeros((ref.shape[0] - head - count, LANES), jnp.int32)
        place_refs[number][:COUNT_ROWS, :] = total


def tables_kernel(bank_ref, mixing_ref, bank_parts_ref, spread_high_ref, spread_low_ref):
    maps = bank_ref.shape[1]
    channels = mixing_ref.shape[0]
    width = spread_high_ref.shape[0]
    high, low = two_parts(bank_ref[...])
    bank_parts_ref[:, :maps] = high
    bank_parts_ref[:, maps:] = low
    dot = functools.partial(jnp.dot, preferred_element_type=jnp.float32)
    down = ones_where(
        lax.broadcasted_iota(jnp.int32, (width, channels), 0) % channels
        == lax.broadcasted_iota(jnp.int32, (width, channels), 1)
    )
    across = ones_where(
        lax.broadcasted_iota(jnp.int32, (channels, width), 1) % channels
        == lax.broadcasted_iota(jnp.int32, (channels, width), 0)
    )
    same = lax.broadcasted_iota(jnp.int32, (width, width), 0) // channels == (
        lax.broadcasted_iota(jnp.int32, (width, width), 1) // channels
    )
    for part, ref in zip(two_parts(mixing_ref[...]), (spread_high_ref, spread_low_ref)):
        tiled = dot(dot(down, part).astype(jnp.bfloat16), across)
        ref[...] = jnp.where(same, tiled, 0.0).astype(jnp.bfloat16)


def after_kernel(*refs):
    pass


def two_parts(value):
    high = value.astype(jnp.bfloat16)
    return high, (value - high.astype(jnp.float32)).astype(jnp.bfloat16)


def load_rows(piece_refs, rows_ref):
    start = 0
    for ref in piece_refs:
        rows = ref.shape[0]

        def widen(i, _, ref=ref, start=start):
            at = pl.multiple_of(i * LANES, LANES)
            value = ref[pl.ds(at, LANES), :].astype(jnp.float32)
            for half in range(2):
                rows_ref[pl.ds(2 * (start + at) + half, LANES, stride=2), :] = value[:, half * LANES : (half + 1) * LANES]
            return 0

        lax.fori_loop(0, rows // LANES, widen, 0, unroll=2)
        start += rows


def add_edges(sizes, words_ref, rows_ref, places_ref, total_ref, bank_parts_ref, gathered_ref, turned_ref, chosen_ref, message_ref, sent_ref, spread_refs=(), finish=None):
    stalk, channels, maps, source_bits, target_bits, nodes = sizes
    target_mask = (1 << target_bits) - 1
    map_mask = (1 << bits_for(maps)) - 1
    edges = chosen_ref.shape[1]
    lists = edges // LANES
    blocks = words_ref.shape[0] // lists
    count = places_ref[0, 0]

    def gather(block):
        for u in range(edges):
            place = pl.multiple_of(places_ref[COUNT_ROWS + block * lists + u // LANES, u % LANES], 2)
            gathered_ref[2 * u : 2 * u + 2, :] = rows_ref[pl.ds(place, 2), :]

    def words_of(block):
        return jnp.concatenate([words_ref[pl.ds(block * lists + part, 1), :] for part in range(lists)], axis=1)

    def turn_rows():
        for part in range(lists):
            lanes = slice(part * LANES, (part + 1) * LANES)
            for half in range(2):
                values = gathered_ref[pl.ds(2 * part * LANES + half, LANES, stride=2), :]
                turned_ref[half * LANES : (half + 1) * LANES, lanes] = values.T

    def choose(block):
        map_ids = (words_of(block) >> (source_bits + target_bits)) & map_mask
        wanted = ones_where(lax.broadcasted_iota(jnp.int32, (maps, edges), 0) == map_ids)
        wanted = jnp.concatenate([wanted, wanted], axis=0)
        chosen_ref[...] = jnp.dot(bank_parts_ref[...], wanted, preferred_element_type=jnp.float32)

    def make_messages():
        for part in range(lists):
            lanes = slice(part * LANES, (part + 1) * LANES)
            features = turned_ref[:, lanes]
            for i in range(stalk):
                message = None
                for j in range(stalk):
                    factor = chosen_ref[i * stalk + j : i * stalk + j + 1, lanes]
                    term = factor * features[j * channels : (j + 1) * channels, :]
                    message = term if message is None else message + term
                message_ref[i * channels : (i + 1) * channels, lanes] = message

    def turn_messages():
        for part in range(lists):
            lanes = slice(part * LANES, (part + 1) * LANES)
            sent_ref[lanes, :] = message_ref[:, lanes].T.astype(jnp.bfloat16)
        if spread_refs:
            mixed = sum(jnp.dot(sent_ref[:edges, :], ref[...], preferred_element_type=jnp.float32) for ref in spread_refs)
            sent_ref[:edges, :], sent_ref[edges:, :] = two_parts(mixed)

    def scatter(block, finish=None):
        words = words_of(block)
        targets = jnp.where(words != 0, (words >> source_bits) & target_mask, -1)
        ids = lax.broadcasted_iota(jnp.int32, (256, edges), 0).astype(jnp.bfloat16)
        one, zero = jnp.bfloat16(1), jnp.bfloat16(0)
        for start in range(0, nodes, ROWS):
            selectors = []
            for base in range(start, start + ROWS, 256):
                wanted_ids = (targets - base).astype(jnp.float32).astype(jnp.bfloat16)
                selectors.append(jnp.where(ids == wanted_ids, one, zero))
            selector = jnp.concatenate(selectors, axis=0)
            here = slice(start, start + ROWS)
            added = total_ref[here, :]
            for part in range(0, sent_ref.shape[0], edges):
                added += jnp.dot(selector, sent_ref[part : part + edges, :], preferred_element_type=jnp.float32)
            if finish is None:
                total_ref[here, :] = added
            else:
                finish(start, added)

    def step(block, _):
        turn_rows()
        choose(block)
        gather(jnp.minimum(block + 1, blocks - 1))
        scatter(block - 1)
        make_messages()
        turn_messages()
        return 0

    last = jnp.maximum(pl.cdiv(count, edges), 1) - 1
    gather(0)
    turn_rows()
    choose(0)
    gather(jnp.minimum(1, blocks - 1))
    make_messages()
    turn_messages()
    lax.fori_loop(1, last + 1, step, 0)
    scatter(last, finish)


def early_places(listed_ref, places_ref, sem):
    early = pl.ds(0, EARLY_ROWS)
    return pltpu.make_async_copy(listed_ref.at[early], places_ref.at[early], sem)


def late_places(listed_ref, places_ref, sem):
    @pl.when(places_ref[0, 0] > (EARLY_ROWS - COUNT_ROWS) * LANES)
    def _():
        rest = pl.ds(EARLY_ROWS, listed_ref.shape[0] - EARLY_ROWS)
        copy = pltpu.make_async_copy(listed_ref.at[rest], places_ref.at[rest], sem)
        copy.start()
        copy.wait()


def near_kernel(sizes, piece_count, soon, *refs):
    word_refs, listed_refs, (bank_parts_ref, spread_high_ref, spread_low_ref), refs = refs[:2], refs[2:4], refs[4:7], refs[7:]
    pieces, refs = refs[:piece_count], refs[piece_count:]
    if soon:
        features_ref, _, _, own_ref, other_ref, *given_refs = refs[:7]
        refs = refs[7:]
    else:
        own_ref, other_ref, refs = refs[0], refs[1], refs[2:]
    rows_ref, place_refs, sems, scratch = refs[0], refs[1:3], refs[3], refs[4:]
    copies = [early_places(listed_refs[i], place_refs[i], sems.at[i]) for i in range(2)]
    for copy in copies:
        copy.start()
    if not soon:
        for total_ref in (own_ref, other_ref):
            total_ref[...] = jnp.zeros_like(total_ref)
    load_rows(pieces, rows_ref)
    for copy in copies:
        copy.wait()

    def mixed(summed):
        high, low = two_parts(summed)
        result = jnp.dot(high, spread_high_ref[...], preferred_element_type=jnp.float32)
        result += jnp.dot(high, spread_low_ref[...], preferred_element_type=jnp.float32)
        return result + jnp.dot(low, spread_high_ref[...], preferred_element_type=jnp.float32)

    def give(start, summed):
        first = given_refs[0].shape[0]
        number, start = (0, start) if start < first else (1, start - first)
        given_refs[number][pl.ds(start, ROWS), :] = mixed(summed).astype(jnp.bfloat16)

    def keep(start, summed):
        here = pl.ds(start, ROWS)
        own_ref[here, :] = features_ref[here, :].astype(jnp.float32) + mixed(summed)

    for i, total_ref, finish in ((1, other_ref, give), (0, own_ref, keep)):
        late_places(listed_refs[i], place_refs[i], sems.at[i])
        add_edges(
            sizes,
            word_refs[i],
            rows_ref,
            place_refs[i],
            total_ref,
            bank_parts_ref,
            *scratch,
            finish=finish if soon else None,
        )


def far_kernel(sizes, piece_count, last, words_ref, listed_ref, bank_parts_ref, spread_high_ref, spread_low_ref, *refs):
    pieces, refs = refs[:piece_count], refs[piece_count + 1 :]
    if last:
        *taken_refs, total_ref, out_ref, made_ref, out_sems = refs[:6]
        refs = refs[6:]
    else:
        total_ref, refs = refs[0], refs[1:]
    rows_ref, places_ref, sem, *scratch = refs
    copy = early_places(listed_ref, places_ref, sem)
    copy.start()
    load_rows(pieces, rows_ref)
    copy.wait()
    late_places(listed_ref, places_ref, sem)
    copies = []

    def give(start, summed):
        here = pl.ds(start, ROWS)
        first = taken_refs[0].shape[0]
        number, start = (0, start) if start < first else (1, start - first)
        taken = taken_refs[number][pl.ds(start, ROWS), :].astype(jnp.float32)
        made_ref[here, :] = (summed + taken).astype(jnp.bfloat16)
        copies.append(pltpu.make_async_copy(made_ref.at[here], out_ref.at[here], out_sems.at[len(copies)]))
        copies[-1].start()

    add_edges(
        sizes,
        words_ref,
        rows_ref,
        places_ref,
        total_ref,
        bank_parts_ref,
        *scratch,
        spread_refs=(spread_high_ref, spread_low_ref),
        finish=give if last else None,
    )
    for copy in copies:
        copy.wait()


def kernel_call(kernel, name, out_shape, in_specs, out_specs, scratch=(), vmem=MIB, aliases=None):
    return pl.pallas_call(
        kernel,
        out_shape=out_shape,
        in_specs=in_specs,
        out_specs=out_specs,
        scratch_shapes=list(scratch),
        input_output_aliases=aliases or {},
        compiler_params=pltpu.CompilerParams(vmem_limit_bytes=vmem),
        cost_estimate=pl.CostEstimate(flops=0, bytes_accessed=1_000, transcendentals=0),
        name=name,
    )


def body(features, restriction, mixing, source_index, target_index, map_index, edge_counts):
    nodes, width = features.shape
    replicas = lax.axis_size("rep")
    near = replicas // 2
    split = nodes // 2
    maps, stalk, _ = restriction.shape
    channels = mixing.shape[0]
    capacity = source_index.shape[3]
    turns = source_index.shape[2]
    node_bits = bits_for(nodes)
    source_bits = bits_for(2 * nodes)
    assert replicas == 4 and turns == 2
    assert nodes == 1 << node_bits and nodes % ROWS == 0 and nodes > ROWS and capacity % LANES == 0
    assert source_bits + node_bits + bits_for(maps) <= 30

    smem = pl.BlockSpec(memory_space=pltpu.SMEM)
    vmem = pl.BlockSpec(memory_space=pltpu.VMEM)
    anywhere = pl.BlockSpec(memory_space=pl.ANY)

    def after(earlier, *values):
        earlier = list(earlier)
        return kernel_call(
            after_kernel,
            "after",
            [jax.ShapeDtypeStruct(value.shape, value.dtype) for value in values],
            [anywhere] * (len(earlier) + len(values)),
            [anywhere] * len(values),
            aliases={len(earlier) + number: number for number in range(len(values))},
        )(*earlier, *values)

    before = passed_along(features, "blk", 1)
    counts = jnp.broadcast_to(edge_counts[0, 0][:, None], (turns, capacity))
    own_edges = jnp.concatenate([source_index[0, 0], target_index[0, 0], map_index[0, 0], counts], axis=0)
    edges = [own_edges] + [swapped(own_edges, bit) for bit in range(1, replicas)]
    (ready,) = after(edges[1:], features)
    across = swapped(ready, near)
    part = replicas * capacity // LANES
    list_edges = (EDGES, EDGES, EDGES, EDGES, FAR_EDGES, FAR_EDGES)
    list_rows = [
        pl.cdiv(count * part * LANES, edges_at_once) * edges_at_once // LANES
        for count, edges_at_once in zip((1, 1, 2, 2, 1, 1), list_edges)
    ]
    listed = kernel_call(
        functools.partial(pick_kernel, (source_bits, node_bits, node_bits, capacity), near),
        "pick_edges",
        [jax.ShapeDtypeStruct((rows, LANES), jnp.int32) for rows in list_rows]
        + [jax.ShapeDtypeStruct((rows + COUNT_ROWS, LANES), jnp.int32) for rows in list_rows],
        [vmem] * replicas,
        [vmem] * 12,
        scratch=[
            pltpu.VMEM((8 * part, LANES), jnp.int32),
            pltpu.VMEM((3 * capacity // LANES, LANES), jnp.int32),
        ],
        vmem=4 * MIB,
    )(*edges)
    table_shapes = [(stalk * stalk, 2 * maps), (width, width), (width, width)]
    bank_parts, spread_high, spread_low = kernel_call(
        tables_kernel,
        "tables",
        [jax.ShapeDtypeStruct(shape, jnp.bfloat16) for shape in table_shapes],
        [vmem] * 2,
        [vmem] * 3,
        vmem=4 * MIB,
    )(restriction.reshape(maps, stalk * stalk).T, mixing)

    sizes = (stalk, channels, maps, source_bits, node_bits, nodes)
    total_shape = jax.ShapeDtypeStruct((nodes, width), jnp.float32)

    def work_space(edges_at_once, message_parts):
        return [
            pltpu.VMEM((2 * edges_at_once, LANES), jnp.float32),
            pltpu.VMEM((width, edges_at_once), jnp.float32),
            pltpu.VMEM((stalk * stalk, edges_at_once), jnp.float32),
            pltpu.VMEM((width, edges_at_once), jnp.float32),
            pltpu.VMEM((message_parts * edges_at_once, width), jnp.bfloat16),
        ]

    def places_of(number):
        return pltpu.SMEM((list_rows[number] + COUNT_ROWS, LANES), jnp.int32)

    tables = [bank_parts, spread_high, spread_low]
    first = nodes * 3 // 4 // ROWS * ROWS
    given_shapes = [jax.ShapeDtypeStruct((count, width), jnp.bfloat16) for count in (first, nodes - first)]

    def with_near(number, pieces, totals=()):
        rows = len(pieces) * nodes
        own_features = [features] if totals else []
        return kernel_call(
            functools.partial(near_kernel, sizes, len(pieces), bool(totals)),
            "soon_edges" if totals else "own_edges",
            [total_shape] * 2 + (given_shapes if totals else []),
            [vmem] * (7 + len(pieces) + len(own_features) + len(totals)),
            [vmem] * (4 if totals else 2),
            scratch=[
                pltpu.VMEM((2 * rows, LANES), jnp.float32),
                places_of(number),
                places_of(number + 1),
                pltpu.SemaphoreType.DMA((2,)),
            ]
            + work_space(EDGES, 1),
            vmem=rows * width * 4 + 6 * MIB,
            aliases={8 + len(pieces) + i: i for i in range(len(totals))},
        )(*listed[number : number + 2], *listed[number + 6 : number + 8], *tables, *pieces, *own_features, *totals)

    totals = with_near(0, [features])
    (across,) = after(totals, across)
    far_low = passed_along(across[:split], "blk", 1)
    (before,) = after(totals, before)
    far_high = swapped(before[split:], near)
    own, _, *given = with_near(2, [across, before], totals)

    def with_far(number, pieces, total, taken=()):
        result = [jax.ShapeDtypeStruct((nodes, width), features.dtype)] if taken else []
        room = [pltpu.VMEM((nodes, width), features.dtype), pltpu.SemaphoreType.DMA((nodes // ROWS,))] if taken else []
        return kernel_call(
            functools.partial(far_kernel, sizes, len(pieces), bool(taken)),
            "last_edges" if taken else "straight_edges",
            [total_shape] + result,
            [vmem] * (6 + len(pieces) + len(taken)),
            [vmem] + [anywhere] * len(result),
            scratch=room
            + [pltpu.VMEM((2 * nodes, LANES), jnp.float32), places_of(number), pltpu.SemaphoreType.DMA]
            + work_space(FAR_EDGES, 2),
            vmem=nodes * width * 4 + 8 * MIB,
            aliases={5 + len(pieces): 0},
        )(listed[number], listed[number + 6], *tables, *pieces, total, *taken)

    taken = [swapped(part, 1) for part in given]
    far_low, far_high = after([own], far_low, far_high)
    (own,) = with_far(4, [far_low, far_high], own)
    _, updated = with_far(5, [swapped(far_low, 1), swapped(far_high, 1)], own, taken)
    return updated


def solution(mesh):
    in_specs = (
        P(("blk", "rep"), None),
        P(),
        P(),
        P("blk", "rep", None, None),
        P("blk", "rep", None, None),
        P("blk", "rep", None, None),
        P("blk", "rep", None),
    )
    out_specs = P(("blk", "rep"), None)
    return jax.shard_map(body, mesh=mesh, in_specs=in_specs, out_specs=out_specs, check_vma=False)
```

```python
import functools

import jax
import jax.numpy as jnp
from jax import lax
from jax.experimental import pallas as pl
from jax.experimental.pallas import tpu as pltpu
from jax.sharding import PartitionSpec as P

EDGES = 256
ROWS = 512
LANES = 128
MIB = 1024 * 1024
COUNT_ROWS = 8
EARLY_ROWS = 24


def bits_for(count):
    return max(1, (count - 1).bit_length())


def passed_along(block, axis, distance):
    devices = range(lax.axis_size(axis))
    route = [((i - distance) % len(devices), i) for i in devices]
    return lax.ppermute(block, axis, route)


def swapped(block, bit):
    route = [(i, i ^ bit) for i in range(lax.axis_size("rep"))]
    return lax.ppermute(block, "rep", route)


def shifted_left(value, distance):
    rows = value.shape[0]
    if distance >= LANES:
        return pltpu.roll(value, rows - distance // LANES, 0)
    turned = pltpu.roll(value, LANES - distance, 1)
    lane = lax.broadcasted_iota(jnp.int32, value.shape, 1)
    return jnp.where(lane >= LANES - distance, pltpu.roll(turned, rows - 1, 0), turned)


def ones_where(condition):
    return jnp.where(condition, 1.0, 0.0).astype(jnp.bfloat16)


def closed_up(words):
    rows = words.shape[0]
    row = lax.broadcasted_iota(jnp.int32, (rows, LANES), 0)
    lane = lax.broadcasted_iota(jnp.int32, (rows, LANES), 1)
    used = ones_where(words != 0)
    upto = ones_where(lax.broadcasted_iota(jnp.int32, (LANES, LANES), 0) <= lax.broadcasted_iota(jnp.int32, (LANES, LANES), 1))
    above = ones_where(lax.broadcasted_iota(jnp.int32, (rows, rows), 1) < lax.broadcasted_iota(jnp.int32, (rows, rows), 0))
    every = jnp.ones((LANES, LANES), jnp.bfloat16)
    dot = functools.partial(jnp.dot, preferred_element_type=jnp.float32)
    earlier = dot(dot(above, used).astype(jnp.bfloat16), every)
    number = (earlier + dot(used, upto)).astype(jnp.int32)
    total = dot(dot(jnp.ones((8, rows), jnp.bfloat16), used).astype(jnp.bfloat16), every).astype(jnp.int32)
    way = jnp.where(words != 0, row * LANES + lane + 1 - number, 0)
    for bit in range(bits_for(rows * LANES)):
        moves = ((way >> bit) & 1) == 1
        moved_words = shifted_left(jnp.where(moves, words, 0), 1 << bit)
        moved_way = shifted_left(jnp.where(moves, way, 0), 1 << bit)
        words = jnp.where(moves, 0, words) | moved_words
        way = jnp.where(moves, 0, way) | moved_way
    return words, total


def pick_kernel(sizes, near, *refs):
    source_bits, target_bits, node_bits, capacity = sizes
    replicas = 2 * near
    edge_refs, refs = refs[:replicas], refs[replicas:]
    word_refs, place_refs, candidates_ref, unpacked_ref = refs[:6], refs[6:12], refs[12], refs[13]
    rows = capacity // LANES
    node_mask = (1 << node_bits) - 1
    me = lax.axis_index("rep")
    positions = lax.broadcasted_iota(jnp.int32, (rows, LANES), 0) * LANES + lax.broadcasted_iota(
        jnp.int32, (rows, LANES), 1
    )
    part = replicas * rows
    for turn in range(2):
        for k, edge_ref in enumerate(edge_refs):
            for number in range(3):
                for row in range(rows):
                    at = number * rows + row
                    index_row = 2 * number + turn
                    unpacked_ref[at : at + 1, :] = edge_ref[index_row : index_row + 1, row * LANES : (row + 1) * LANES]
            source, target, map_id = (unpacked_ref[number * rows : (number + 1) * rows, :] for number in range(3))
            live = positions < edge_ref[6 + turn : 7 + turn, :LANES]
            slot = (source >> node_bits) ^ me
            owner = (target >> node_bits) ^ me
            held = live & ((slot & (near - 1)) == 0)
            far = slot >= near
            word = (source & node_mask) | ((target & node_mask) << source_bits)
            word |= (map_id << (source_bits + target_bits)) | jnp.int32(1 << 30)
            at = k * rows
            for other in range(2):
                wanted = held & (owner == other)
                choices = [((2 + 2 * other + turn) * part, wanted & (far if turn == 0 else ~far), word | (turn << node_bits))]
                if turn == 0:
                    choices.append((other * part, wanted & ~far, word))
                else:
                    turned = live & far & (owner == 0) & ((slot & (near - 1)) == other)
                    choices.append(((6 + other) * part, turned, word))
                for first, chosen, chosen_word in choices:
                    candidates_ref[first + at : first + at + rows, :] = jnp.where(chosen, chosen_word, 0)
    stops = [count * part for count in (0, 1, 2, 4, 6, 7, 8)]
    for number, (start, stop) in enumerate(zip(stops[:-1], stops[1:])):
        words, total = closed_up(candidates_ref[start:stop, :])
        word_refs[number][...] = words
        place_refs[number][:COUNT_ROWS, :] = total
        place_refs[number][COUNT_ROWS:, :] = (words & ((1 << source_bits) - 1)) * 2


def tables_kernel(bank_ref, mixing_ref, bank_parts_ref, spread_high_ref, spread_low_ref):
    maps = bank_ref.shape[1]
    channels = mixing_ref.shape[0]
    width = spread_high_ref.shape[0]
    high, low = two_parts(bank_ref[...])
    bank_parts_ref[:, :maps] = high
    bank_parts_ref[:, maps:] = low
    dot = functools.partial(jnp.dot, preferred_element_type=jnp.float32)
    down = ones_where(
        lax.broadcasted_iota(jnp.int32, (width, channels), 0) % channels
        == lax.broadcasted_iota(jnp.int32, (width, channels), 1)
    )
    across = ones_where(
        lax.broadcasted_iota(jnp.int32, (channels, width), 1) % channels
        == lax.broadcasted_iota(jnp.int32, (channels, width), 0)
    )
    same = lax.broadcasted_iota(jnp.int32, (width, width), 0) // channels == (
        lax.broadcasted_iota(jnp.int32, (width, width), 1) // channels
    )
    for part, ref in zip(two_parts(mixing_ref[...]), (spread_high_ref, spread_low_ref)):
        tiled = dot(dot(down, part).astype(jnp.bfloat16), across)
        ref[...] = jnp.where(same, tiled, 0.0).astype(jnp.bfloat16)


def after_kernel(*refs):
    pass


def two_parts(value):
    high = value.astype(jnp.bfloat16)
    return high, (value - high.astype(jnp.float32)).astype(jnp.bfloat16)


def load_rows(piece_refs, rows_ref):
    start = 0
    for ref in piece_refs:
        rows = ref.shape[0]

        def widen(i, _, ref=ref, start=start):
            at = pl.multiple_of(i * LANES, LANES)
            value = ref[pl.ds(at, LANES), :].astype(jnp.float32)
            for half in range(2):
                rows_ref[pl.ds(2 * (start + at) + half, LANES, stride=2), :] = value[:, half * LANES : (half + 1) * LANES]
            return 0

        lax.fori_loop(0, rows // LANES, widen, 0, unroll=2)
        start += rows


def add_edges(sizes, words_ref, rows_ref, places_ref, total_ref, bank_parts_ref, gathered_ref, turned_ref, chosen_ref, message_ref, sent_ref, spread_refs=(), finish=None):
    stalk, channels, maps, source_bits, target_bits, nodes = sizes
    target_mask = (1 << target_bits) - 1
    map_mask = (1 << bits_for(maps)) - 1
    edges = EDGES
    lists = edges // LANES
    blocks = words_ref.shape[0] // lists
    count = places_ref[0, 0]

    def gather(block):
        for u in range(edges):
            place = pl.multiple_of(places_ref[COUNT_ROWS + block * lists + u // LANES, u % LANES], 2)
            gathered_ref[2 * u : 2 * u + 2, :] = rows_ref[pl.ds(place, 2), :]

    def words_of(block):
        return jnp.concatenate([words_ref[pl.ds(block * lists + part, 1), :] for part in range(lists)], axis=1)

    def turn_rows():
        for part in range(lists):
            lanes = slice(part * LANES, (part + 1) * LANES)
            for half in range(2):
                values = gathered_ref[pl.ds(2 * part * LANES + half, LANES, stride=2), :]
                turned_ref[half * LANES : (half + 1) * LANES, lanes] = values.T

    def choose(block):
        map_ids = (words_of(block) >> (source_bits + target_bits)) & map_mask
        wanted = ones_where(lax.broadcasted_iota(jnp.int32, (maps, edges), 0) == map_ids)
        wanted = jnp.concatenate([wanted, wanted], axis=0)
        chosen_ref[...] = jnp.dot(bank_parts_ref[...], wanted, preferred_element_type=jnp.float32)

    def make_messages():
        for part in range(lists):
            lanes = slice(part * LANES, (part + 1) * LANES)
            features = turned_ref[:, lanes]
            for i in range(stalk):
                message = None
                for j in range(stalk):
                    factor = chosen_ref[i * stalk + j : i * stalk + j + 1, lanes]
                    term = factor * features[j * channels : (j + 1) * channels, :]
                    message = term if message is None else message + term
                message_ref[i * channels : (i + 1) * channels, lanes] = message

    def turn_messages():
        for part in range(lists):
            lanes = slice(part * LANES, (part + 1) * LANES)
            sent_ref[lanes, :] = message_ref[:, lanes].T.astype(jnp.bfloat16)
        if spread_refs:
            mixed = sum(jnp.dot(sent_ref[:edges, :], ref[...], preferred_element_type=jnp.float32) for ref in spread_refs)
            sent_ref[:edges, :], sent_ref[edges:, :] = two_parts(mixed)

    def scatter(block, finish=None):
        words = words_of(block)
        targets = jnp.where(words != 0, (words >> source_bits) & target_mask, -1)
        ids = lax.broadcasted_iota(jnp.int32, (256, edges), 0).astype(jnp.bfloat16)
        one, zero = jnp.bfloat16(1), jnp.bfloat16(0)
        for start in range(0, nodes, ROWS):
            selectors = []
            for base in range(start, start + ROWS, 256):
                wanted_ids = (targets - base).astype(jnp.float32).astype(jnp.bfloat16)
                selectors.append(jnp.where(ids == wanted_ids, one, zero))
            selector = jnp.concatenate(selectors, axis=0)
            here = slice(start, start + ROWS)
            added = total_ref[here, :]
            for part in range(0, sent_ref.shape[0], edges):
                added += jnp.dot(selector, sent_ref[part : part + edges, :], preferred_element_type=jnp.float32)
            if finish is None:
                total_ref[here, :] = added
            else:
                finish(start, added)

    def step(block, _):
        turn_rows()
        choose(block)
        gather(jnp.minimum(block + 1, blocks - 1))
        scatter(block - 1)
        make_messages()
        turn_messages()
        return 0

    last = jnp.maximum(pl.cdiv(count, edges), 1) - 1
    gather(0)
    turn_rows()
    choose(0)
    gather(jnp.minimum(1, blocks - 1))
    make_messages()
    turn_messages()
    lax.fori_loop(1, last + 1, step, 0)
    scatter(last, finish)


def early_places(listed_ref, places_ref, sem):
    early = pl.ds(0, EARLY_ROWS)
    return pltpu.make_async_copy(listed_ref.at[early], places_ref.at[early], sem)


def late_places(listed_ref, places_ref, sem):
    @pl.when(places_ref[0, 0] > (EARLY_ROWS - COUNT_ROWS) * LANES)
    def _():
        rest = pl.ds(EARLY_ROWS, listed_ref.shape[0] - EARLY_ROWS)
        copy = pltpu.make_async_copy(listed_ref.at[rest], places_ref.at[rest], sem)
        copy.start()
        copy.wait()


def near_kernel(sizes, piece_count, soon, *refs):
    word_refs, listed_refs, (bank_parts_ref, spread_high_ref, spread_low_ref), refs = refs[:2], refs[2:4], refs[4:7], refs[7:]
    pieces, refs = refs[:piece_count], refs[piece_count:]
    if soon:
        features_ref, _, _, own_ref, other_ref, *given_refs = refs[:7]
        refs = refs[7:]
    else:
        own_ref, other_ref, refs = refs[0], refs[1], refs[2:]
    rows_ref, place_refs, sems, scratch = refs[0], refs[1:3], refs[3], refs[4:]
    copies = [early_places(listed_refs[i], place_refs[i], sems.at[i]) for i in range(2)]
    for copy in copies:
        copy.start()
    if not soon:
        for total_ref in (own_ref, other_ref):
            total_ref[...] = jnp.zeros_like(total_ref)
    load_rows(pieces, rows_ref)
    for copy in copies:
        copy.wait()

    def mixed(summed):
        high, low = two_parts(summed)
        result = jnp.dot(high, spread_high_ref[...], preferred_element_type=jnp.float32)
        result += jnp.dot(high, spread_low_ref[...], preferred_element_type=jnp.float32)
        return result + jnp.dot(low, spread_high_ref[...], preferred_element_type=jnp.float32)

    def give(start, summed):
        first = given_refs[0].shape[0]
        number, start = (0, start) if start < first else (1, start - first)
        given_refs[number][pl.ds(start, ROWS), :] = mixed(summed).astype(jnp.bfloat16)

    def keep(start, summed):
        here = pl.ds(start, ROWS)
        own_ref[here, :] = features_ref[here, :].astype(jnp.float32) + mixed(summed)

    for i, total_ref, finish in ((1, other_ref, give), (0, own_ref, keep)):
        late_places(listed_refs[i], place_refs[i], sems.at[i])
        add_edges(
            sizes,
            word_refs[i],
            rows_ref,
            place_refs[i],
            total_ref,
            bank_parts_ref,
            *scratch,
            finish=finish if soon else None,
        )


def far_kernel(sizes, piece_count, last, words_ref, listed_ref, bank_parts_ref, spread_high_ref, spread_low_ref, *refs):
    pieces, refs = refs[:piece_count], refs[piece_count + 1 :]
    if last:
        *taken_refs, total_ref, out_ref, made_ref, out_sems = refs[:6]
        refs = refs[6:]
    else:
        total_ref, refs = refs[0], refs[1:]
    rows_ref, places_ref, sem, *scratch = refs
    copy = early_places(listed_ref, places_ref, sem)
    copy.start()
    load_rows(pieces, rows_ref)
    copy.wait()
    late_places(listed_ref, places_ref, sem)
    copies = []

    def give(start, summed):
        here = pl.ds(start, ROWS)
        first = taken_refs[0].shape[0]
        number, start = (0, start) if start < first else (1, start - first)
        taken = taken_refs[number][pl.ds(start, ROWS), :].astype(jnp.float32)
        made_ref[here, :] = (summed + taken).astype(jnp.bfloat16)
        copies.append(pltpu.make_async_copy(made_ref.at[here], out_ref.at[here], out_sems.at[len(copies)]))
        copies[-1].start()

    add_edges(
        sizes,
        words_ref,
        rows_ref,
        places_ref,
        total_ref,
        bank_parts_ref,
        *scratch,
        spread_refs=(spread_high_ref, spread_low_ref),
        finish=give if last else None,
    )
    for copy in copies:
        copy.wait()


def kernel_call(kernel, name, out_shape, in_specs, out_specs, scratch=(), vmem=MIB, aliases=None):
    return pl.pallas_call(
        kernel,
        out_shape=out_shape,
        in_specs=in_specs,
        out_specs=out_specs,
        scratch_shapes=list(scratch),
        input_output_aliases=aliases or {},
        compiler_params=pltpu.CompilerParams(vmem_limit_bytes=vmem),
        cost_estimate=pl.CostEstimate(flops=0, bytes_accessed=1_000, transcendentals=0),
        name=name,
    )


def body(features, restriction, mixing, source_index, target_index, map_index, edge_counts):
    nodes, width = features.shape
    replicas = lax.axis_size("rep")
    near = replicas // 2
    split = nodes * 9 // 16 // LANES * LANES
    maps, stalk, _ = restriction.shape
    channels = mixing.shape[0]
    capacity = source_index.shape[3]
    turns = source_index.shape[2]
    node_bits = bits_for(nodes)
    source_bits = bits_for(2 * nodes)
    assert replicas == 4 and turns == 2
    assert nodes == 1 << node_bits and nodes % ROWS == 0 and nodes > ROWS and capacity % LANES == 0
    assert source_bits + node_bits + bits_for(maps) <= 30

    smem = pl.BlockSpec(memory_space=pltpu.SMEM)
    vmem = pl.BlockSpec(memory_space=pltpu.VMEM)
    anywhere = pl.BlockSpec(memory_space=pl.ANY)

    def after(earlier, *values):
        earlier = list(earlier)
        return kernel_call(
            after_kernel,
            "after",
            [jax.ShapeDtypeStruct(value.shape, value.dtype) for value in values],
            [anywhere] * (len(earlier) + len(values)),
            [anywhere] * len(values),
            aliases={len(earlier) + number: number for number in range(len(values))},
        )(*earlier, *values)

    before = passed_along(features, "blk", 1)
    counts = jnp.broadcast_to(edge_counts[0, 0][:, None], (turns, capacity))
    own_edges = jnp.concatenate([source_index[0, 0], target_index[0, 0], map_index[0, 0], counts], axis=0)
    edges = [own_edges] + [swapped(own_edges, bit) for bit in range(1, replicas)]
    across_low = swapped(features[:split], near)
    (high,) = after(edges[1:], features[split:])
    across_high = swapped(high, near)
    far_low = passed_along(across_low, "blk", 1)
    part = replicas * capacity // LANES
    list_rows = [count * part for count in (1, 1, 2, 2, 1, 1)]
    listed = kernel_call(
        functools.partial(pick_kernel, (source_bits, node_bits, node_bits, capacity), near),
        "pick_edges",
        [jax.ShapeDtypeStruct((rows, LANES), jnp.int32) for rows in list_rows]
        + [jax.ShapeDtypeStruct((rows + COUNT_ROWS, LANES), jnp.int32) for rows in list_rows],
        [vmem] * replicas,
        [vmem] * 12,
        scratch=[
            pltpu.VMEM((8 * part, LANES), jnp.int32),
            pltpu.VMEM((3 * capacity // LANES, LANES), jnp.int32),
        ],
        vmem=4 * MIB,
    )(*edges)
    table_shapes = [(stalk * stalk, 2 * maps), (width, width), (width, width)]
    bank_parts, spread_high, spread_low = kernel_call(
        tables_kernel,
        "tables",
        [jax.ShapeDtypeStruct(shape, jnp.bfloat16) for shape in table_shapes],
        [vmem] * 2,
        [vmem] * 3,
        vmem=4 * MIB,
    )(restriction.reshape(maps, stalk * stalk).T, mixing)

    sizes = (stalk, channels, maps, source_bits, node_bits, nodes)
    total_shape = jax.ShapeDtypeStruct((nodes, width), jnp.float32)

    def work_space(message_parts):
        return [
            pltpu.VMEM((2 * EDGES, LANES), jnp.float32),
            pltpu.VMEM((width, EDGES), jnp.float32),
            pltpu.VMEM((stalk * stalk, EDGES), jnp.float32),
            pltpu.VMEM((width, EDGES), jnp.float32),
            pltpu.VMEM((message_parts * EDGES, width), jnp.bfloat16),
        ]

    def places_of(number):
        return pltpu.SMEM((list_rows[number] + COUNT_ROWS, LANES), jnp.int32)

    tables = [bank_parts, spread_high, spread_low]
    first = nodes * 3 // 4 // ROWS * ROWS
    given_shapes = [jax.ShapeDtypeStruct((count, width), jnp.bfloat16) for count in (first, nodes - first)]

    def with_near(number, pieces, totals=()):
        rows = sum(piece.shape[0] for piece in pieces)
        own_features = [features] if totals else []
        return kernel_call(
            functools.partial(near_kernel, sizes, len(pieces), bool(totals)),
            "soon_edges" if totals else "own_edges",
            [total_shape] * 2 + (given_shapes if totals else []),
            [vmem] * (7 + len(pieces) + len(own_features) + len(totals)),
            [vmem] * (4 if totals else 2),
            scratch=[
                pltpu.VMEM((2 * rows, LANES), jnp.float32),
                places_of(number),
                places_of(number + 1),
                pltpu.SemaphoreType.DMA((2,)),
            ]
            + work_space(1),
            vmem=rows * width * 4 + 6 * MIB,
            aliases={8 + len(pieces) + i: i for i in range(len(totals))},
        )(*listed[number : number + 2], *listed[number + 6 : number + 8], *tables, *pieces, *own_features, *totals)

    totals = with_near(0, [features])
    (across_high,) = after(totals, across_high)
    (before,) = after(totals, before)
    far_high = swapped(before[split:], near)
    own, _, *given = with_near(2, [across_low, across_high, before], totals)

    def with_far(number, pieces, total, taken=()):
        result = [jax.ShapeDtypeStruct((nodes, width), features.dtype)] if taken else []
        room = [pltpu.VMEM((nodes, width), features.dtype), pltpu.SemaphoreType.DMA((nodes // ROWS,))] if taken else []
        return kernel_call(
            functools.partial(far_kernel, sizes, len(pieces), bool(taken)),
            "last_edges" if taken else "straight_edges",
            [total_shape] + result,
            [vmem] * (6 + len(pieces) + len(taken)),
            [vmem] + [anywhere] * len(result),
            scratch=room
            + [pltpu.VMEM((2 * nodes, LANES), jnp.float32), places_of(number), pltpu.SemaphoreType.DMA]
            + work_space(2),
            vmem=nodes * width * 4 + 8 * MIB,
            aliases={5 + len(pieces): 0},
        )(listed[number], listed[number + 6], *tables, *pieces, total, *taken)

    taken = [swapped(part, 1) for part in given]
    far_low, far_high = after([own], far_low, far_high)
    (own,) = with_far(4, [far_low, far_high], own)
    _, updated = with_far(5, [swapped(far_low, 1), swapped(far_high, 1)], own, taken)
    return updated


def solution(mesh):
    in_specs = (
        P(("blk", "rep"), None),
        P(),
        P(),
        P("blk", "rep", None, None),
        P("blk", "rep", None, None),
        P("blk", "rep", None, None),
        P("blk", "rep", None),
    )
    out_specs = P(("blk", "rep"), None)
    return jax.shard_map(body, mesh=mesh, in_specs=in_specs, out_specs=out_specs, check_vma=False)
```

```python
import functools

import jax
import jax.numpy as jnp
from jax import lax
from jax.experimental import pallas as pl
from jax.experimental.pallas import tpu as pltpu
from jax.sharding import PartitionSpec as P

EDGES = 256
ROWS = 512
LANES = 128
MIB = 1024 * 1024
COUNT_ROWS = 8
EARLY_ROWS = 24


def bits_for(count):
    return max(1, (count - 1).bit_length())


def passed_along(block, axis, distance):
    devices = range(lax.axis_size(axis))
    route = [((i - distance) % len(devices), i) for i in devices]
    return lax.ppermute(block, axis, route)


def swapped(block, bit):
    route = [(i, i ^ bit) for i in range(lax.axis_size("rep"))]
    return lax.ppermute(block, "rep", route)


def shifted_left(value, distance):
    rows = value.shape[0]
    if distance >= LANES:
        return pltpu.roll(value, rows - distance // LANES, 0)
    turned = pltpu.roll(value, LANES - distance, 1)
    lane = lax.broadcasted_iota(jnp.int32, value.shape, 1)
    return jnp.where(lane >= LANES - distance, pltpu.roll(turned, rows - 1, 0), turned)


def ones_where(condition):
    return jnp.where(condition, 1.0, 0.0).astype(jnp.bfloat16)


def closed_up(words):
    rows = words.shape[0]
    row = lax.broadcasted_iota(jnp.int32, (rows, LANES), 0)
    lane = lax.broadcasted_iota(jnp.int32, (rows, LANES), 1)
    used = ones_where(words != 0)
    upto = ones_where(lax.broadcasted_iota(jnp.int32, (LANES, LANES), 0) <= lax.broadcasted_iota(jnp.int32, (LANES, LANES), 1))
    above = ones_where(lax.broadcasted_iota(jnp.int32, (rows, rows), 1) < lax.broadcasted_iota(jnp.int32, (rows, rows), 0))
    every = jnp.ones((LANES, LANES), jnp.bfloat16)
    dot = functools.partial(jnp.dot, preferred_element_type=jnp.float32)
    earlier = dot(dot(above, used).astype(jnp.bfloat16), every)
    number = (earlier + dot(used, upto)).astype(jnp.int32)
    total = dot(dot(jnp.ones((8, rows), jnp.bfloat16), used).astype(jnp.bfloat16), every).astype(jnp.int32)
    way = jnp.where(words != 0, row * LANES + lane + 1 - number, 0)
    for bit in range(bits_for(rows * LANES)):
        moves = ((way >> bit) & 1) == 1
        moved_words = shifted_left(jnp.where(moves, words, 0), 1 << bit)
        moved_way = shifted_left(jnp.where(moves, way, 0), 1 << bit)
        words = jnp.where(moves, 0, words) | moved_words
        way = jnp.where(moves, 0, way) | moved_way
    return words, total


def pick_kernel(sizes, near, *refs):
    source_bits, target_bits, node_bits, capacity = sizes
    replicas = 2 * near
    edge_refs, refs = refs[:replicas], refs[replicas:]
    word_refs, place_refs, candidates_ref, unpacked_ref = refs[:6], refs[6:12], refs[12], refs[13]
    rows = capacity // LANES
    node_mask = (1 << node_bits) - 1
    me = lax.axis_index("rep")
    positions = lax.broadcasted_iota(jnp.int32, (rows, LANES), 0) * LANES + lax.broadcasted_iota(
        jnp.int32, (rows, LANES), 1
    )
    part = replicas * rows
    for turn in range(2):
        for k, edge_ref in enumerate(edge_refs):
            for number in range(3):
                for row in range(rows):
                    at = number * rows + row
                    index_row = 2 * number + turn
                    unpacked_ref[at : at + 1, :] = edge_ref[index_row : index_row + 1, row * LANES : (row + 1) * LANES]
            source, target, map_id = (unpacked_ref[number * rows : (number + 1) * rows, :] for number in range(3))
            live = positions < edge_ref[6 + turn : 7 + turn, :LANES]
            slot = (source >> node_bits) ^ me
            owner = (target >> node_bits) ^ me
            held = live & ((slot & (near - 1)) == 0)
            far = slot >= near
            word = (source & node_mask) | ((target & node_mask) << source_bits)
            word |= (map_id << (source_bits + target_bits)) | jnp.int32(1 << 30)
            at = k * rows
            for other in range(2):
                wanted = held & (owner == other)
                choices = [((2 + 2 * other + turn) * part, wanted & (far if turn == 0 else ~far), word | (turn << node_bits))]
                if turn == 0:
                    choices.append((other * part, wanted & ~far, word))
                else:
                    turned = live & far & (owner == 0) & ((slot & (near - 1)) == other)
                    choices.append(((6 + other) * part, turned, word))
                for first, chosen, chosen_word in choices:
                    candidates_ref[first + at : first + at + rows, :] = jnp.where(chosen, chosen_word, 0)
    stops = [count * part for count in (0, 1, 2, 4, 6, 7, 8)]
    for number, (start, stop) in enumerate(zip(stops[:-1], stops[1:])):
        words, total = closed_up(candidates_ref[start:stop, :])
        word_refs[number][...] = words
        place_refs[number][:COUNT_ROWS, :] = total
        place_refs[number][COUNT_ROWS:, :] = (words & ((1 << source_bits) - 1)) * 2


def tables_kernel(bank_ref, mixing_ref, bank_parts_ref, spread_high_ref, spread_low_ref):
    maps = bank_ref.shape[1]
    channels = mixing_ref.shape[0]
    width = spread_high_ref.shape[0]
    high, low = two_parts(bank_ref[...])
    bank_parts_ref[:, :maps] = high
    bank_parts_ref[:, maps:] = low
    dot = functools.partial(jnp.dot, preferred_element_type=jnp.float32)
    down = ones_where(
        lax.broadcasted_iota(jnp.int32, (width, channels), 0) % channels
        == lax.broadcasted_iota(jnp.int32, (width, channels), 1)
    )
    across = ones_where(
        lax.broadcasted_iota(jnp.int32, (channels, width), 1) % channels
        == lax.broadcasted_iota(jnp.int32, (channels, width), 0)
    )
    same = lax.broadcasted_iota(jnp.int32, (width, width), 0) // channels == (
        lax.broadcasted_iota(jnp.int32, (width, width), 1) // channels
    )
    for part, ref in zip(two_parts(mixing_ref[...]), (spread_high_ref, spread_low_ref)):
        tiled = dot(dot(down, part).astype(jnp.bfloat16), across)
        ref[...] = jnp.where(same, tiled, 0.0).astype(jnp.bfloat16)


def after_kernel(*refs):
    pass


def two_parts(value):
    high = value.astype(jnp.bfloat16)
    return high, (value - high.astype(jnp.float32)).astype(jnp.bfloat16)


def load_rows(piece_refs, rows_ref):
    start = 0
    for ref in piece_refs:
        rows = ref.shape[0]

        def widen(i, _, ref=ref, start=start):
            at = pl.multiple_of(i * LANES, LANES)
            value = ref[pl.ds(at, LANES), :].astype(jnp.float32)
            for half in range(2):
                rows_ref[pl.ds(2 * (start + at) + half, LANES, stride=2), :] = value[:, half * LANES : (half + 1) * LANES]
            return 0

        lax.fori_loop(0, rows // LANES, widen, 0, unroll=2)
        start += rows


def add_edges(sizes, words_ref, rows_ref, places_ref, total_ref, bank_parts_ref, gathered_ref, turned_ref, chosen_ref, message_ref, sent_ref, spread_refs=(), finish=None):
    stalk, channels, maps, source_bits, target_bits, nodes = sizes
    target_mask = (1 << target_bits) - 1
    map_mask = (1 << bits_for(maps)) - 1
    lists = EDGES // LANES
    blocks = words_ref.shape[0] // lists
    count = places_ref[0, 0]

    def gather(block):
        for u in range(EDGES):
            place = pl.multiple_of(places_ref[COUNT_ROWS + block * lists + u // LANES, u % LANES], 2)
            gathered_ref[2 * u : 2 * u + 2, :] = rows_ref[pl.ds(place, 2), :]

    def words_of(block):
        return jnp.concatenate([words_ref[pl.ds(block * lists + part, 1), :] for part in range(lists)], axis=1)

    def turn_rows():
        for part in range(lists):
            lanes = slice(part * LANES, (part + 1) * LANES)
            for half in range(2):
                values = gathered_ref[pl.ds(2 * part * LANES + half, LANES, stride=2), :]
                turned_ref[half * LANES : (half + 1) * LANES, lanes] = values.T

    def choose(block):
        map_ids = (words_of(block) >> (source_bits + target_bits)) & map_mask
        wanted = ones_where(lax.broadcasted_iota(jnp.int32, (maps, EDGES), 0) == map_ids)
        wanted = jnp.concatenate([wanted, wanted], axis=0)
        chosen_ref[...] = jnp.dot(bank_parts_ref[...], wanted, preferred_element_type=jnp.float32)

    def make_messages():
        for part in range(lists):
            lanes = slice(part * LANES, (part + 1) * LANES)
            features = turned_ref[:, lanes]
            for i in range(stalk):
                message = None
                for j in range(stalk):
                    factor = chosen_ref[i * stalk + j : i * stalk + j + 1, lanes]
                    term = factor * features[j * channels : (j + 1) * channels, :]
                    message = term if message is None else message + term
                message_ref[i * channels : (i + 1) * channels, lanes] = message

    def turn_messages():
        for part in range(lists):
            lanes = slice(part * LANES, (part + 1) * LANES)
            sent_ref[lanes, :] = message_ref[:, lanes].T.astype(jnp.bfloat16)
        if spread_refs:
            mixed = sum(jnp.dot(sent_ref[...], ref[...], preferred_element_type=jnp.float32) for ref in spread_refs)
            sent_ref[...] = mixed.astype(jnp.bfloat16)

    def scatter(block, finish=None):
        words = words_of(block)
        targets = jnp.where(words != 0, (words >> source_bits) & target_mask, -1)
        ids = lax.broadcasted_iota(jnp.int32, (256, EDGES), 0).astype(jnp.bfloat16)
        one, zero = jnp.bfloat16(1), jnp.bfloat16(0)
        for start in range(0, nodes, ROWS):
            selectors = []
            for base in range(start, start + ROWS, 256):
                wanted_ids = (targets - base).astype(jnp.float32).astype(jnp.bfloat16)
                selectors.append(jnp.where(ids == wanted_ids, one, zero))
            selector = jnp.concatenate(selectors, axis=0)
            here = slice(start, start + ROWS)
            added = total_ref[here, :]
            added += jnp.dot(selector, sent_ref[...], preferred_element_type=jnp.float32)
            if finish is None:
                total_ref[here, :] = added
            else:
                finish(start, added)

    def step(block, _):
        turn_rows()
        choose(block)
        gather(jnp.minimum(block + 1, blocks - 1))
        scatter(block - 1)
        make_messages()
        turn_messages()
        return 0

    last = jnp.maximum(pl.cdiv(count, EDGES), 1) - 1
    gather(0)
    turn_rows()
    choose(0)
    gather(jnp.minimum(1, blocks - 1))
    make_messages()
    turn_messages()
    lax.fori_loop(1, last + 1, step, 0)
    scatter(last, finish)


def early_places(listed_ref, places_ref, sem):
    early = pl.ds(0, EARLY_ROWS)
    return pltpu.make_async_copy(listed_ref.at[early], places_ref.at[early], sem)


def late_places(listed_ref, places_ref, sem):
    @pl.when(places_ref[0, 0] > (EARLY_ROWS - COUNT_ROWS) * LANES)
    def _():
        rest = pl.ds(EARLY_ROWS, listed_ref.shape[0] - EARLY_ROWS)
        copy = pltpu.make_async_copy(listed_ref.at[rest], places_ref.at[rest], sem)
        copy.start()
        copy.wait()


def near_kernel(sizes, piece_count, soon, *refs):
    word_refs, listed_refs, (bank_parts_ref, spread_high_ref, spread_low_ref), refs = refs[:2], refs[2:4], refs[4:7], refs[7:]
    pieces, refs = refs[:piece_count], refs[piece_count:]
    if soon:
        features_ref, _, _, own_ref, other_ref, *given_refs = refs[:7]
        refs = refs[7:]
    else:
        own_ref, other_ref, refs = refs[0], refs[1], refs[2:]
    rows_ref, place_refs, sems, scratch = refs[0], refs[1:3], refs[3], refs[4:]
    copies = [early_places(listed_refs[i], place_refs[i], sems.at[i]) for i in range(2)]
    for copy in copies:
        copy.start()
    if not soon:
        for total_ref in (own_ref, other_ref):
            total_ref[...] = jnp.zeros_like(total_ref)
    load_rows(pieces, rows_ref)
    for copy in copies:
        copy.wait()

    def mixed(summed):
        high, low = two_parts(summed)
        result = jnp.dot(high, spread_high_ref[...], preferred_element_type=jnp.float32)
        result += jnp.dot(high, spread_low_ref[...], preferred_element_type=jnp.float32)
        return result + jnp.dot(low, spread_high_ref[...], preferred_element_type=jnp.float32)

    def give(start, summed):
        first = given_refs[0].shape[0]
        number, start = (0, start) if start < first else (1, start - first)
        given_refs[number][pl.ds(start, ROWS), :] = mixed(summed).astype(jnp.bfloat16)

    def keep(start, summed):
        here = pl.ds(start, ROWS)
        own_ref[here, :] = features_ref[here, :].astype(jnp.float32) + mixed(summed)

    for i, total_ref, finish in ((1, other_ref, give), (0, own_ref, keep)):
        late_places(listed_refs[i], place_refs[i], sems.at[i])
        add_edges(
            sizes,
            word_refs[i],
            rows_ref,
            place_refs[i],
            total_ref,
            bank_parts_ref,
            *scratch,
            finish=finish if soon else None,
        )


def far_kernel(sizes, piece_count, last, words_ref, listed_ref, bank_parts_ref, spread_high_ref, spread_low_ref, *refs):
    pieces, refs = refs[:piece_count], refs[piece_count + 1 :]
    if last:
        *taken_refs, total_ref, out_ref, made_ref, out_sems = refs[:6]
        refs = refs[6:]
    else:
        total_ref, refs = refs[0], refs[1:]
    rows_ref, places_ref, sem, *scratch = refs
    copy = early_places(listed_ref, places_ref, sem)
    copy.start()
    load_rows(pieces, rows_ref)
    copy.wait()
    late_places(listed_ref, places_ref, sem)
    copies = []

    def give(start, summed):
        here = pl.ds(start, ROWS)
        first = taken_refs[0].shape[0]
        number, start = (0, start) if start < first else (1, start - first)
        taken = taken_refs[number][pl.ds(start, ROWS), :].astype(jnp.float32)
        made_ref[here, :] = (summed + taken).astype(jnp.bfloat16)
        copies.append(pltpu.make_async_copy(made_ref.at[here], out_ref.at[here], out_sems.at[len(copies)]))
        copies[-1].start()

    add_edges(
        sizes,
        words_ref,
        rows_ref,
        places_ref,
        total_ref,
        bank_parts_ref,
        *scratch,
        spread_refs=(spread_high_ref, spread_low_ref),
        finish=give if last else None,
    )
    for copy in copies:
        copy.wait()


def kernel_call(kernel, name, out_shape, in_specs, out_specs, scratch=(), vmem=MIB, aliases=None):
    return pl.pallas_call(
        kernel,
        out_shape=out_shape,
        in_specs=in_specs,
        out_specs=out_specs,
        scratch_shapes=list(scratch),
        input_output_aliases=aliases or {},
        compiler_params=pltpu.CompilerParams(vmem_limit_bytes=vmem),
        cost_estimate=pl.CostEstimate(flops=0, bytes_accessed=1_000, transcendentals=0),
        name=name,
    )


def body(features, restriction, mixing, source_index, target_index, map_index, edge_counts):
    nodes, width = features.shape
    replicas = lax.axis_size("rep")
    near = replicas // 2
    split = nodes // 2
    first_rows = split + LANES
    maps, stalk, _ = restriction.shape
    channels = mixing.shape[0]
    capacity = source_index.shape[3]
    turns = source_index.shape[2]
    node_bits = bits_for(nodes)
    source_bits = bits_for(2 * nodes)
    assert replicas == 4 and turns == 2
    assert nodes == 1 << node_bits and nodes % ROWS == 0 and nodes > ROWS and capacity % LANES == 0
    assert source_bits + node_bits + bits_for(maps) <= 30

    smem = pl.BlockSpec(memory_space=pltpu.SMEM)
    vmem = pl.BlockSpec(memory_space=pltpu.VMEM)
    anywhere = pl.BlockSpec(memory_space=pl.ANY)

    def after(earlier, *values):
        earlier = list(earlier)
        return kernel_call(
            after_kernel,
            "after",
            [jax.ShapeDtypeStruct(value.shape, value.dtype) for value in values],
            [anywhere] * (len(earlier) + len(values)),
            [anywhere] * len(values),
            aliases={len(earlier) + number: number for number in range(len(values))},
        )(*earlier, *values)

    first_part = features[:first_rows]
    across_low = swapped(first_part, near)
    low, high = after([first_part], features[:split], features[split:])
    before_high = passed_along(high, "blk", 1)
    before_low = passed_along(low, "blk", 1)
    counts = jnp.broadcast_to(edge_counts[0, 0][:, None], (turns, capacity))
    own_edges = jnp.concatenate([source_index[0, 0], target_index[0, 0], map_index[0, 0], counts], axis=0)
    edges = [own_edges] + [swapped(own_edges, bit) for bit in range(1, replicas)]
    (high,) = after(edges[1:], features[first_rows:])
    across_high = swapped(high, near)
    far_low = passed_along(across_low[:split], "blk", 1)
    far_high = swapped(before_high, near)
    part = replicas * capacity // LANES
    list_rows = [count * part for count in (1, 1, 2, 2, 1, 1)]
    listed = kernel_call(
        functools.partial(pick_kernel, (source_bits, node_bits, node_bits, capacity), near),
        "pick_edges",
        [jax.ShapeDtypeStruct((rows, LANES), jnp.int32) for rows in list_rows]
        + [jax.ShapeDtypeStruct((rows + COUNT_ROWS, LANES), jnp.int32) for rows in list_rows],
        [vmem] * replicas,
        [vmem] * 12,
        scratch=[
            pltpu.VMEM((8 * part, LANES), jnp.int32),
            pltpu.VMEM((3 * capacity // LANES, LANES), jnp.int32),
        ],
        vmem=4 * MIB,
    )(*edges)
    table_shapes = [(stalk * stalk, 2 * maps), (width, width), (width, width)]
    bank_parts, spread_high, spread_low = kernel_call(
        tables_kernel,
        "tables",
        [jax.ShapeDtypeStruct(shape, jnp.bfloat16) for shape in table_shapes],
        [vmem] * 2,
        [vmem] * 3,
        vmem=4 * MIB,
    )(restriction.reshape(maps, stalk * stalk).T, mixing)

    sizes = (stalk, channels, maps, source_bits, node_bits, nodes)
    total_shape = jax.ShapeDtypeStruct((nodes, width), jnp.float32)

    def work_space():
        return [
            pltpu.VMEM((2 * EDGES, LANES), jnp.float32),
            pltpu.VMEM((width, EDGES), jnp.float32),
            pltpu.VMEM((stalk * stalk, EDGES), jnp.float32),
            pltpu.VMEM((width, EDGES), jnp.float32),
            pltpu.VMEM((EDGES, width), jnp.bfloat16),
        ]

    def places_of(number):
        return pltpu.SMEM((list_rows[number] + COUNT_ROWS, LANES), jnp.int32)

    tables = [bank_parts, spread_high, spread_low]
    first = nodes * 3 // 4 // ROWS * ROWS
    given_shapes = [jax.ShapeDtypeStruct((count, width), jnp.bfloat16) for count in (first, nodes - first)]

    def with_near(number, pieces, totals=()):
        rows = sum(piece.shape[0] for piece in pieces)
        own_features = [features] if totals else []
        return kernel_call(
            functools.partial(near_kernel, sizes, len(pieces), bool(totals)),
            "soon_edges" if totals else "own_edges",
            [total_shape] * 2 + (given_shapes if totals else []),
            [vmem] * (7 + len(pieces) + len(own_features) + len(totals)),
            [vmem] * (4 if totals else 2),
            scratch=[
                pltpu.VMEM((2 * rows, LANES), jnp.float32),
                places_of(number),
                places_of(number + 1),
                pltpu.SemaphoreType.DMA((2,)),
            ]
            + work_space(),
            vmem=rows * width * 4 + 6 * MIB,
            aliases={8 + len(pieces) + i: i for i in range(len(totals))},
        )(*listed[number : number + 2], *listed[number + 6 : number + 8], *tables, *pieces, *own_features, *totals)

    totals = with_near(0, [features])
    across_high, before_low = after(totals, across_high, before_low)
    own, _, *given = with_near(2, [across_low, across_high, before_low, before_high], totals)

    def with_far(number, pieces, total, taken=()):
        result = [jax.ShapeDtypeStruct((nodes, width), features.dtype)] if taken else []
        room = [pltpu.VMEM((nodes, width), features.dtype), pltpu.SemaphoreType.DMA((nodes // ROWS,))] if taken else []
        return kernel_call(
            functools.partial(far_kernel, sizes, len(pieces), bool(taken)),
            "last_edges" if taken else "straight_edges",
            [total_shape] + result,
            [vmem] * (6 + len(pieces) + len(taken)),
            [vmem] + [anywhere] * len(result),
            scratch=room
            + [pltpu.VMEM((2 * nodes, LANES), jnp.float32), places_of(number), pltpu.SemaphoreType.DMA]
            + work_space(),
            vmem=nodes * width * 4 + 8 * MIB,
            aliases={5 + len(pieces): 0},
        )(listed[number], listed[number + 6], *tables, *pieces, total, *taken)

    taken = [swapped(part, 1) for part in given]
    far_low, far_high = after([own], far_low, far_high)
    (own,) = with_far(4, [far_low, far_high], own)
    _, updated = with_far(5, [swapped(far_low, 1), swapped(far_high, 1)], own, taken)
    return updated


def solution(mesh):
    in_specs = (
        P(("blk", "rep"), None),
        P(),
        P(),
        P("blk", "rep", None, None),
        P("blk", "rep", None, None),
        P("blk", "rep", None, None),
        P("blk", "rep", None),
    )
    out_specs = P(("blk", "rep"), None)
    return jax.shard_map(body, mesh=mesh, in_specs=in_specs, out_specs=out_specs, check_vma=False)
```

```python
import functools

import jax
import jax.numpy as jnp
from jax import lax
from jax.experimental import pallas as pl
from jax.experimental.pallas import tpu as pltpu
from jax.sharding import PartitionSpec as P

EDGES = 256
ROWS = 512
LANES = 128
MIB = 1024 * 1024
COUNT_ROWS = 8
EARLY_ROWS = 24


def bits_for(count):
    return max(1, (count - 1).bit_length())


def passed_along(block, axis, distance):
    devices = range(lax.axis_size(axis))
    route = [((i - distance) % len(devices), i) for i in devices]
    return lax.ppermute(block, axis, route)


def swapped(block, bit):
    route = [(i, i ^ bit) for i in range(lax.axis_size("rep"))]
    return lax.ppermute(block, "rep", route)


def shifted_left(value, distance):
    rows = value.shape[0]
    if distance >= LANES:
        return pltpu.roll(value, rows - distance // LANES, 0)
    turned = pltpu.roll(value, LANES - distance, 1)
    lane = lax.broadcasted_iota(jnp.int32, value.shape, 1)
    return jnp.where(lane >= LANES - distance, pltpu.roll(turned, rows - 1, 0), turned)


def ones_where(condition):
    return jnp.where(condition, 1.0, 0.0).astype(jnp.bfloat16)


def closed_up(words):
    rows = words.shape[0]
    row = lax.broadcasted_iota(jnp.int32, (rows, LANES), 0)
    lane = lax.broadcasted_iota(jnp.int32, (rows, LANES), 1)
    used = ones_where(words != 0)
    upto = ones_where(lax.broadcasted_iota(jnp.int32, (LANES, LANES), 0) <= lax.broadcasted_iota(jnp.int32, (LANES, LANES), 1))
    above = ones_where(lax.broadcasted_iota(jnp.int32, (rows, rows), 1) < lax.broadcasted_iota(jnp.int32, (rows, rows), 0))
    every = jnp.ones((LANES, LANES), jnp.bfloat16)
    dot = functools.partial(jnp.dot, preferred_element_type=jnp.float32)
    earlier = dot(dot(above, used).astype(jnp.bfloat16), every)
    number = (earlier + dot(used, upto)).astype(jnp.int32)
    total = dot(dot(jnp.ones((8, rows), jnp.bfloat16), used).astype(jnp.bfloat16), every).astype(jnp.int32)
    way = jnp.where(words != 0, row * LANES + lane + 1 - number, 0)
    for bit in range(bits_for(rows * LANES)):
        moves = ((way >> bit) & 1) == 1
        moved_words = shifted_left(jnp.where(moves, words, 0), 1 << bit)
        moved_way = shifted_left(jnp.where(moves, way, 0), 1 << bit)
        words = jnp.where(moves, 0, words) | moved_words
        way = jnp.where(moves, 0, way) | moved_way
    return words, total


def pick_kernel(sizes, near, *refs):
    source_bits, target_bits, node_bits, capacity = sizes
    replicas = 2 * near
    edge_refs, refs = refs[:replicas], refs[replicas:]
    word_refs, place_refs, candidates_ref, unpacked_ref = refs[:6], refs[6:12], refs[12], refs[13]
    rows = capacity // LANES
    node_mask = (1 << node_bits) - 1
    me = lax.axis_index("rep")
    positions = lax.broadcasted_iota(jnp.int32, (rows, LANES), 0) * LANES + lax.broadcasted_iota(
        jnp.int32, (rows, LANES), 1
    )
    part = replicas * rows
    for turn in range(2):
        for k, edge_ref in enumerate(edge_refs):
            for number in range(3):
                for row in range(rows):
                    at = number * rows + row
                    index_row = 2 * number + turn
                    unpacked_ref[at : at + 1, :] = edge_ref[index_row : index_row + 1, row * LANES : (row + 1) * LANES]
            source, target, map_id = (unpacked_ref[number * rows : (number + 1) * rows, :] for number in range(3))
            live = positions < edge_ref[6 + turn : 7 + turn, :LANES]
            slot = (source >> node_bits) ^ me
            owner = (target >> node_bits) ^ me
            held = live & ((slot & (near - 1)) == 0)
            far = slot >= near
            word = (source & node_mask) | ((target & node_mask) << source_bits)
            word |= (map_id << (source_bits + target_bits)) | jnp.int32(1 << 30)
            at = k * rows
            for other in range(2):
                wanted = held & (owner == other)
                choices = [((2 + 2 * other + turn) * part, wanted & (far if turn == 0 else ~far), word | (turn << node_bits))]
                if turn == 0:
                    choices.append((other * part, wanted & ~far, word))
                else:
                    turned = live & far & (owner == 0) & ((slot & (near - 1)) == other)
                    choices.append(((6 + other) * part, turned, word))
                for first, chosen, chosen_word in choices:
                    candidates_ref[first + at : first + at + rows, :] = jnp.where(chosen, chosen_word, 0)
    stops = [count * part for count in (0, 1, 2, 4, 6, 7, 8)]
    for number, (start, stop) in enumerate(zip(stops[:-1], stops[1:])):
        words, total = closed_up(candidates_ref[start:stop, :])
        word_refs[number][...] = words
        place_refs[number][:COUNT_ROWS, :] = total
        place_refs[number][COUNT_ROWS:, :] = (words & ((1 << source_bits) - 1)) * 2


def tables_kernel(bank_ref, mixing_ref, bank_parts_ref, spread_high_ref, spread_low_ref):
    maps = bank_ref.shape[1]
    channels = mixing_ref.shape[0]
    width = spread_high_ref.shape[0]
    high, low = two_parts(bank_ref[...])
    bank_parts_ref[:, :maps] = high
    bank_parts_ref[:, maps:] = low
    dot = functools.partial(jnp.dot, preferred_element_type=jnp.float32)
    down = ones_where(
        lax.broadcasted_iota(jnp.int32, (width, channels), 0) % channels
        == lax.broadcasted_iota(jnp.int32, (width, channels), 1)
    )
    across = ones_where(
        lax.broadcasted_iota(jnp.int32, (channels, width), 1) % channels
        == lax.broadcasted_iota(jnp.int32, (channels, width), 0)
    )
    same = lax.broadcasted_iota(jnp.int32, (width, width), 0) // channels == (
        lax.broadcasted_iota(jnp.int32, (width, width), 1) // channels
    )
    for part, ref in zip(two_parts(mixing_ref[...]), (spread_high_ref, spread_low_ref)):
        tiled = dot(dot(down, part).astype(jnp.bfloat16), across)
        ref[...] = jnp.where(same, tiled, 0.0).astype(jnp.bfloat16)


def after_kernel(*refs):
    pass


def two_parts(value):
    high = value.astype(jnp.bfloat16)
    return high, (value - high.astype(jnp.float32)).astype(jnp.bfloat16)


def load_rows(piece_refs, rows_ref):
    start = 0
    for ref in piece_refs:
        rows = ref.shape[0]

        def widen(i, _, ref=ref, start=start):
            at = pl.multiple_of(i * LANES, LANES)
            value = ref[pl.ds(at, LANES), :].astype(jnp.float32)
            for half in range(2):
                rows_ref[pl.ds(2 * (start + at) + half, LANES, stride=2), :] = value[:, half * LANES : (half + 1) * LANES]
            return 0

        lax.fori_loop(0, rows // LANES, widen, 0, unroll=2)
        start += rows


def add_edges(sizes, words_ref, rows_ref, places_ref, total_ref, bank_parts_ref, gathered_ref, turned_ref, chosen_ref, message_ref, sent_ref, spread_refs=(), finish=None):
    stalk, channels, maps, source_bits, target_bits, nodes = sizes
    target_mask = (1 << target_bits) - 1
    map_mask = (1 << bits_for(maps)) - 1
    lists = EDGES // LANES
    blocks = words_ref.shape[0] // lists
    count = places_ref[0, 0]

    def gather(block):
        for u in range(EDGES):
            place = pl.multiple_of(places_ref[COUNT_ROWS + block * lists + u // LANES, u % LANES], 2)
            gathered_ref[2 * u : 2 * u + 2, :] = rows_ref[pl.ds(place, 2), :]

    def words_of(block):
        return jnp.concatenate([words_ref[pl.ds(block * lists + part, 1), :] for part in range(lists)], axis=1)

    def turn_rows():
        for part in range(lists):
            lanes = slice(part * LANES, (part + 1) * LANES)
            for half in range(2):
                values = gathered_ref[pl.ds(2 * part * LANES + half, LANES, stride=2), :]
                turned_ref[half * LANES : (half + 1) * LANES, lanes] = values.T

    def choose(block):
        map_ids = (words_of(block) >> (source_bits + target_bits)) & map_mask
        wanted = ones_where(lax.broadcasted_iota(jnp.int32, (maps, EDGES), 0) == map_ids)
        wanted = jnp.concatenate([wanted, wanted], axis=0)
        chosen_ref[...] = jnp.dot(bank_parts_ref[...], wanted, preferred_element_type=jnp.float32)

    def make_messages():
        for part in range(lists):
            lanes = slice(part * LANES, (part + 1) * LANES)
            features = turned_ref[:, lanes]
            for i in range(stalk):
                message = None
                for j in range(stalk):
                    factor = chosen_ref[i * stalk + j : i * stalk + j + 1, lanes]
                    term = factor * features[j * channels : (j + 1) * channels, :]
                    message = term if message is None else message + term
                message_ref[i * channels : (i + 1) * channels, lanes] = message

    def turn_messages():
        for part in range(lists):
            lanes = slice(part * LANES, (part + 1) * LANES)
            sent_ref[lanes, :] = message_ref[:, lanes].T.astype(jnp.bfloat16)
        if spread_refs:
            mixed = sum(jnp.dot(sent_ref[...], ref[...], preferred_element_type=jnp.float32) for ref in spread_refs)
            sent_ref[...] = mixed.astype(jnp.bfloat16)

    def scatter(block, finish=None):
        words = words_of(block)
        targets = jnp.where(words != 0, (words >> source_bits) & target_mask, -1)
        ids = lax.broadcasted_iota(jnp.int32, (256, EDGES), 0).astype(jnp.bfloat16)
        one, zero = jnp.bfloat16(1), jnp.bfloat16(0)
        for start in range(0, nodes, ROWS):
            selectors = []
            for base in range(start, start + ROWS, 256):
                wanted_ids = (targets - base).astype(jnp.float32).astype(jnp.bfloat16)
                selectors.append(jnp.where(ids == wanted_ids, one, zero))
            selector = jnp.concatenate(selectors, axis=0)
            here = slice(start, start + ROWS)
            added = total_ref[here, :]
            added += jnp.dot(selector, sent_ref[...], preferred_element_type=jnp.float32)
            if finish is None:
                total_ref[here, :] = added
            else:
                finish(start, added)

    def step(block, _):
        turn_rows()
        choose(block)
        gather(jnp.minimum(block + 1, blocks - 1))
        scatter(block - 1)
        make_messages()
        turn_messages()
        return 0

    last = jnp.maximum(pl.cdiv(count, EDGES), 1) - 1
    gather(0)
    turn_rows()
    choose(0)
    gather(jnp.minimum(1, blocks - 1))
    make_messages()
    turn_messages()
    lax.fori_loop(1, last + 1, step, 0)
    scatter(last, finish)


def early_places(listed_ref, places_ref, sem):
    early = pl.ds(0, EARLY_ROWS)
    return pltpu.make_async_copy(listed_ref.at[early], places_ref.at[early], sem)


def late_places(listed_ref, places_ref, sem):
    @pl.when(places_ref[0, 0] > (EARLY_ROWS - COUNT_ROWS) * LANES)
    def _():
        rest = pl.ds(EARLY_ROWS, listed_ref.shape[0] - EARLY_ROWS)
        copy = pltpu.make_async_copy(listed_ref.at[rest], places_ref.at[rest], sem)
        copy.start()
        copy.wait()


def near_kernel(sizes, piece_count, soon, *refs):
    word_refs, listed_refs, (bank_parts_ref, spread_high_ref, spread_low_ref), refs = refs[:2], refs[2:4], refs[4:7], refs[7:]
    pieces, refs = refs[:piece_count], refs[piece_count:]
    if soon:
        features_ref, _, _, own_ref, other_ref, *given_refs = refs[:7]
        refs = refs[7:]
    else:
        own_ref, other_ref, refs = refs[0], refs[1], refs[2:]
    rows_ref, place_refs, sems, scratch = refs[0], refs[1:3], refs[3], refs[4:]
    copies = [early_places(listed_refs[i], place_refs[i], sems.at[i]) for i in range(2)]
    for copy in copies:
        copy.start()
    if not soon:
        for total_ref in (own_ref, other_ref):
            total_ref[...] = jnp.zeros_like(total_ref)
    load_rows(pieces, rows_ref)
    for copy in copies:
        copy.wait()

    def mixed(summed):
        high, low = two_parts(summed)
        result = jnp.dot(high, spread_high_ref[...], preferred_element_type=jnp.float32)
        result += jnp.dot(high, spread_low_ref[...], preferred_element_type=jnp.float32)
        return result + jnp.dot(low, spread_high_ref[...], preferred_element_type=jnp.float32)

    def give(start, summed):
        first = given_refs[0].shape[0]
        number, start = (0, start) if start < first else (1, start - first)
        given_refs[number][pl.ds(start, ROWS), :] = mixed(summed).astype(jnp.bfloat16)

    def keep(start, summed):
        here = pl.ds(start, ROWS)
        own_ref[here, :] = features_ref[here, :].astype(jnp.float32) + mixed(summed)

    for i, total_ref, finish in ((1, other_ref, give), (0, own_ref, keep)):
        late_places(listed_refs[i], place_refs[i], sems.at[i])
        add_edges(
            sizes,
            word_refs[i],
            rows_ref,
            place_refs[i],
            total_ref,
            bank_parts_ref,
            *scratch,
            finish=finish if soon else None,
        )


def far_kernel(sizes, piece_count, last, words_ref, listed_ref, bank_parts_ref, spread_high_ref, spread_low_ref, *refs):
    pieces, refs = refs[:piece_count], refs[piece_count + 1 :]
    if last:
        *taken_refs, total_ref, out_ref, made_ref, out_sems = refs[:6]
        refs = refs[6:]
    else:
        total_ref, refs = refs[0], refs[1:]
    rows_ref, places_ref, sem, *scratch = refs
    copy = early_places(listed_ref, places_ref, sem)
    copy.start()
    load_rows(pieces, rows_ref)
    copy.wait()
    late_places(listed_ref, places_ref, sem)
    copies = []

    def give(start, summed):
        here = pl.ds(start, ROWS)
        first = taken_refs[0].shape[0]
        number, start = (0, start) if start < first else (1, start - first)
        taken = taken_refs[number][pl.ds(start, ROWS), :].astype(jnp.float32)
        made_ref[here, :] = (summed + taken).astype(jnp.bfloat16)
        copies.append(pltpu.make_async_copy(made_ref.at[here], out_ref.at[here], out_sems.at[len(copies)]))
        copies[-1].start()

    add_edges(
        sizes,
        words_ref,
        rows_ref,
        places_ref,
        total_ref,
        bank_parts_ref,
        *scratch,
        spread_refs=(spread_high_ref, spread_low_ref),
        finish=give if last else None,
    )
    for copy in copies:
        copy.wait()


def kernel_call(kernel, name, out_shape, in_specs, out_specs, scratch=(), vmem=MIB, aliases=None):
    return pl.pallas_call(
        kernel,
        out_shape=out_shape,
        in_specs=in_specs,
        out_specs=out_specs,
        scratch_shapes=list(scratch),
        input_output_aliases=aliases or {},
        compiler_params=pltpu.CompilerParams(vmem_limit_bytes=vmem),
        cost_estimate=pl.CostEstimate(flops=0, bytes_accessed=1_000, transcendentals=0),
        name=name,
    )


def body(features, restriction, mixing, source_index, target_index, map_index, edge_counts):
    nodes, width = features.shape
    replicas = lax.axis_size("rep")
    near = replicas // 2
    half = nodes // 2
    split = half + LANES
    maps, stalk, _ = restriction.shape
    channels = mixing.shape[0]
    capacity = source_index.shape[3]
    turns = source_index.shape[2]
    node_bits = bits_for(nodes)
    source_bits = bits_for(2 * nodes)
    assert replicas == 4 and turns == 2
    assert nodes == 1 << node_bits and nodes % ROWS == 0 and nodes > ROWS and capacity % LANES == 0
    assert source_bits + node_bits + bits_for(maps) <= 30

    smem = pl.BlockSpec(memory_space=pltpu.SMEM)
    vmem = pl.BlockSpec(memory_space=pltpu.VMEM)
    anywhere = pl.BlockSpec(memory_space=pl.ANY)

    def after(earlier, *values):
        earlier = list(earlier)
        return kernel_call(
            after_kernel,
            "after",
            [jax.ShapeDtypeStruct(value.shape, value.dtype) for value in values],
            [anywhere] * (len(earlier) + len(values)),
            [anywhere] * len(values),
            aliases={len(earlier) + number: number for number in range(len(values))},
        )(*earlier, *values)

    first_part = features[:split]
    across_low = swapped(first_part, near)
    low, high = after([first_part], features[:half], features[half:])
    before_high = passed_along(high, "blk", 1)
    before_low = passed_along(low, "blk", 1)
    counts = jnp.broadcast_to(edge_counts[0, 0][:, None], (turns, capacity))
    own_edges = jnp.concatenate([source_index[0, 0], target_index[0, 0], map_index[0, 0], counts], axis=0)
    edges = [own_edges] + [swapped(own_edges, bit) for bit in range(1, replicas)]
    (high,) = after(edges[1:], features[split:])
    across_high = swapped(high, near)
    far_low = passed_along(across_low, "blk", 1)
    far_high = swapped(before_high[split - half :], near)
    part = replicas * capacity // LANES
    list_rows = [count * part for count in (1, 1, 2, 2, 1, 1)]
    listed = kernel_call(
        functools.partial(pick_kernel, (source_bits, node_bits, node_bits, capacity), near),
        "pick_edges",
        [jax.ShapeDtypeStruct((rows, LANES), jnp.int32) for rows in list_rows]
        + [jax.ShapeDtypeStruct((rows + COUNT_ROWS, LANES), jnp.int32) for rows in list_rows],
        [vmem] * replicas,
        [vmem] * 12,
        scratch=[
            pltpu.VMEM((8 * part, LANES), jnp.int32),
            pltpu.VMEM((3 * capacity // LANES, LANES), jnp.int32),
        ],
        vmem=4 * MIB,
    )(*edges)
    table_shapes = [(stalk * stalk, 2 * maps), (width, width), (width, width)]
    bank_parts, spread_high, spread_low = kernel_call(
        tables_kernel,
        "tables",
        [jax.ShapeDtypeStruct(shape, jnp.bfloat16) for shape in table_shapes],
        [vmem] * 2,
        [vmem] * 3,
        vmem=4 * MIB,
    )(restriction.reshape(maps, stalk * stalk).T, mixing)

    sizes = (stalk, channels, maps, source_bits, node_bits, nodes)
    total_shape = jax.ShapeDtypeStruct((nodes, width), jnp.float32)

    def work_space():
        return [
            pltpu.VMEM((2 * EDGES, LANES), jnp.float32),
            pltpu.VMEM((width, EDGES), jnp.float32),
            pltpu.VMEM((stalk * stalk, EDGES), jnp.float32),
            pltpu.VMEM((width, EDGES), jnp.float32),
            pltpu.VMEM((EDGES, width), jnp.bfloat16),
        ]

    def places_of(number):
        return pltpu.SMEM((list_rows[number] + COUNT_ROWS, LANES), jnp.int32)

    tables = [bank_parts, spread_high, spread_low]
    first = nodes * 3 // 4 // ROWS * ROWS
    given_shapes = [jax.ShapeDtypeStruct((count, width), jnp.bfloat16) for count in (first, nodes - first)]

    def with_near(number, pieces, totals=()):
        rows = sum(piece.shape[0] for piece in pieces)
        own_features = [features] if totals else []
        return kernel_call(
            functools.partial(near_kernel, sizes, len(pieces), bool(totals)),
            "soon_edges" if totals else "own_edges",
            [total_shape] * 2 + (given_shapes if totals else []),
            [vmem] * (7 + len(pieces) + len(own_features) + len(totals)),
            [vmem] * (4 if totals else 2),
            scratch=[
                pltpu.VMEM((2 * rows, LANES), jnp.float32),
                places_of(number),
                places_of(number + 1),
                pltpu.SemaphoreType.DMA((2,)),
            ]
            + work_space(),
            vmem=rows * width * 4 + 6 * MIB,
            aliases={8 + len(pieces) + i: i for i in range(len(totals))},
        )(*listed[number : number + 2], *listed[number + 6 : number + 8], *tables, *pieces, *own_features, *totals)

    totals = with_near(0, [features])
    across_high, before_low = after(totals, across_high, before_low)
    own, _, *given = with_near(2, [across_low, across_high, before_low, before_high], totals)

    def with_far(number, pieces, total, taken=()):
        result = [jax.ShapeDtypeStruct((nodes, width), features.dtype)] if taken else []
        room = [pltpu.VMEM((nodes, width), features.dtype), pltpu.SemaphoreType.DMA((nodes // ROWS,))] if taken else []
        return kernel_call(
            functools.partial(far_kernel, sizes, len(pieces), bool(taken)),
            "last_edges" if taken else "straight_edges",
            [total_shape] + result,
            [vmem] * (6 + len(pieces) + len(taken)),
            [vmem] + [anywhere] * len(result),
            scratch=room
            + [pltpu.VMEM((2 * nodes, LANES), jnp.float32), places_of(number), pltpu.SemaphoreType.DMA]
            + work_space(),
            vmem=nodes * width * 4 + 8 * MIB,
            aliases={5 + len(pieces): 0},
        )(listed[number], listed[number + 6], *tables, *pieces, total, *taken)

    taken = [swapped(part, 1) for part in given]
    far_low, far_high = after([own], far_low, far_high)
    (own,) = with_far(4, [far_low, far_high], own)
    _, updated = with_far(5, [swapped(far_low, 1), swapped(far_high, 1)], own, taken)
    return updated


def solution(mesh):
    in_specs = (
        P(("blk", "rep"), None),
        P(),
        P(),
        P("blk", "rep", None, None),
        P("blk", "rep", None, None),
        P("blk", "rep", None, None),
        P("blk", "rep", None),
    )
    out_specs = P(("blk", "rep"), None)
    return jax.shard_map(body, mesh=mesh, in_specs=in_specs, out_specs=out_specs, check_vma=False)
```
